32 devices in a mesh: dp: 2 (over x), expert: 16 (over z, y, core).
Axes of the slice: x: 2, y: 2, z: 4, core: 2. Of those that a mesh axis runs over, the one named last changes fastest.
Arguments:
- expert_ids: int32 [1536, 8], P(('dp', 'expert')), may hold values from 0 to 15, all different within a row; in each aligned block of 48 rows (0 to 47, 48 to 95, ...) at most 36 rows name the same one
- route_probs: float32 [1536, 8], P(('dp', 'expert')), may hold values from 0.02 to 0.5
- expert_hidden: bfloat16 [2, 16, 16, 36, 768], P('dp', 'expert'), may hold values from -6 to 6
- down_weight: bfloat16 [16, 768, 4096], P('expert', None, 'dp'), may hold values from -0.21875 to 0.21875
- out_grad: bfloat16 [1536, 4096], P(('dp', 'expert')), may hold values from -0.75 to 0.75
Outputs:
- layer_out: bfloat16 [1536, 4096], P(('dp', 'expert'))
- prob_grad: float32 [1536, 8], P(('dp', 'expert'))
- hidden_grad: bfloat16 [2, 16, 16, 36, 768], P('dp', 'expert')
- weight_grad: float32 [16, 768, 4096], P('expert', None, 'dp')
The draws below stay inside these ranges and needn't reach their ends.
Inputs may be any that keep to these rules, and one draw needn't show every extreme that they name: `expert_ids`: each row names 8 different experts. Among the rows of one device no expert is named by more than 36 rows, and in every draw some device names some expert exactly 36 times.
All inputs are finite; a program needn't handle non-finite values.
Results may differ from the reference program's by a relative error of at most 0.0085.
Values may be sent and summed in bfloat16 or wider, within the bound.
No kernel may reach another device: no remote copies, remote signals or barrier semaphores. Data moves between devices by JAX's collectives and lax.ppermute only.
A program may use at most 128 MiB of HBM per device.

```python
import math
import jax
import jax.numpy as jnp
import numpy as np
from jax import lax

D = 4096
FF = 768
TOP = 8
TOK_DEV = 48
EXPERTS = 16
CAP = 36
TOKENS = 1536
N_DP = 2
N_EXPERT = 16


def levels(rng, dims, split, low, top_value):
    gain = 1.0
    for dim, blocks in split:
        heights = jax.random.uniform(jax.random.fold_in(jax.random.fold_in(rng, 6), dim), (blocks,), jnp.float32, low / len(split), top_value / len(split))
        gain = gain * jnp.repeat(jnp.exp(heights), dims[dim] // blocks).reshape((-1,) + (1,) * (len(dims) - 1 - dim))
    return gain


def shared_out(stream_key, own, number, rows, amount, top, most, lean):
    order = jax.random.permutation(stream_key, amount)
    packed, common = portions_of(amount, rows * top, most, lean, True), portions_of(amount, rows * top, most, lean, False)
    places = jnp.arange(amount)

    def named(sizes, offset_by):
        used = int((sizes > 0).sum())
        fixed = max(1, used // 4)
        passed = fixed + (places - fixed + offset_by * (used - fixed)) % max(1, amount - fixed)
        return jnp.zeros((amount,), jnp.int32).at[order[jnp.where(places < fixed, places, passed)]].set(jnp.asarray(sizes, jnp.int32))

    sizes = jnp.where(number % 4 == 0, named(packed, number // 4), named(common, number - number // 4 - 1))
    mixed = jax.random.permutation(jax.random.fold_in(own, 3), amount)
    giver, taker = mixed[0:amount // 2 * 2:2], mixed[1:amount // 2 * 2:2]
    room = jnp.minimum(sizes[giver] - 1, most - sizes[taker]) // 2
    room = jnp.where((giver == order[0]) | (taker == order[0]) | (sizes[taker] == 0), 0, jnp.maximum(room, 0))
    passed = jax.random.randint(jax.random.fold_in(own, 4), (amount // 2,), 0, 1 << 20) % (room + 1)
    sizes = sizes.at[giver].add(-passed).at[taker].add(passed)
    labels = jnp.searchsorted(jnp.cumsum(sizes), jnp.arange(rows * top), side="right").astype(jnp.int32)
    grid = labels.reshape(top, rows).T
    grid = grid[jax.random.permutation(jax.random.fold_in(own, 1), rows)]
    offset_by = jax.random.randint(jax.random.fold_in(own, 2), (rows, 1), 0, top)
    return jnp.take_along_axis(grid, (jnp.arange(top)[None, :] + offset_by) % top, axis=1)


def portions_of(count, total, reach, skew, full):
    weights = [(1 << 20) // math.isqrt(rank ** skew) + 1 for rank in range(1, count + 1)]
    largest = reach if full else min(reach, max(-(-total // count), total * weights[0] // sum(weights)))
    least = 1 if total - largest >= count - 1 else 0
    counts, surplus = [largest] + [least] * (count - 1), total - largest - least * (count - 1)
    while surplus > 0:
        free = [i for i in range(1, count) if counts[i] < largest] or [i for i in range(1, count) if counts[i] < reach]
        pool, budget = sum([weights[i] for i in free]), surplus
        for i in free:
            extra = min(reach - counts[i], max(1, budget * weights[i] // pool), surplus)
            counts[i] = counts[i] + extra
            surplus = surplus - extra
    return np.array(counts)


def gaussian(stream_key, extent, width, reach, split=(), kind=jnp.bfloat16):
    result = jax.random.normal(stream_key, extent, jnp.float32) * width
    if len(split) > 0:
        result = levels(stream_key, extent, split, -0.22, 0.18) * result
    return jnp.clip(result, min=-reach, max=reach).astype(kind)


def setup_inputs(seed: int = 0) -> dict:
    seeds = jax.random.split(jax.random.key(seed), 6)
    expert_ids_keys = jax.random.split(jax.random.fold_in(seeds[0], 1), TOKENS // TOK_DEV)
    expert_ids_turns = jax.random.permutation(jax.random.fold_in(seeds[0], 3), TOKENS // TOK_DEV)
    expert_ids = jax.vmap(lambda own, number: shared_out(jax.random.fold_in(seeds[0], 2), own, number, TOK_DEV, EXPERTS, TOP, CAP, 1))(expert_ids_keys, expert_ids_turns).reshape((TOKENS, TOP))
    route_probs = jnp.clip(jnp.exp(math.log(0.5) - 3.218876 * jax.random.uniform(seeds[1], (TOKENS, TOP), jnp.float32) ** levels(seeds[1], (TOKENS, TOP), ((0, 32),), -0.2, 0.2)), 0.02, 0.5)
    expert_hidden = gaussian(seeds[2], (N_DP, EXPERTS, N_EXPERT, CAP, FF), 1.0, 6.0, ((0, 2), (1, 16)))
    down_weight = gaussian(seeds[3], (EXPERTS, FF, D), FF ** -0.5, 0.21875, ((0, 16), (2, 2)))
    out_grad = gaussian(seeds[4], (TOKENS, D), 0.125, 0.75, ((0, 32),))
    return {"expert_ids": expert_ids, "route_probs": route_probs, "expert_hidden": expert_hidden, "down_weight": down_weight, "out_grad": out_grad}


def reference(expert_ids, route_probs, expert_hidden, down_weight, out_grad):
    blocks = N_DP * N_EXPERT
    routes = TOK_DEV * TOP
    route_ids = expert_ids.reshape(blocks, routes).astype(jnp.int32)
    onehot = (route_ids[:, :, None] == jnp.arange(EXPERTS, dtype=jnp.int32)[None, None, :]).astype(jnp.int32)
    earlier = jnp.cumsum(onehot, axis=1) - onehot
    position = jnp.sum(earlier * onehot, axis=2).astype(jnp.int32)
    block_index = jnp.broadcast_to(jnp.arange(blocks, dtype=jnp.int32)[:, None], (blocks, routes))
    route_index = jnp.broadcast_to(jnp.arange(routes, dtype=jnp.int32)[None, :], (blocks, routes))
    slot_route = jnp.full((blocks, EXPERTS, CAP), -1, dtype=jnp.int32)
    slot_route = slot_route.at[block_index, route_ids, position].set(route_index)
    slot_route = slot_route.reshape(N_DP, N_EXPERT, EXPERTS, CAP).transpose(0, 2, 1, 3)
    probs_blocks = route_probs.reshape(N_DP, N_EXPERT, routes)
    grads_blocks = out_grad.reshape(N_DP, N_EXPERT, TOK_DEV, D)
    sources = jnp.arange(N_EXPERT, dtype=jnp.int32)[:, None]

    def step(carry, expert):
        layer_acc, prob_acc = carry
        weight = lax.dynamic_index_in_dim(down_weight, expert, 0, keepdims=False)
        grads_out = []
        weight_sum = jnp.zeros((FF, D), jnp.float32)
        for replica in range(N_DP):
            owners = lax.dynamic_index_in_dim(slot_route[replica], expert, 0, keepdims=False)
            filled = owners >= 0
            safe_owner = jnp.maximum(owners, 0)
            slot_token = safe_owner // TOP
            hidden_rows = lax.dynamic_index_in_dim(expert_hidden[replica], expert, 0, keepdims=False).reshape(N_EXPERT * CAP, FF)
            slot_out = jnp.dot(hidden_rows, weight, preferred_element_type=jnp.float32).astype(jnp.bfloat16)
            slot_cube = slot_out.reshape(N_EXPERT, CAP, D).astype(jnp.float32)
            slot_prob = jnp.where(filled, probs_blocks[replica][sources, safe_owner], jnp.float32(0.0))
            slot_cot = grads_blocks[replica][sources, slot_token].astype(jnp.float32)
            layer_acc = layer_acc.at[replica, sources, slot_token].add(slot_prob[:, :, None] * slot_cube)
            inner = jnp.sum(slot_cot * slot_cube, axis=2)
            prob_acc = prob_acc.at[replica, sources, safe_owner].add(jnp.where(filled, inner, jnp.float32(0.0)))
            scaled = (slot_prob[:, :, None] * slot_cot).astype(jnp.bfloat16).reshape(N_EXPERT * CAP, D)
            back = jnp.dot(scaled, weight.T, preferred_element_type=jnp.float32).astype(jnp.bfloat16)
            grads_out.append(back.reshape(N_EXPERT, CAP, FF))
            partial_value = jnp.dot(hidden_rows.T, scaled, preferred_element_type=jnp.float32).astype(jnp.bfloat16)
            weight_sum = weight_sum + partial_value.astype(jnp.float32)
        return (layer_acc, prob_acc), (jnp.stack(grads_out), weight_sum)

    start = (jnp.zeros((N_DP, N_EXPERT, TOK_DEV, D), jnp.float32), jnp.zeros((N_DP, N_EXPERT, routes), jnp.float32))
    (layer_acc, prob_acc), (grads_all, weight_grad) = lax.scan(step, start, jnp.arange(EXPERTS, dtype=jnp.int32))
    layer_out = layer_acc.reshape(TOKENS, D).astype(jnp.bfloat16)
    prob_grad = prob_acc.reshape(TOKENS, TOP)
    hidden_grad = grads_all.transpose(1, 0, 2, 3, 4)
    return layer_out, prob_grad, hidden_grad, weight_grad
```

```python
import jax
import jax.numpy as jnp
from jax import lax
from jax.sharding import PartitionSpec as P


def dot(a, b, ca, cb):
    return lax.dot_general(a, b, (((ca,), (cb,)), ((), ())), preferred_element_type=jnp.float32)


def shards(expert_ids, route_probs, expert_hidden, down_weight, out_grad):
    tok, _ = expert_ids.shape
    n_dp = lax.axis_size("dp")
    n_ex = lax.axis_size("expert")
    cap = expert_hidden.shape[3]
    ff = down_weight.shape[1]
    width = down_weight.shape[2]
    weight = down_weight[0]
    me_dp = lax.axis_index("dp")

    names = expert_ids[:, :, None] == jnp.arange(n_ex, dtype=jnp.int32)[None, None, :]
    table = jnp.sum(jnp.where(names, route_probs[:, :, None], 0.0), axis=1)
    mine = lax.all_to_all(table.T, "expert", 0, 0, tiled=True)
    mine = lax.all_gather(mine, "dp", axis=0)
    taken = (mine > 0.0).astype(jnp.float32)
    earlier = jnp.tril(jnp.ones((tok, tok), jnp.float32), -1)
    place = jnp.einsum("nst,ut->nsu", taken, earlier).astype(jnp.int32)
    place = jnp.where(mine > 0.0, place, -1)

    grads = out_grad.reshape(tok, n_dp, width).transpose(1, 0, 2)
    grads = lax.all_to_all(grads, "dp", 0, 0, tiled=True)
    grads = lax.all_gather(grads, "expert", axis=0)
    rows = grads.reshape(n_ex * n_dp * tok, width)

    hidden = expert_hidden[0, 0].transpose(1, 0, 2).reshape(cap * n_ex, ff)
    hidden = lax.all_gather(hidden, "dp", axis=0)

    slot_c = jnp.arange(cap * n_ex, dtype=jnp.int32) // n_ex
    slot_s = jnp.arange(cap * n_ex, dtype=jnp.int32) % n_ex
    source = jnp.arange(n_ex, dtype=jnp.int32)
    pick = (place.reshape(n_dp, n_ex, tok, 1) == slot_c) & (source[None, :, None, None] == slot_s)
    pick = pick.reshape(n_dp, n_ex * tok, cap * n_ex).astype(jnp.bfloat16)
    held = jnp.einsum("ntr,nrf->ntf", pick, hidden)
    held = held.reshape(n_dp, n_ex, tok, ff).transpose(1, 0, 2, 3)
    prob_rows = mine.transpose(1, 0, 2)[..., None]
    scaled = (held * prob_rows).astype(jnp.bfloat16).reshape(-1, ff)

    part = dot(scaled, weight, 1, 0).astype(jnp.bfloat16)
    part = part.reshape(n_ex, n_dp, tok, width)
    layer = lax.psum_scatter(part, "expert", scatter_dimension=0, tiled=True)[0]
    layer = lax.all_to_all(layer, "dp", 0, 0, tiled=True)
    layer_out = layer.transpose(1, 0, 2).reshape(tok, n_dp * width)

    layer, rows = lax.optimization_barrier((layer, rows))
    back = dot(rows, weight, 1, 1).astype(jnp.bfloat16).reshape(n_ex, n_dp, tok, ff)
    inner = jnp.sum(back.astype(jnp.float32) * held, axis=3)
    inner = lax.psum_scatter(inner.transpose(1, 0, 2), "dp", scatter_dimension=0, tiled=True)[0]
    inner = lax.all_to_all(inner, "expert", 0, 0, tiled=True).T
    prob_grad = jnp.sum(jnp.where(names, inner[:, None, :], 0.0), axis=2)

    spread = (back * prob_rows).astype(jnp.bfloat16).transpose(1, 0, 2, 3)
    spread = spread.reshape(n_dp, n_ex * tok, ff)
    spread = jnp.einsum("ntr,ntf->nrf", pick, spread, preferred_element_type=jnp.float32)
    spread = lax.all_to_all(spread.astype(jnp.bfloat16), "dp", 0, 0, tiled=True)
    hidden_grad = jnp.sum(spread.astype(jnp.float32), axis=0).astype(jnp.bfloat16)
    hidden_grad = hidden_grad.reshape(cap, n_ex, ff).transpose(1, 0, 2)[None, None]

    weight_grad = dot(scaled, rows, 0, 0)[None]
    return (layer_out, prob_grad, hidden_grad, weight_grad)


def solution(mesh):
    placed = (
        P(("dp", "expert"), None),
        P(("dp", "expert"), None),
        P("dp", "expert", None, None, None),
        P("expert", None, "dp"),
        P(("dp", "expert"), None),
    )
    return jax.shard_map(
        shards,
        mesh=mesh,
        in_specs=placed,
        out_specs=(
            P(("dp", "expert"), None),
            P(("dp", "expert"), None),
            P("dp", "expert", None, None, None),
            P("expert", None, "dp"),
        ),
        check_vma=False,
    )
```

```python
import jax
import jax.numpy as jnp
import numpy as np
from jax import lax
from jax.sharding import PartitionSpec as P


def dot(a, b, ca, cb):
    return lax.dot_general(a, b, (((ca,), (cb,)), ((), ())), preferred_element_type=jnp.float32)


def chip_ring(mesh):
    chips = mesh.shape["expert"] // 2
    devices = mesh.devices.reshape(mesh.shape["dp"], -1)
    if not hasattr(devices[0, 0], "coords"):
        return list(range(chips))
    at = [tuple(devices[0, 2 * chip].coords)[1:] for chip in range(chips)]
    rows = max(z for _, z in at) + 1
    cols = max(y for y, _ in at) + 1
    if rows * cols != chips or rows % 2:
        return list(range(chips))
    walk = [(0, z) for z in range(rows)]
    for step, z in enumerate(reversed(range(rows))):
        span = range(1, cols)
        walk += [(y, z) for y in (span if step % 2 == 0 else reversed(span))]
    return [at.index(place) for place in walk]


def body(ring):
    chips = len(ring)
    half = chips // 2
    offsets = [0]
    for step in range(1, half):
        offsets += [-step, step]
    offsets.append(half)
    lookup = np.zeros((chips,), np.int32)
    lookup[np.asarray(ring)] = np.arange(chips)

    def along(step):
        pairs = []
        for at in range(chips):
            for core in range(2):
                pairs.append((2 * ring[at] + core, 2 * ring[(at + step) % chips] + core))
        return pairs

    forward, backward = along(1), along(-1)
    sibling = [(e, e ^ 1) for e in range(2 * chips)]

    def shards(expert_ids, route_probs, expert_hidden, down_weight, out_grad):
        tok, top = expert_ids.shape
        n_dp = lax.axis_size("dp")
        n_ex = lax.axis_size("expert")
        cap = expert_hidden.shape[3]
        slots = cap * n_ex
        ff = down_weight.shape[1]
        width = down_weight.shape[2]
        weight = down_weight[0]
        replica = lax.axis_index("dp")
        expert = lax.axis_index("expert")
        core = expert % 2
        place = jnp.asarray(lookup)[expert // 2]
        groups = [list(range(n_dp // 2)), list(range(n_dp // 2, n_dp))]
        per = n_dp // 2

        def shift(value, step):
            return lax.ppermute(value, "dp", [(i, (i + step) % n_dp) for i in range(n_dp)])

        def ring_send(value, step):
            return lax.ppermute(value, "expert", forward if step > 0 else backward)

        def swap(value):
            return lax.ppermute(value, "expert", sibling)

        table = jnp.asarray(np.asarray(ring, np.int32))
        order = []
        for off in offsets:
            for other in range(2):
                order.append(2 * table[(place + off) % chips] + (core ^ other))
        order = jnp.stack(order)

        facts = jnp.concatenate([expert_ids.astype(jnp.float32), route_probs], axis=1).T
        facts = lax.all_gather(facts, ("dp", "expert"), axis=0)
        names = facts[:, :top] == expert.astype(jnp.float32)
        probs = jnp.sum(jnp.where(names, facts[:, top:], 0.0), axis=1).reshape(n_dp, n_ex, tok)
        taken = (probs > 0.0).astype(jnp.float32)
        earlier = jnp.tril(jnp.ones((tok, tok), jnp.float32), -1)
        position = jnp.einsum("nst,ut->nsu", taken, earlier).astype(jnp.int32)
        position = jnp.where(probs > 0.0, position, -1)

        shard_of = lambda d: lax.dynamic_slice_in_dim(
            out_grad, ((replica + d) % n_dp) * width, width, axis=1
        )
        exchanged = [shard_of(0)] + [shift(shard_of(d), d) for d in range(1, n_dp)]
        seed = [jnp.stack([exchanged[d] for d in group]) for group in groups]
        blocks = {0: list(seed)}
        for step in range(1, half):
            blocks[-step] = [ring_send(blocks[1 - step][g], 1) for g in range(2)]
            blocks[step] = [ring_send(blocks[step - 1][g], -1) for g in range(2)]
        blocks[half] = [ring_send(blocks[1 - half][0], 1), ring_send(blocks[half - 1][1], -1)]

        hidden = expert_hidden[0, 0].transpose(1, 0, 2).reshape(slots, ff)
        hiddens = [hidden] + [shift(hidden, d) for d in range(1, n_dp)]

        slot_c = jnp.arange(slots, dtype=jnp.int32) // n_ex
        slot_s = jnp.arange(slots, dtype=jnp.int32) % n_ex
        picks, helds, scaleds, prob_rows, parts = [], [], [], [], []
        for d in range(n_dp):
            at = (replica - d) % n_dp
            position_d = lax.dynamic_index_in_dim(position, at, 0, keepdims=False)[order]
            prob_d = lax.dynamic_index_in_dim(probs, at, 0, keepdims=False)[order]
            pick = (position_d[:, :, None] == slot_c) & (order[:, None, None] == slot_s)
            pick = pick.reshape(n_ex * tok, slots).astype(jnp.bfloat16)
            held = dot(pick, hiddens[d], 1, 0)
            prob_row = prob_d.reshape(n_ex * tok, 1)
            scaled = (held * prob_row).astype(jnp.bfloat16)
            part = dot(scaled, weight, 1, 0).astype(jnp.bfloat16)
            picks.append(pick)
            helds.append(held.astype(jnp.bfloat16))
            scaleds.append(scaled)
            prob_rows.append(prob_row)
            parts.append(part.reshape(chips, 2, tok, width))

        own = [jnp.stack([parts[d][:, 0] for d in group], axis=1) for group in groups]
        other = [swap(jnp.stack([parts[d][:, 1] for d in group], axis=1)) for group in groups]

        def term(off, g):
            index = offsets.index(off)
            return own[g][index].astype(jnp.float32) + other[g][index].astype(jnp.float32)

        arrived = {}
        for g in range(2):
            for direction in (1, -1):
                first = half if (direction == 1) == (g == 0) else half - 1
                carry = None
                for hop in range(first, 0, -1):
                    off = half if hop == half else hop * direction
                    value = term(off, g)
                    if carry is not None:
                        value = value + carry.astype(jnp.float32)
                    carry = ring_send(value.astype(jnp.bfloat16), direction)
                arrived[g, direction] = carry
        layer_out = jnp.zeros((tok, n_dp * width), jnp.bfloat16)
        for g, group in enumerate(groups):
            total = term(0, g) + arrived[g, 1].astype(jnp.float32)
            total = (total + arrived[g, -1].astype(jnp.float32)).astype(jnp.bfloat16)
            for i, d in enumerate(group):
                piece = total[i] if d == 0 else shift(total[i], -d)
                layer_out = lax.dynamic_update_slice_in_dim(
                    layer_out, piece, ((replica + d) % n_dp) * width, axis=1
                )

        others = {off: [swap(value) for value in blocks[off]] for off in offsets}
        weight_sum = None
        spreads, inners = [], []
        for d in range(n_dp):
            g, i = divmod(d, per)
            rows = jnp.concatenate(
                [x for off in offsets for x in (blocks[off][g][i], others[off][g][i])], axis=0
            )
            back = dot(rows, weight, 1, 1)
            inners.append(jnp.sum(back * helds[d].astype(jnp.float32), axis=1))
            spread = (back * prob_rows[d]).astype(jnp.bfloat16)
            spreads.append(dot(picks[d], spread, 0, 0).astype(jnp.bfloat16))
            more = dot(scaleds[d], rows, 0, 0)
            weight_sum = more if weight_sum is None else weight_sum + more
        hidden_sum = spreads[0].astype(jnp.float32)
        for d in range(1, n_dp):
            hidden_sum = hidden_sum + shift(spreads[d], -d).astype(jnp.float32)
        hidden_grad = hidden_sum.astype(jnp.bfloat16).reshape(cap, n_ex, ff).transpose(1, 0, 2)

        inverse = jnp.argsort(order)
        inner = jnp.stack(inners)[(replica - jnp.arange(n_dp)) % n_dp].reshape(n_dp, n_ex, tok)
        inner = inner[:, inverse].reshape(n_dp * n_ex, tok)
        inner = lax.all_to_all(inner, ("dp", "expert"), 0, 0, tiled=True)
        inner = jnp.sum(inner.reshape(n_dp, n_ex, tok), axis=0)
        mine = expert_ids[:, :, None] == jnp.arange(n_ex, dtype=jnp.int32)
        prob_grad = jnp.sum(jnp.where(mine, inner.T[:, None, :], 0.0), axis=2)
        return (layer_out, prob_grad, hidden_grad[None, None], weight_sum[None])

    return shards


def solution(mesh):
    placed = (
        P(("dp", "expert"), None),
        P(("dp", "expert"), None),
        P("dp", "expert", None, None, None),
        P("expert", None, "dp"),
        P(("dp", "expert"), None),
    )
    return jax.shard_map(
        body(chip_ring(mesh)),
        mesh=mesh,
        in_specs=placed,
        out_specs=(
            P(("dp", "expert"), None),
            P(("dp", "expert"), None),
            P("dp", "expert", None, None, None),
            P("expert", None, "dp"),
        ),
        check_vma=False,
    )
```

```python
import jax
import jax.numpy as jnp
from jax import lax
from jax.sharding import PartitionSpec as P


def dot(a, b, ca, cb):
    return lax.dot_general(a, b, (((ca,), (cb,)), ((), ())), preferred_element_type=jnp.float32)


def shards(expert_ids, route_probs, expert_hidden, down_weight, out_grad):
    tok, top = expert_ids.shape
    n_dp = lax.axis_size("dp")
    n_ex = lax.axis_size("expert")
    chips = n_ex // 2
    cap = expert_hidden.shape[3]
    slots = cap * n_ex
    ff = down_weight.shape[1]
    width = down_weight.shape[2]
    weight = down_weight[0]
    replica = lax.axis_index("dp")
    expert = lax.axis_index("expert")
    core = expert % 2
    rows = chips * tok
    same_core = [[2 * chip + c for chip in range(chips)] for c in range(2)]
    sibling = [(e, e ^ 1) for e in range(n_ex)]

    def shift(value, step):
        return lax.ppermute(value, "dp", [(i, (i + step) % n_dp) for i in range(n_dp)])

    def swap(value):
        return lax.ppermute(value, "expert", sibling)

    def width_shard(d):
        at = ((replica + d) % n_dp) * width
        return lax.dynamic_slice_in_dim(out_grad, at, width, axis=1)

    grads = []
    for d in range(n_dp):
        piece = width_shard(0) if d == 0 else shift(width_shard(d), d)
        piece = lax.all_gather(piece, "expert", axis=0, axis_index_groups=same_core)
        grads.append(piece.reshape(rows, width))

    weights = jnp.concatenate([weight, swap(weight)], axis=0)
    hidden = expert_hidden[0, 0].transpose(1, 0, 2).reshape(slots, ff)
    hiddens = [hidden, swap(hidden)]

    names = expert_ids.T[None] == jnp.arange(n_ex, dtype=jnp.int32)[:, None, None]
    table = jnp.sum(jnp.where(names, route_probs.T[None], 0.0), axis=1)
    table = lax.all_to_all(
        table.reshape(chips, 2, tok), "expert", 0, 0, tiled=True, axis_index_groups=same_core
    )
    table = jnp.where(core == 0, table, table[:, ::-1])
    taken = (table > 0.0).astype(jnp.float32)
    earlier = jnp.tril(jnp.ones((tok, tok), jnp.float32), -1)
    position = jnp.einsum("set,ut->seu", taken, earlier).astype(jnp.int32)
    position = jnp.where(table > 0.0, position, -1)

    slot_c = jnp.arange(slots, dtype=jnp.int32) // n_ex
    slot_s = jnp.arange(slots, dtype=jnp.int32) % n_ex
    source = 2 * jnp.arange(chips, dtype=jnp.int32) + core
    here = source[:, None, None] == slot_s
    picks, helds, prob_rows = [], [], []
    for x in range(2):
        pick = (position[:, x, :, None] == slot_c) & here
        pick = pick.reshape(rows, slots).astype(jnp.bfloat16)
        picks.append(pick)
        helds.append(dot(pick, hiddens[x], 1, 0).astype(jnp.bfloat16))
        prob_rows.append(table[:, x].reshape(rows, 1))
    scaled = jnp.concatenate(
        [(helds[x].astype(jnp.float32) * prob_rows[x]).astype(jnp.bfloat16) for x in range(2)], axis=1
    )
    scaleds = [scaled] + [shift(scaled, d) for d in range(1, n_dp)]

    layer_out = jnp.zeros((tok, n_dp * width), jnp.bfloat16)
    for d in range(n_dp):
        part = dot(scaleds[d], weights, 1, 0).astype(jnp.bfloat16)
        piece = lax.psum_scatter(
            part.reshape(chips, tok, width), "expert", scatter_dimension=0, axis_index_groups=same_core
        )
        piece = piece if d == 0 else shift(piece, -d)
        layer_out = lax.dynamic_update_slice_in_dim(
            layer_out, piece, ((replica + d) % n_dp) * width, axis=1
        )

    back = dot(grads[0], weights, 1, 1)
    for d in range(1, n_dp):
        part = dot(grads[d], weights, 1, 1).astype(jnp.bfloat16)
        back = back + shift(part, -d).astype(jnp.float32)
    spreads, inners = [], []
    for x in range(2):
        mine = back[:, x * ff : (x + 1) * ff]
        inners.append(jnp.sum(mine * helds[x].astype(jnp.float32), axis=1).reshape(chips, tok))
        mine = (mine * prob_rows[x]).astype(jnp.bfloat16)
        spreads.append(dot(picks[x], mine, 0, 0).astype(jnp.bfloat16))
    hidden_grad = spreads[0] + swap(spreads[1])
    hidden_grad = hidden_grad.reshape(cap, n_ex, ff).transpose(1, 0, 2)[None, None]

    total = dot(scaleds[0], grads[0], 0, 0)
    for d in range(1, n_dp):
        total = total + dot(scaleds[d], grads[d], 0, 0)
    weight_grad = total[:ff] + swap(total[ff:].astype(jnp.bfloat16)).astype(jnp.float32)

    inner = jnp.stack(inners, axis=1)
    inner = jnp.where(core == 0, inner, inner[:, ::-1])
    inner = lax.all_to_all(inner, "expert", 0, 0, tiled=True, axis_index_groups=same_core)
    inner = inner.reshape(n_ex, tok)
    mine = expert_ids[:, :, None] == jnp.arange(n_ex, dtype=jnp.int32)
    prob_grad = jnp.sum(jnp.where(mine, inner.T[:, None, :], 0.0), axis=2)
    return (layer_out, prob_grad, hidden_grad, weight_grad[None])


def solution(mesh):
    placed = (
        P(("dp", "expert"), None),
        P(("dp", "expert"), None),
        P("dp", "expert", None, None, None),
        P("expert", None, "dp"),
        P(("dp", "expert"), None),
    )
    return jax.shard_map(
        shards,
        mesh=mesh,
        in_specs=placed,
        out_specs=(
            P(("dp", "expert"), None),
            P(("dp", "expert"), None),
            P("dp", "expert", None, None, None),
            P("expert", None, "dp"),
        ),
        check_vma=False,
    )
```

```python
import functools

import jax
import jax.numpy as jnp
import numpy as np
from jax import lax
from jax.experimental import pallas as pl
from jax.experimental.pallas import tpu as pltpu
from jax.sharding import PartitionSpec as P

VMEM_BYTES = 48 * 1024 * 1024


def dot(a, b, ca, cb):
    return lax.dot_general(a, b, (((ca,), (cb,)), ((), ())), preferred_element_type=jnp.float32)


def after(value, *done):
    return lax.optimization_barrier((value, *done))[0]


def chip_ring(mesh):
    chips = mesh.shape["expert"] // 2
    devices = mesh.devices.reshape(mesh.shape["dp"], -1)
    if not hasattr(devices[0, 0], "coords"):
        return list(range(chips))
    at = [tuple(devices[0, 2 * chip].coords)[1:] for chip in range(chips)]
    rows = max(z for _, z in at) + 1
    cols = max(y for y, _ in at) + 1
    if rows * cols != chips or rows % 2:
        return list(range(chips))
    walk = [(0, z) for z in range(rows)]
    for step, z in enumerate(reversed(range(rows))):
        span = range(1, cols)
        walk += [(y, z) for y in (span if step % 2 == 0 else reversed(span))]
    return [at.index(place) for place in walk]


def back_kernel(n_blocks, *refs):
    blocks, w_ref, out_ref = refs[:n_blocks], refs[n_blocks], refs[n_blocks + 1]
    n_dp, tok, _ = blocks[0].shape
    for d in range(n_dp):
        rows = jnp.concatenate([block[d] for block in blocks], axis=0)
        out_ref[d] = dot(rows, w_ref[...], 1, 1).astype(jnp.bfloat16)


def back_product(blocks, weights):
    n_dp, tok, width = blocks[0].shape
    ff2 = weights.shape[0]
    rows = len(blocks) * tok
    tile = 256
    return pl.pallas_call(
        functools.partial(back_kernel, len(blocks)),
        grid=(ff2 // tile,),
        in_specs=[
            pl.BlockSpec((n_dp, tok, width), lambda i: (0, 0, 0), pipeline_mode=pl.Buffered(1))
            for _ in blocks
        ]
        + [pl.BlockSpec((tile, width), lambda i: (i, 0))],
        out_specs=pl.BlockSpec((n_dp, rows, tile), lambda i: (0, 0, i)),
        out_shape=jax.ShapeDtypeStruct((n_dp, rows, ff2), jnp.bfloat16),
        compiler_params=pltpu.CompilerParams(vmem_limit_bytes=VMEM_BYTES),
        cost_estimate=pl.CostEstimate(
            flops=2 * n_dp * rows * width * ff2,
            bytes_accessed=2 * (n_dp * rows * (width + ff2) + ff2 * width),
            transcendentals=0,
        ),
        name="back_product",
    )(*blocks, weights)


def weight_kernel(n_blocks, n_dp, *refs):
    blocks, held = refs[:n_blocks], refs[n_blocks : n_blocks + n_dp]
    own_ref, other_ref = refs[n_blocks + n_dp :]
    ff = own_ref.shape[0]
    own, other = None, None
    for d in range(n_dp):
        rows = jnp.concatenate([block[d] for block in blocks], axis=0)
        mine = dot(held[d][:ff, :], rows, 1, 0)
        theirs = dot(held[d][ff:, :], rows, 1, 0)
        own = mine if own is None else own + mine
        other = theirs if other is None else other + theirs
    own_ref[...] = own
    other_ref[...] = other.astype(jnp.bfloat16)


def weight_product(blocks, helds):
    n_dp, tok, width = blocks[0].shape
    ff2, rows = helds[0].shape
    tile = 512
    return pl.pallas_call(
        functools.partial(weight_kernel, len(blocks), n_dp),
        grid=(width // tile,),
        in_specs=[pl.BlockSpec((n_dp, tok, tile), lambda i: (0, 0, i)) for _ in blocks]
        + [
            pl.BlockSpec((ff2, rows), lambda i: (0, 0), pipeline_mode=pl.Buffered(1))
            for _ in helds
        ],
        out_specs=[pl.BlockSpec((ff2 // 2, tile), lambda i: (0, i))] * 2,
        out_shape=[
            jax.ShapeDtypeStruct((ff2 // 2, width), jnp.float32),
            jax.ShapeDtypeStruct((ff2 // 2, width), jnp.bfloat16),
        ],
        compiler_params=pltpu.CompilerParams(vmem_limit_bytes=VMEM_BYTES),
        cost_estimate=pl.CostEstimate(
            flops=2 * n_dp * rows * width * ff2,
            bytes_accessed=2 * n_dp * rows * (width + ff2) + 3 * ff2 * width,
            transcendentals=0,
        ),
        name="weight_product",
    )(*blocks, *helds)


def body(ring):
    chips = len(ring)
    half = chips // 2
    offsets = [0]
    for step in range(1, half):
        offsets += [-step, step]
    offsets.append(half)
    place_of = {chip: at for at, chip in enumerate(ring)}
    order_table = np.asarray(
        [[ring[(place_of[c] + off) % chips] for off in offsets] for c in range(chips)], np.int32
    )
    inverse_table = np.argsort(order_table, axis=1).astype(np.int32)

    def along(step):
        return [
            (2 * ring[at] + core, 2 * ring[(at + step) % chips] + core)
            for at in range(chips)
            for core in range(2)
        ]

    forward, backward = along(1), along(-1)
    sibling = [(e, e ^ 1) for e in range(2 * chips)]
    same_core = [[2 * chip + c for chip in range(chips)] for c in range(2)]

    def shards(expert_ids, route_probs, expert_hidden, down_weight, out_grad):
        tok, top = expert_ids.shape
        n_dp = lax.axis_size("dp")
        n_ex = lax.axis_size("expert")
        cap = expert_hidden.shape[3]
        slots = cap * n_ex
        ff = down_weight.shape[1]
        width = down_weight.shape[2]
        weight = down_weight[0]
        replica = lax.axis_index("dp")
        expert = lax.axis_index("expert")
        core = expert % 2
        rows = chips * tok
        per = n_dp // 2
        groups = [list(range(per)), list(range(per, n_dp))]
        order = lax.dynamic_index_in_dim(jnp.asarray(order_table), expert // 2, 0, keepdims=False)
        inverse = lax.dynamic_index_in_dim(jnp.asarray(inverse_table), expert // 2, 0, keepdims=False)

        def shift(value, step):
            return lax.ppermute(value, "dp", [(i, (i + step) % n_dp) for i in range(n_dp)])

        def ring_send(value, step):
            return lax.ppermute(value, "expert", forward if step > 0 else backward)

        def swap(value):
            return lax.ppermute(value, "expert", sibling)

        def width_shard(d):
            at = ((replica + d) % n_dp) * width
            return lax.dynamic_slice_in_dim(out_grad, at, width, axis=1)

        blocks = {0: jnp.stack([width_shard(0)] + [shift(width_shard(d), d) for d in range(1, n_dp)])}
        for step in range(1, half):
            blocks[-step] = ring_send(blocks[1 - step], 1)
            blocks[step] = ring_send(blocks[step - 1], -1)
        blocks[half] = jnp.concatenate(
            [ring_send(blocks[1 - half][:per], 1), ring_send(blocks[half - 1][per:], -1)], axis=0
        )
        grads = [blocks[off] for off in offsets]

        weights = jnp.concatenate([weight, swap(weight)], axis=0)
        hidden = expert_hidden[0, 0].transpose(1, 0, 2).reshape(slots, ff)
        hiddens = [hidden, swap(hidden)]

        names = expert_ids.T[None] == jnp.arange(n_ex, dtype=jnp.int32)[:, None, None]
        table = jnp.sum(jnp.where(names, route_probs.T[None], 0.0), axis=1)
        table = lax.all_to_all(
            table.reshape(chips, 2, tok), "expert", 0, 0, tiled=True, axis_index_groups=same_core
        )
        table = jnp.where(core == 0, table, table[:, ::-1])[order]
        taken = (table > 0.0).astype(jnp.float32)
        earlier = jnp.tril(jnp.ones((tok, tok), jnp.float32), -1)
        position = jnp.einsum("set,ut->seu", taken, earlier).astype(jnp.int32)
        position = jnp.where(table > 0.0, position, -1)

        slot_c = jnp.arange(slots, dtype=jnp.int32) // n_ex
        slot_s = jnp.arange(slots, dtype=jnp.int32) % n_ex
        here = (2 * order + core)[:, None, None] == slot_s
        picks, helds, prob_rows = [], [], []
        for x in range(2):
            pick = (position[:, x, :, None] == slot_c) & here
            pick = pick.reshape(rows, slots).astype(jnp.bfloat16)
            picks.append(pick)
            helds.append(dot(hiddens[x], pick, 0, 1).astype(jnp.bfloat16))
            prob_rows.append(table[:, x].reshape(1, rows))
        scaled = jnp.concatenate(
            [(helds[x].astype(jnp.float32) * prob_rows[x]).astype(jnp.bfloat16) for x in range(2)],
            axis=0,
        )
        scaleds = [scaled] + [shift(scaled, d) for d in range(1, n_dp)]

        layer_out = jnp.zeros((tok, n_dp * width), jnp.bfloat16)
        for g, group in enumerate(groups):
            parts = [dot(scaleds[d], weights, 0, 0).astype(jnp.bfloat16) for d in group]
            parts = [part.reshape(chips, tok, width) for part in parts]

            def term(off):
                index = offsets.index(off)
                return jnp.stack([part[index] for part in parts])

            total = term(0).astype(jnp.float32)
            for direction in (1, -1):
                first = half if (direction == 1) == (g == 0) else half - 1
                carry = None
                for hop in range(first, 0, -1):
                    value = term(half if hop == half else hop * direction)
                    if carry is not None:
                        value = (value.astype(jnp.float32) + carry.astype(jnp.float32)).astype(jnp.bfloat16)
                    carry = ring_send(value, direction)
                total = total + carry.astype(jnp.float32)
            total = total.astype(jnp.bfloat16)
            for i, d in enumerate(group):
                piece = total[i] if d == 0 else shift(total[i], -d)
                layer_out = lax.dynamic_update_slice_in_dim(
                    layer_out, piece, ((replica + d) % n_dp) * width, axis=1
                )

        backs = back_product(grads, weights)
        back = backs[0].astype(jnp.float32)
        for d in range(1, n_dp):
            back = back + shift(backs[d], -d).astype(jnp.float32)
        spreads, inners = [], []
        for x in range(2):
            mine = back[:, x * ff : (x + 1) * ff]
            inner = jnp.sum(mine * helds[x].T.astype(jnp.float32), axis=1)
            inners.append(inner.reshape(chips, tok))
            mine = (mine * prob_rows[x].reshape(rows, 1)).astype(jnp.bfloat16)
            spreads.append(dot(picks[x], mine, 0, 0).astype(jnp.bfloat16))
        hidden_grad = spreads[0] + swap(spreads[1])
        hidden_grad = hidden_grad.reshape(cap, n_ex, ff).transpose(1, 0, 2)[None, None]

        own, other = weight_product(grads, scaleds)
        weight_grad = own + swap(other).astype(jnp.float32)

        inner = jnp.stack(inners, axis=1)[inverse]
        inner = jnp.where(core == 0, inner, inner[:, ::-1])
        inner = lax.all_to_all(inner, "expert", 0, 0, tiled=True, axis_index_groups=same_core)
        inner = inner.reshape(n_ex, tok)
        mine = expert_ids[:, :, None] == jnp.arange(n_ex, dtype=jnp.int32)
        prob_grad = jnp.sum(jnp.where(mine, inner.T[:, None, :], 0.0), axis=2)
        return (layer_out, prob_grad, hidden_grad, weight_grad[None])

    return shards


def solution(mesh):
    placed = (
        P(("dp", "expert"), None),
        P(("dp", "expert"), None),
        P("dp", "expert", None, None, None),
        P("expert", None, "dp"),
        P(("dp", "expert"), None),
    )
    return jax.shard_map(
        body(chip_ring(mesh)),
        mesh=mesh,
        in_specs=placed,
        out_specs=(
            P(("dp", "expert"), None),
            P(("dp", "expert"), None),
            P("dp", "expert", None, None, None),
            P("expert", None, "dp"),
        ),
        check_vma=False,
    )
```

```python
import functools

import jax
import jax.numpy as jnp
import numpy as np
from jax import lax
from jax.experimental import pallas as pl
from jax.experimental.pallas import tpu as pltpu
from jax.sharding import PartitionSpec as P

VMEM_BYTES = 48 * 1024 * 1024


def dot(a, b, ca, cb):
    return lax.dot_general(a, b, (((ca,), (cb,)), ((), ())), preferred_element_type=jnp.float32)


def after(value, *done):
    return lax.optimization_barrier((value, *done))[0]


def chip_ring(mesh):
    chips = mesh.shape["expert"] // 2
    devices = mesh.devices.reshape(mesh.shape["dp"], -1)
    if not hasattr(devices[0, 0], "coords"):
        return list(range(chips))
    at = [tuple(devices[0, 2 * chip].coords)[1:] for chip in range(chips)]
    rows = max(z for _, z in at) + 1
    cols = max(y for y, _ in at) + 1
    if rows * cols != chips or rows % 2:
        return list(range(chips))
    walk = [(0, z) for z in range(rows)]
    for step, z in enumerate(reversed(range(rows))):
        span = range(1, cols)
        walk += [(y, z) for y in (span if step % 2 == 0 else reversed(span))]
    return [at.index(place) for place in walk]


def forward_kernel(keep, rows_of, table, hid_own, hid_sib, w_own, w_sib, *refs):
    part, scaled = refs[:2]
    held, index, prob = refs[2:5] if keep else (None, None, None)
    picked, facts = refs[-2:]
    n_ex, tok = table.shape
    chips = n_ex // 2
    slots = hid_own.shape[0]
    rows = chips * tok

    @pl.when(pl.program_id(0) == 0)
    def _():
        for j in range(n_ex):
            facts[j : j + 1, :] = table[pl.ds(rows_of[j], 1), :]
        weights = facts[...]
        taken = (weights > 0.0).astype(jnp.float32)
        row = lax.broadcasted_iota(jnp.int32, (tok, tok), 0)
        col = lax.broadcasted_iota(jnp.int32, (tok, tok), 1)
        position = dot((col < row).astype(jnp.float32), taken, 1, 1).astype(jnp.int32)
        column = lax.dot_general(
            (col == row).astype(jnp.float32),
            weights,
            (((1,), (1,)), ((), ())),
            precision=lax.Precision.HIGHEST,
            preferred_element_type=jnp.float32,
        )
        lane = lax.broadcasted_iota(jnp.int32, (tok, slots), 1)
        for x, hid in enumerate((hid_own, hid_sib)):
            columns = []
            for o in range(chips):
                j = x * chips + o
                here = column[:, j : j + 1]
                slot = jnp.where(here > 0.0, position[:, j : j + 1] * n_ex + rows_of[o], -1)
                picked[x, o * tok : (o + 1) * tok, :] = (lane == slot).astype(jnp.bfloat16)
                columns.append(here)
                if keep:
                    index[o * tok : (o + 1) * tok, x : x + 1] = slot
                    prob[o * tok : (o + 1) * tok, x : x + 1] = here
            found = dot(picked[x], hid[...], 1, 0)
            if keep:
                held[x] = found.astype(jnp.bfloat16)
            scaled[x] = (found * jnp.concatenate(columns, axis=0)).astype(jnp.bfloat16)

    value = dot(scaled[0], w_own[...], 1, 0) + dot(scaled[1], w_sib[...], 1, 0)
    part[...] = value.astype(jnp.bfloat16).reshape(part.shape)


def forward_product(keep, rows_of, table, hid_own, hid_sib, w_own, w_sib):
    n_ex, tok = table.shape
    chips = n_ex // 2
    rows = chips * tok
    slots, ff = hid_own.shape
    width = w_own.shape[1]
    tile = 512
    whole = lambda shape: pl.BlockSpec(shape, lambda i: (0,) * len(shape))
    out_specs = [pl.BlockSpec((chips, tok, tile), lambda i: (0, 0, i)), whole((2, rows, ff))]
    out_shape = [
        jax.ShapeDtypeStruct((chips, tok, width), jnp.bfloat16),
        jax.ShapeDtypeStruct((2, rows, ff), jnp.bfloat16),
    ]
    if keep:
        out_specs += [whole((2, rows, ff)), whole((rows, 2)), whole((rows, 2))]
        out_shape += [
            jax.ShapeDtypeStruct((2, rows, ff), jnp.bfloat16),
            jax.ShapeDtypeStruct((rows, 2), jnp.int32),
            jax.ShapeDtypeStruct((rows, 2), jnp.float32),
        ]
    return pl.pallas_call(
        functools.partial(forward_kernel, keep),
        grid=(width // tile,),
        in_specs=[pl.BlockSpec(memory_space=pltpu.SMEM), whole((n_ex, tok))]
        + [whole((slots, ff))] * 2
        + [pl.BlockSpec((ff, tile), lambda i: (0, i))] * 2,
        out_specs=out_specs,
        out_shape=out_shape,
        scratch_shapes=[
            pltpu.VMEM((2, rows, slots), jnp.bfloat16),
            pltpu.VMEM((n_ex, tok), jnp.float32),
        ],
        compiler_params=pltpu.CompilerParams(vmem_limit_bytes=VMEM_BYTES),
        cost_estimate=pl.CostEstimate(
            flops=4 * rows * ff * (width + slots),
            bytes_accessed=4 * ff * (width + slots) + 2 * rows * (width + 2 * ff),
            transcendentals=0,
        ),
        name="forward_product",
    )(rows_of, table, hid_own, hid_sib, w_own, w_sib)


def gathered(refs, layout, d):
    return jnp.concatenate([refs[where][at] for where, at in (row[d] for row in layout)], axis=0)


def back_kernel(n_refs, layout, *refs):
    blocks, (w_own, w_sib), outs = refs[:n_refs], refs[n_refs : n_refs + 2], refs[n_refs + 2 :]
    for d, out in enumerate(outs):
        rows = gathered(blocks, layout, d)
        out[0] = dot(rows, w_own[...], 1, 1).astype(jnp.bfloat16)
        out[1] = dot(rows, w_sib[...], 1, 1).astype(jnp.bfloat16)


def back_product(blocks, layout, w_own, w_sib):
    n_dp = len(layout[0])
    _, tok, width = blocks[0].shape
    ff = w_own.shape[0]
    rows = len(layout) * tok
    tile = 256
    return pl.pallas_call(
        functools.partial(back_kernel, len(blocks), layout),
        grid=(ff // tile,),
        in_specs=[
            pl.BlockSpec(block.shape, lambda i: (0, 0, 0), pipeline_mode=pl.Buffered(1))
            for block in blocks
        ]
        + [pl.BlockSpec((tile, width), lambda i: (i, 0))] * 2,
        out_specs=[pl.BlockSpec((2, rows, tile), lambda i: (0, 0, i))] * n_dp,
        out_shape=[jax.ShapeDtypeStruct((2, rows, ff), jnp.bfloat16)] * n_dp,
        compiler_params=pltpu.CompilerParams(vmem_limit_bytes=VMEM_BYTES),
        cost_estimate=pl.CostEstimate(
            flops=4 * n_dp * rows * width * ff,
            bytes_accessed=2 * (n_dp * rows * (width + 2 * ff) + 2 * ff * width),
            transcendentals=0,
        ),
        name="back_product",
    )(*blocks, w_own, w_sib)


def spread_kernel(n_parts, n_dp, *refs):
    rows_of, index, prob, held = refs[:4]
    backs = refs[4 : 4 + n_parts * n_dp]
    own, other, inner = refs[4 + n_parts * n_dp :]
    n_ex, tok = inner.shape
    chips = n_ex // 2
    rows, slots = index.shape[0], own.shape[0]
    ones = jnp.ones((8, held.shape[2]), jnp.float32)
    lane = lax.broadcasted_iota(jnp.int32, (rows, slots), 1)
    for x, out in enumerate((own, other)):
        back = None
        for d in range(n_dp):
            pieces = [backs[d * n_parts + i][x] for i in range(n_parts)]
            value = jnp.concatenate(pieces, axis=0).astype(jnp.float32)
            back = value if back is None else back + value
        product = back * held[x].astype(jnp.float32)
        sums = lax.dot_general(
            ones,
            product,
            (((1,), (1,)), ((), ())),
            precision=lax.Precision.HIGHEST,
            preferred_element_type=jnp.float32,
        )
        for o in range(chips):
            inner[pl.ds(rows_of[x * chips + o], 1), :] = sums[:1, o * tok : (o + 1) * tok]
        pick = (lane == index[:, x : x + 1]).astype(jnp.bfloat16)
        mine = (back * prob[:, x : x + 1]).astype(jnp.bfloat16)
        out[...] = dot(pick, mine, 0, 0).astype(jnp.bfloat16)


def spread_product(rows_of, index, prob, held, backs, slots, n_ex):
    n_dp, n_parts = len(backs), len(backs[0])
    _, rows, ff = held.shape
    flat = [part for parts in backs for part in parts]
    vmem = pl.BlockSpec(memory_space=pltpu.VMEM)
    return pl.pallas_call(
        functools.partial(spread_kernel, n_parts, n_dp),
        in_specs=[pl.BlockSpec(memory_space=pltpu.SMEM)] + [vmem] * (3 + len(flat)),
        out_specs=[vmem] * 3,
        out_shape=[
            jax.ShapeDtypeStruct((slots, ff), jnp.bfloat16),
            jax.ShapeDtypeStruct((slots, ff), jnp.bfloat16),
            jax.ShapeDtypeStruct((n_ex, 2 * rows // n_ex), jnp.float32),
        ],
        compiler_params=pltpu.CompilerParams(vmem_limit_bytes=VMEM_BYTES),
        cost_estimate=pl.CostEstimate(
            flops=4 * rows * slots * ff,
            bytes_accessed=4 * (2 + n_dp) * rows * ff,
            transcendentals=0,
        ),
        name="spread_product",
    )(rows_of, index, prob, held, *flat)


def weight_kernel(n_refs, n_dp, layout, *refs):
    blocks, scaleds = refs[:n_refs], refs[n_refs : n_refs + n_dp]
    own, other, turned = refs[n_refs + n_dp :]

    @pl.when(pl.program_id(0) == 0)
    def _():
        for d in range(n_dp):
            for x in range(2):
                turned[d, x] = scaleds[d][x].T

    rows = [gathered(blocks, layout, d) for d in range(n_dp)]
    for x, out in enumerate((own, other)):
        total = dot(turned[0, x], rows[0], 1, 0)
        for d in range(1, n_dp):
            total = total + dot(turned[d, x], rows[d], 1, 0)
        out[...] = total.astype(out.dtype)


def weight_product(blocks, layout, scaleds):
    n_dp = len(scaleds)
    _, tok, width = blocks[0].shape
    _, rows, ff = scaleds[0].shape
    tile = 512 if width >= 2048 else 256
    return pl.pallas_call(
        functools.partial(weight_kernel, len(blocks), n_dp, layout),
        grid=(width // tile,),
        in_specs=[pl.BlockSpec(block.shape[:2] + (tile,), lambda i: (0, 0, i)) for block in blocks]
        + [
            pl.BlockSpec((2, rows, ff), lambda i: (0, 0, 0), pipeline_mode=pl.Buffered(1))
            for _ in scaleds
        ],
        out_specs=[pl.BlockSpec((ff, tile), lambda i: (0, i))] * 2,
        out_shape=[
            jax.ShapeDtypeStruct((ff, width), jnp.float32),
            jax.ShapeDtypeStruct((ff, width), jnp.bfloat16),
        ],
        scratch_shapes=[pltpu.VMEM((n_dp, 2, ff, rows), jnp.bfloat16)],
        compiler_params=pltpu.CompilerParams(vmem_limit_bytes=VMEM_BYTES),
        cost_estimate=pl.CostEstimate(
            flops=4 * n_dp * rows * width * ff,
            bytes_accessed=2 * n_dp * rows * (width + 2 * ff) + 6 * ff * width,
            transcendentals=0,
        ),
        name="weight_product",
    )(*blocks, *scaleds)


def body(ring):
    chips = len(ring)
    half = chips // 2
    offsets = [0]
    for step in range(1, half):
        offsets += [-step, step]
    offsets.append(half)
    place_of = {chip: at for at, chip in enumerate(ring)}
    row_table = np.asarray(
        [
            [2 * ring[(place_of[e // 2] + off) % chips] + (e % 2 ^ x) for x in range(2) for off in offsets]
            for e in range(2 * chips)
        ],
        np.int32,
    )

    def along(step):
        return [
            (2 * ring[at] + core, 2 * ring[(at + step) % chips] + core)
            for at in range(chips)
            for core in range(2)
        ]

    forward, backward = along(1), along(-1)
    sibling = [(e, e ^ 1) for e in range(2 * chips)]
    same_core = [[2 * chip + c for chip in range(chips)] for c in range(2)]

    def shards(expert_ids, route_probs, expert_hidden, down_weight, out_grad):
        tok, top = expert_ids.shape
        n_dp = lax.axis_size("dp")
        n_ex = lax.axis_size("expert")
        cap = expert_hidden.shape[3]
        slots = cap * n_ex
        ff = down_weight.shape[1]
        width = down_weight.shape[2]
        weight = down_weight[0]
        replica = lax.axis_index("dp")
        expert = lax.axis_index("expert")
        per = n_dp // 2
        groups = [list(range(per)), list(range(per, n_dp))]
        rows_of = lax.dynamic_index_in_dim(jnp.asarray(row_table), expert, 0, keepdims=False)

        def shift(value, step):
            return lax.ppermute(value, "dp", [(i, (i + step) % n_dp) for i in range(n_dp)])

        def ring_send(value, step):
            return lax.ppermute(value, "expert", forward if step > 0 else backward)

        def swap(value):
            return lax.ppermute(value, "expert", sibling)

        def width_shard(d):
            at = ((replica + d) % n_dp) * width
            return lax.dynamic_slice_in_dim(out_grad, at, width, axis=1)

        blocks = {0: jnp.stack([width_shard(0)] + [shift(width_shard(d), d) for d in range(1, n_dp)])}
        for step in range(1, half):
            blocks[-step] = ring_send(blocks[1 - step], 1)
            blocks[step] = ring_send(blocks[step - 1], -1)
        last = [ring_send(blocks[1 - half][:per], 1), ring_send(blocks[half - 1][per:], -1)]

        cut = max(1, chips - 3)
        early = [blocks[off] for off in offsets[:cut]]
        late = [blocks[off] for off in offsets[cut:-1]]
        early_layout = [[(i, d) for d in range(n_dp)] for i in range(len(early))]
        late_layout = [[(i, d) for d in range(n_dp)] for i in range(len(late))]
        halves = lambda base: [(base + d // per, d % per) for d in range(n_dp)]
        full_layout = early_layout + [[(len(early) + i, d) for d in range(n_dp)] for i in range(len(late))]
        full_layout = full_layout + [halves(len(early) + len(late))]
        late_layout = late_layout + [halves(len(late))]

        sibling_weight = swap(weight)
        hidden = expert_hidden[0, 0].transpose(1, 0, 2).reshape(slots, ff)
        names = expert_ids.T[None] == jnp.arange(n_ex, dtype=jnp.int32)[:, None, None]
        table = jnp.sum(jnp.where(names, route_probs.T[None], 0.0), axis=1)
        table = lax.all_to_all(
            table.reshape(chips, 2 * tok), "expert", 0, 0, tiled=True, axis_index_groups=same_core
        ).reshape(n_ex, tok)
        tables = [table] + [shift(table, d) for d in range(1, n_dp)]
        hiddens = [hidden] + [shift(hidden, d) for d in range(1, n_dp)]
        hiddens = [(value, swap(value)) for value in hiddens]

        parts, scaleds = [], []
        for d in range(n_dp):
            made = forward_product(d == 0, rows_of, tables[d], *hiddens[d], weight, sibling_weight)
            parts.append(made[0])
            scaleds.append(made[1])
            if d == 0:
                held, index, prob = made[2:]
        layer_out = jnp.zeros((tok, n_dp * width), jnp.bfloat16)
        for g, group in enumerate(groups):

            def term(off):
                at = offsets.index(off)
                return jnp.stack([parts[d][at] for d in group])

            total = term(0).astype(jnp.float32)
            for direction in (1, -1):
                first = half if (direction == 1) == (g == 0) else half - 1
                carry = None
                for hop in range(first, 0, -1):
                    value = term(half if hop == half else hop * direction)
                    if carry is not None:
                        value = (value.astype(jnp.float32) + carry.astype(jnp.float32)).astype(jnp.bfloat16)
                    carry = ring_send(value, direction)
                total = total + carry.astype(jnp.float32)
            total = total.astype(jnp.bfloat16)
            for i, d in enumerate(group):
                piece = total[i] if d == 0 else shift(total[i], -d)
                layer_out = lax.dynamic_update_slice_in_dim(
                    layer_out, piece, ((replica + d) % n_dp) * width, axis=1
                )

        back_early = back_product(early, early_layout, weight, sibling_weight)
        back_late = back_product(late + last, late_layout, weight, sibling_weight)
        backs = [[back_early[0], back_late[0]]]
        for d in range(1, n_dp):
            backs.append([shift(back_early[d], -d), shift(back_late[d], -d)])
        spread, spread_other, inner = spread_product(rows_of, index, prob, held, backs, slots, n_ex)
        hidden_grad = spread + swap(spread_other)
        hidden_grad = hidden_grad.reshape(cap, n_ex, ff).transpose(1, 0, 2)[None, None]

        own, other = weight_product(early + late + last, full_layout, scaleds)
        weight_grad = own + swap(other).astype(jnp.float32)

        inner = lax.all_to_all(
            inner.reshape(chips, 2 * tok), "expert", 0, 0, tiled=True, axis_index_groups=same_core
        ).reshape(n_ex, tok)
        mine = expert_ids[:, :, None] == jnp.arange(n_ex, dtype=jnp.int32)
        prob_grad = jnp.sum(jnp.where(mine, inner.T[:, None, :], 0.0), axis=2)
        return (layer_out, prob_grad, hidden_grad, weight_grad[None])

    return shards


def solution(mesh):
    placed = (
        P(("dp", "expert"), None),
        P(("dp", "expert"), None),
        P("dp", "expert", None, None, None),
        P("expert", None, "dp"),
        P(("dp", "expert"), None),
    )
    return jax.shard_map(
        body(chip_ring(mesh)),
        mesh=mesh,
        in_specs=placed,
        out_specs=(
            P(("dp", "expert"), None),
            P(("dp", "expert"), None),
            P("dp", "expert", None, None, None),
            P("expert", None, "dp"),
        ),
        check_vma=False,
    )
```

```python
import functools

import jax
import jax.numpy as jnp
import numpy as np
from jax import lax
from jax.experimental import pallas as pl
from jax.experimental.pallas import tpu as pltpu
from jax.sharding import PartitionSpec as P

VMEM_BYTES = 48 * 1024 * 1024


def dot(a, b, ca, cb):
    return lax.dot_general(a, b, (((ca,), (cb,)), ((), ())), preferred_element_type=jnp.float32)


def after(value, *done):
    return lax.optimization_barrier((value, *done))[0]


def chip_ring(mesh):
    chips = mesh.shape["expert"] // 2
    devices = mesh.devices.reshape(mesh.shape["dp"], -1)
    if not hasattr(devices[0, 0], "coords"):
        return list(range(chips))
    at = [tuple(devices[0, 2 * chip].coords)[1:] for chip in range(chips)]
    rows = max(z for _, z in at) + 1
    cols = max(y for y, _ in at) + 1
    if rows * cols != chips or rows % 2:
        return list(range(chips))
    walk = [(0, z) for z in range(rows)]
    for step, z in enumerate(reversed(range(rows))):
        span = range(1, cols)
        walk += [(y, z) for y in (span if step % 2 == 0 else reversed(span))]
    return [at.index(place) for place in walk]


def forward_kernel(keep, rows_of, table, hid_own, hid_sib, w_own, w_sib, *refs):
    part, scaled = refs[:2]
    held, index, prob = refs[2:5] if keep else (None, None, None)
    picked, facts = refs[-2:]
    n_ex, tok = table.shape
    chips = n_ex // 2
    slots = hid_own.shape[0]
    rows = chips * tok

    @pl.when(pl.program_id(0) == 0)
    def _():
        for j in range(n_ex):
            facts[j : j + 1, :] = table[pl.ds(rows_of[j], 1), :]
        weights = facts[...]
        taken = (weights > 0.0).astype(jnp.float32)
        row = lax.broadcasted_iota(jnp.int32, (tok, tok), 0)
        col = lax.broadcasted_iota(jnp.int32, (tok, tok), 1)
        position = dot((col < row).astype(jnp.float32), taken, 1, 1).astype(jnp.int32)
        column = lax.dot_general(
            (col == row).astype(jnp.float32),
            weights,
            (((1,), (1,)), ((), ())),
            precision=lax.Precision.HIGHEST,
            preferred_element_type=jnp.float32,
        )
        lane = lax.broadcasted_iota(jnp.int32, (tok, slots), 1)
        for x, hid in enumerate((hid_own, hid_sib)):
            columns = []
            for o in range(chips):
                j = x * chips + o
                here = column[:, j : j + 1]
                slot = jnp.where(here > 0.0, position[:, j : j + 1] * n_ex + rows_of[o], -1)
                picked[x, o * tok : (o + 1) * tok, :] = (lane == slot).astype(jnp.bfloat16)
                columns.append(here)
                if keep:
                    index[o * tok : (o + 1) * tok, x : x + 1] = slot
                    prob[o * tok : (o + 1) * tok, x : x + 1] = here
            found = dot(picked[x], hid[...], 1, 0)
            if keep:
                held[x] = found.astype(jnp.bfloat16)
            scaled[x] = (found * jnp.concatenate(columns, axis=0)).astype(jnp.bfloat16)

    value = dot(scaled[0], w_own[...], 1, 0) + dot(scaled[1], w_sib[...], 1, 0)
    part[...] = value.astype(jnp.bfloat16).reshape(part.shape)


def forward_product(keep, rows_of, table, hid_own, hid_sib, w_own, w_sib):
    n_ex, tok = table.shape
    chips = n_ex // 2
    rows = chips * tok
    slots, ff = hid_own.shape
    width = w_own.shape[1]
    tile = 512
    whole = lambda shape: pl.BlockSpec(shape, lambda i: (0,) * len(shape))
    out_specs = [pl.BlockSpec((chips, tok, tile), lambda i: (0, 0, i)), whole((2, rows, ff))]
    out_shape = [
        jax.ShapeDtypeStruct((chips, tok, width), jnp.bfloat16),
        jax.ShapeDtypeStruct((2, rows, ff), jnp.bfloat16),
    ]
    if keep:
        out_specs += [whole((2, rows, ff)), whole((rows, 2)), whole((rows, 2))]
        out_shape += [
            jax.ShapeDtypeStruct((2, rows, ff), jnp.bfloat16),
            jax.ShapeDtypeStruct((rows, 2), jnp.int32),
            jax.ShapeDtypeStruct((rows, 2), jnp.float32),
        ]
    return pl.pallas_call(
        functools.partial(forward_kernel, keep),
        grid=(width // tile,),
        in_specs=[pl.BlockSpec(memory_space=pltpu.SMEM), whole((n_ex, tok))]
        + [whole((slots, ff))] * 2
        + [pl.BlockSpec((ff, tile), lambda i: (0, i))] * 2,
        out_specs=out_specs,
        out_shape=out_shape,
        scratch_shapes=[
            pltpu.VMEM((2, rows, slots), jnp.bfloat16),
            pltpu.VMEM((n_ex, tok), jnp.float32),
        ],
        compiler_params=pltpu.CompilerParams(vmem_limit_bytes=VMEM_BYTES),
        cost_estimate=pl.CostEstimate(
            flops=4 * rows * ff * (width + slots),
            bytes_accessed=4 * ff * (width + slots) + 2 * rows * (width + 2 * ff),
            transcendentals=0,
        ),
        name="forward_product",
    )(rows_of, table, hid_own, hid_sib, w_own, w_sib)


def gathered(refs, layout, d):
    return jnp.concatenate([refs[where][at] for where, at in (row[d] for row in layout)], axis=0)


def back_kernel(n_refs, layout, *refs):
    blocks, (w_own, w_sib), outs = refs[:n_refs], refs[n_refs : n_refs + 2], refs[n_refs + 2 :]
    rows = jnp.concatenate([gathered(blocks, layout, d) for d in range(len(outs))], axis=0)
    count = outs[0].shape[1]
    for x, w_ref in enumerate((w_own, w_sib)):
        value = dot(rows, w_ref[...], 1, 1).astype(jnp.bfloat16)
        for d, out in enumerate(outs):
            out[x] = value[d * count : (d + 1) * count]


def back_product(blocks, layout, w_own, w_sib):
    n_dp = len(layout[0])
    _, tok, width = blocks[0].shape
    ff = w_own.shape[0]
    rows = len(layout) * tok
    tile = 256
    return pl.pallas_call(
        functools.partial(back_kernel, len(blocks), layout),
        grid=(ff // tile,),
        in_specs=[
            pl.BlockSpec(block.shape, lambda i: (0, 0, 0), pipeline_mode=pl.Buffered(1))
            for block in blocks
        ]
        + [pl.BlockSpec((tile, width), lambda i: (i, 0))] * 2,
        out_specs=[pl.BlockSpec((2, rows, tile), lambda i: (0, 0, i))] * n_dp,
        out_shape=[jax.ShapeDtypeStruct((2, rows, ff), jnp.bfloat16)] * n_dp,
        compiler_params=pltpu.CompilerParams(vmem_limit_bytes=VMEM_BYTES),
        cost_estimate=pl.CostEstimate(
            flops=4 * n_dp * rows * width * ff,
            bytes_accessed=2 * (n_dp * rows * (width + 2 * ff) + 2 * ff * width),
            transcendentals=0,
        ),
        name="back_product",
    )(*blocks, w_own, w_sib)


def spread_kernel(n_parts, n_dp, *refs):
    rows_of, index, prob, held = refs[:4]
    backs = refs[4 : 4 + n_parts * n_dp]
    own, other, inner = refs[4 + n_parts * n_dp :]
    n_ex, tok = inner.shape
    chips = n_ex // 2
    rows, slots = index.shape[0], own.shape[0]
    ones = jnp.ones((8, held.shape[2]), jnp.float32)
    lane = lax.broadcasted_iota(jnp.int32, (rows, slots), 1)
    for x, out in enumerate((own, other)):
        back = None
        for d in range(n_dp):
            pieces = [backs[d * n_parts + i][x] for i in range(n_parts)]
            value = jnp.concatenate(pieces, axis=0).astype(jnp.float32)
            back = value if back is None else back + value
        product = back * held[x].astype(jnp.float32)
        sums = lax.dot_general(
            ones,
            product,
            (((1,), (1,)), ((), ())),
            precision=lax.Precision.HIGHEST,
            preferred_element_type=jnp.float32,
        )
        for o in range(chips):
            inner[pl.ds(rows_of[x * chips + o], 1), :] = sums[:1, o * tok : (o + 1) * tok]
        pick = (lane == index[:, x : x + 1]).astype(jnp.bfloat16)
        mine = (back * prob[:, x : x + 1]).astype(jnp.bfloat16)
        out[...] = dot(pick, mine, 0, 0).astype(jnp.bfloat16)


def spread_product(rows_of, index, prob, held, backs, slots, n_ex):
    n_dp, n_parts = len(backs), len(backs[0])
    _, rows, ff = held.shape
    flat = [part for parts in backs for part in parts]
    vmem = pl.BlockSpec(memory_space=pltpu.VMEM)
    return pl.pallas_call(
        functools.partial(spread_kernel, n_parts, n_dp),
        in_specs=[pl.BlockSpec(memory_space=pltpu.SMEM)] + [vmem] * (3 + len(flat)),
        out_specs=[vmem] * 3,
        out_shape=[
            jax.ShapeDtypeStruct((slots, ff), jnp.bfloat16),
            jax.ShapeDtypeStruct((slots, ff), jnp.bfloat16),
            jax.ShapeDtypeStruct((n_ex, 2 * rows // n_ex), jnp.float32),
        ],
        compiler_params=pltpu.CompilerParams(vmem_limit_bytes=VMEM_BYTES),
        cost_estimate=pl.CostEstimate(
            flops=4 * rows * slots * ff,
            bytes_accessed=4 * (2 + n_dp) * rows * ff,
            transcendentals=0,
        ),
        name="spread_product",
    )(rows_of, index, prob, held, *flat)


def weight_kernel(n_refs, n_dp, layout, *refs):
    blocks, scaleds, more = refs[:n_refs], refs[n_refs : n_refs + n_dp], refs[n_refs + n_dp : -2]
    out, turned = refs[-2:]
    count = scaleds[0].shape[1]

    @pl.when(pl.program_id(0) == 0)
    def _():
        for d in range(n_dp):
            turned[:, d * count : (d + 1) * count] = scaleds[d][0].T

    rows = jnp.concatenate([gathered(blocks, layout, d) for d in range(n_dp)], axis=0)
    total = dot(turned[...], rows, 1, 0)
    for ref in more:
        total = total + ref[...].astype(jnp.float32)
    out[...] = total.astype(out.dtype)


def weight_product(blocks, layout, scaleds, x, dtype, *more):
    n_dp = len(scaleds)
    _, tok, width = blocks[0].shape
    _, rows, ff = scaleds[0].shape
    tile = 512 if width >= 2048 else 256
    return pl.pallas_call(
        functools.partial(weight_kernel, len(blocks), n_dp, layout),
        grid=(width // tile,),
        in_specs=[pl.BlockSpec(block.shape[:2] + (tile,), lambda i: (0, 0, i)) for block in blocks]
        + [
            pl.BlockSpec((1, rows, ff), lambda i: (x, 0, 0), pipeline_mode=pl.Buffered(1))
            for _ in scaleds
        ]
        + [pl.BlockSpec((ff, tile), lambda i: (0, i)) for _ in more],
        out_specs=pl.BlockSpec((ff, tile), lambda i: (0, i)),
        out_shape=jax.ShapeDtypeStruct((ff, width), dtype),
        scratch_shapes=[pltpu.VMEM((ff, n_dp * rows), jnp.bfloat16)],
        compiler_params=pltpu.CompilerParams(vmem_limit_bytes=VMEM_BYTES),
        cost_estimate=pl.CostEstimate(
            flops=2 * n_dp * rows * width * ff,
            bytes_accessed=2 * n_dp * rows * (width + ff) + 4 * ff * width,
            transcendentals=0,
        ),
        name="weight_product",
    )(*blocks, *scaleds, *more)


def body(ring):
    chips = len(ring)
    half = chips // 2
    offsets = [0]
    for step in range(1, half):
        offsets += [-step, step]
    offsets.append(half)
    place_of = {chip: at for at, chip in enumerate(ring)}
    row_table = np.asarray(
        [
            [2 * ring[(place_of[e // 2] + off) % chips] + (e % 2 ^ x) for x in range(2) for off in offsets]
            for e in range(2 * chips)
        ],
        np.int32,
    )

    def along(step):
        return [
            (2 * ring[at] + core, 2 * ring[(at + step) % chips] + core)
            for at in range(chips)
            for core in range(2)
        ]

    forward, backward = along(1), along(-1)
    sibling = [(e, e ^ 1) for e in range(2 * chips)]
    same_core = [[2 * chip + c for chip in range(chips)] for c in range(2)]

    def shards(expert_ids, route_probs, expert_hidden, down_weight, out_grad):
        tok, top = expert_ids.shape
        n_dp = lax.axis_size("dp")
        n_ex = lax.axis_size("expert")
        cap = expert_hidden.shape[3]
        slots = cap * n_ex
        ff = down_weight.shape[1]
        width = down_weight.shape[2]
        weight = down_weight[0]
        replica = lax.axis_index("dp")
        expert = lax.axis_index("expert")
        per = n_dp // 2
        groups = [list(range(per)), list(range(per, n_dp))]
        rows_of = lax.dynamic_index_in_dim(jnp.asarray(row_table), expert, 0, keepdims=False)

        def shift(value, step):
            return lax.ppermute(value, "dp", [(i, (i + step) % n_dp) for i in range(n_dp)])

        def ring_send(value, step):
            return lax.ppermute(value, "expert", forward if step > 0 else backward)

        def swap(value):
            return lax.ppermute(value, "expert", sibling)

        def width_shard(d):
            at = ((replica + d) % n_dp) * width
            return lax.dynamic_slice_in_dim(out_grad, at, width, axis=1)

        blocks = {0: jnp.stack([width_shard(0)] + [shift(width_shard(d), d) for d in range(1, n_dp)])}

        sibling_weight = swap(weight)
        hidden = expert_hidden[0, 0].transpose(1, 0, 2).reshape(slots, ff)
        names = expert_ids.T[None] == jnp.arange(n_ex, dtype=jnp.int32)[:, None, None]
        table = jnp.sum(jnp.where(names, route_probs.T[None], 0.0), axis=1)
        table = lax.all_to_all(
            table.reshape(chips, 2 * tok), "expert", 0, 0, tiled=True, axis_index_groups=same_core
        ).reshape(n_ex, tok)
        tables = [table] + [shift(table, d) for d in range(1, n_dp)]
        hiddens = [hidden] + [shift(hidden, d) for d in range(1, n_dp)]

        parts, scaleds, gate = [], [], (table,)
        for step in range(1, half):
            sent = blocks[1 - step], blocks[step - 1]
            if step > 1:
                sent = after(sent[0], *gate), after(sent[1], *gate)
            blocks[-step] = ring_send(sent[0], 1)
            blocks[step] = ring_send(sent[1], -1)
            arrived = blocks[-step], blocks[step]
            for d in [step - 1] if step < half - 1 else range(step - 1, n_dp):
                if d < n_dp:
                    ours = after(hiddens[d], *parts[-1:])
                    made = forward_product(
                        d == 0, rows_of, after(tables[d], *arrived), ours, swap(ours), weight, sibling_weight
                    )
                    parts.append(made[0])
                    scaleds.append(made[1])
                    gate = (made[0],)
                    if d == 0:
                        held, index, prob = made[2:]
        sent = after(blocks[1 - half][:per], *gate), after(blocks[half - 1][per:], *gate)
        last = [ring_send(sent[0], 1), ring_send(sent[1], -1)]

        cut = max(1, chips - 3)
        early = [blocks[off] for off in offsets[:cut]]
        late = [blocks[off] for off in offsets[cut:-1]]
        early_layout = [[(i, d) for d in range(n_dp)] for i in range(len(early))]
        late_layout = [[(i, d) for d in range(n_dp)] for i in range(len(late))]
        halves = lambda base: [(base + d // per, d % per) for d in range(n_dp)]
        full_layout = early_layout + [[(len(early) + i, d) for d in range(n_dp)] for i in range(len(late))]
        full_layout = full_layout + [halves(len(early) + len(late))]
        late_layout = late_layout + [halves(len(late))]

        def term(off, g):
            at = offsets.index(off)
            return jnp.stack([parts[d][at] for d in groups[g]])

        carry = {}

        def hop_on(hop, g, done):
            for direction in (1, -1):
                if hop == half and (direction == 1) != (g == 0):
                    continue
                value = term(half if hop == half else hop * direction, g)
                if (g, direction) in carry:
                    value = value.astype(jnp.float32) + carry[g, direction].astype(jnp.float32)
                    value = value.astype(jnp.bfloat16)
                carry[g, direction] = ring_send(after(value, *done), direction)

        def carried():
            return tuple(carry.values())

        hop_on(half, 0, ())
        hop_on(half, 1, ())
        hop_on(half - 1, 0, ())
        back_early = back_product([after(early[0], *parts)] + early[1:], early_layout, weight, sibling_weight)
        held_up = carried()
        hop_on(half - 1, 1, (back_early[0],))
        for hop in range(half - 2, 1, -1):
            hop_on(hop, 0, (back_early[0],))
            if hop > 2:
                hop_on(hop, 1, ())
        back_late = back_product(
            [after((late + last)[0], *held_up)] + (late + last)[1:], late_layout, weight, sibling_weight
        )
        other = weight_product(
            [after(early[0], *carried(), back_late[0])] + early[1:] + late + last,
            full_layout,
            scaleds,
            1,
            jnp.bfloat16,
        )
        hop_on(1, 0, (back_late[0],))
        hop_on(min(2, half - 2), 1, (back_late[0],))
        backs = [[back_early[0], back_late[0]]]
        for d in range(1, n_dp):
            backs.append([shift(back_early[d], -d), shift(back_late[d], -d)])
        spread, spread_other, inner = spread_product(
            rows_of, index, after(prob, other), held, backs, slots, n_ex
        )
        hop_on(1, 1, (other,))

        weight_grad = weight_product(
            [after(early[0], spread)] + early[1:] + late + last,
            full_layout,
            scaleds,
            0,
            jnp.float32,
            swap(other),
        )
        hidden_grad = spread + swap(spread_other)
        hidden_grad = hidden_grad.reshape(cap, n_ex, ff).transpose(1, 0, 2)[None, None]

        layer_out = jnp.zeros((tok, n_dp * width), jnp.bfloat16)
        for g in (1, 0):
            total = term(0, g).astype(jnp.float32)
            total = total + carry[g, 1].astype(jnp.float32) + carry[g, -1].astype(jnp.float32)
            total = total.astype(jnp.bfloat16)
            for i, d in enumerate(groups[g]):
                piece = total[i] if d == 0 else shift(total[i], -d)
                layer_out = lax.dynamic_update_slice_in_dim(
                    layer_out, piece, ((replica + d) % n_dp) * width, axis=1
                )

        inner = lax.all_to_all(
            inner.reshape(chips, 2 * tok), "expert", 0, 0, tiled=True, axis_index_groups=same_core
        ).reshape(n_ex, tok)
        mine = expert_ids[:, :, None] == jnp.arange(n_ex, dtype=jnp.int32)
        prob_grad = jnp.sum(jnp.where(mine, inner.T[:, None, :], 0.0), axis=2)
        return (layer_out, prob_grad, hidden_grad, weight_grad[None])

    return shards


def solution(mesh):
    placed = (
        P(("dp", "expert"), None),
        P(("dp", "expert"), None),
        P("dp", "expert", None, None, None),
        P("expert", None, "dp"),
        P(("dp", "expert"), None),
    )
    return jax.shard_map(
        body(chip_ring(mesh)),
        mesh=mesh,
        in_specs=placed,
        out_specs=(
            P(("dp", "expert"), None),
            P(("dp", "expert"), None),
            P("dp", "expert", None, None, None),
            P("expert", None, "dp"),
        ),
        check_vma=False,
    )
```

```python
import functools

import jax
import jax.numpy as jnp
import numpy as np
from jax import lax
from jax.experimental import pallas as pl
from jax.experimental.pallas import tpu as pltpu
from jax.sharding import PartitionSpec as P

VMEM_BYTES = 48 * 1024 * 1024


def dot(a, b, ca, cb):
    return lax.dot_general(a, b, (((ca,), (cb,)), ((), ())), preferred_element_type=jnp.float32)


def after(value, *done):
    return lax.optimization_barrier((value, *done))[0]


def chip_ring(mesh):
    chips = mesh.shape["expert"] // 2
    devices = mesh.devices.reshape(mesh.shape["dp"], -1)
    if not hasattr(devices[0, 0], "coords"):
        return list(range(chips))
    at = [tuple(devices[0, 2 * chip].coords)[1:] for chip in range(chips)]
    rows = max(z for _, z in at) + 1
    cols = max(y for y, _ in at) + 1
    if rows * cols != chips or rows % 2:
        return list(range(chips))
    walk = [(0, z) for z in range(rows)]
    for step, z in enumerate(reversed(range(rows))):
        span = range(1, cols)
        walk += [(y, z) for y in (span if step % 2 == 0 else reversed(span))]
    return [at.index(place) for place in walk]


def block_kernel(plan, refs_in, n_dp, n_ex, top, *refs):
    meta = refs[0]
    blocks = refs[1 : 1 + refs_in]
    at = 1 + refs_in
    replicas = sorted({item[2] for item in plan})
    hid = {d: refs[at + 2 * i : at + 2 * i + 2] for i, d in enumerate(replicas)}
    at += 2 * len(replicas)
    weights = refs[at : at + 2]
    at += 2
    parts = refs[at : at + len(plan)]
    at += len(plan)
    outs = {d: refs[at + 2 * i : at + 2 * i + 2] for i, d in enumerate(replicas)}
    at += 2 * len(replicas)
    index, prob = refs[at : at + 2] if 0 in replicas else (None, None)

    _, tok, full = blocks[0].shape
    ff, width = weights[0].shape
    slots = hid[replicas[0]][0].shape[0]
    count = len(plan) * tok
    rows = [blocks[where][place] for where, place, _, _ in plan]
    routes = jnp.concatenate([row[:, width:] for row in rows], axis=0).astype(jnp.float32)
    named = routes[:, :top]
    chance = routes[:, top : 2 * top] + routes[:, 2 * top : 3 * top] + routes[:, 3 * top : 4 * top]
    row = lax.broadcasted_iota(jnp.int32, (tok, tok), 0)
    col = lax.broadcasted_iota(jnp.int32, (tok, tok), 1)
    earlier = (col < row).astype(jnp.float32)
    lane = lax.broadcasted_iota(jnp.int32, (tok, slots), 1)
    spans = {d: [i for i, item in enumerate(plan) if item[2] == d] for d in replicas}
    helds, scaleds = [], []
    for x in range(2):
        mine = named == meta[x].astype(jnp.float32)
        here = jnp.sum(jnp.where(mine, chance, 0.0), axis=1, keepdims=True)
        taken = jnp.broadcast_to((here > 0.0).astype(jnp.float32), (count, 128))
        held = []
        for d in replicas:
            picks = []
            for n, i in enumerate(spans[d]):
                span = slice(i * tok, (i + 1) * tok)
                position = dot(earlier, taken[span], 1, 0)[:, :1].astype(jnp.int32)
                slot = jnp.where(here[span] > 0.0, position * n_ex + meta[2 + plan[i][3]], -1)
                picks.append((lane == slot).astype(jnp.bfloat16))
                if d == 0:
                    index[n * tok : (n + 1) * tok, x : x + 1] = slot
                    prob[n * tok : (n + 1) * tok, x : x + 1] = here[span]
            held.append(dot(jnp.concatenate(picks, axis=0), hid[d][x][...], 1, 0))
        held = jnp.concatenate(held, axis=0)
        scaled = (held * here).astype(jnp.bfloat16)
        base = 0
        for d in replicas:
            size = len(spans[d]) * tok
            outs[d][0][x] = scaled[base : base + size]
            base += size
        helds.append(held)
        scaleds.append(scaled)

    tile = 512
    for step in range(width // tile):
        cols = slice(step * tile, (step + 1) * tile)
        value = dot(scaleds[0], weights[0][:, cols], 1, 0) + dot(scaleds[1], weights[1][:, cols], 1, 0)
        value = value.astype(jnp.bfloat16)
        for i, out in enumerate(parts):
            out[:, cols] = value[i * tok : (i + 1) * tok]

    lhs = jnp.concatenate([row[:, :width] for row in rows], axis=0)
    lane = lax.broadcasted_iota(jnp.int32, (count, full - width), 1)
    extra = jnp.zeros((count, full - width), jnp.float32)
    for x in range(2):
        inner = jnp.zeros((count, 1), jnp.float32)
        step_ff = 256
        for step in range(ff // step_ff):
            cols = slice(step * step_ff, (step + 1) * step_ff)
            value = dot(lhs, weights[x][cols, :], 1, 1)
            inner = inner + jnp.sum(value * helds[x][:, cols], axis=1, keepdims=True)
            value = value.astype(jnp.bfloat16)
            base = 0
            for d in replicas:
                size = len(spans[d]) * tok
                outs[d][1][x, :, cols] = value[base : base + size]
                base += size
        high = inner.astype(jnp.bfloat16).astype(jnp.float32)
        extra = jnp.where(lane == meta[x], high, extra)
        extra = jnp.where(lane == meta[x] + n_ex, inner - high, extra)
    extra = extra.astype(jnp.bfloat16)
    for i, out in enumerate(parts):
        out[:, width:] = extra[i * tok : (i + 1) * tok]


def block_product(plan, meta, blocks, hiddens, w_own, w_sib, n_ex, top):
    n_dp = len(hiddens)
    _, tok, full = blocks[0].shape
    ff, width = w_own.shape
    slots = hiddens[0][0].shape[0]
    replicas = sorted({item[2] for item in plan})
    vmem = pl.BlockSpec(memory_space=pltpu.VMEM)
    bf16 = lambda *shape: jax.ShapeDtypeStruct(shape, jnp.bfloat16)
    out_shape = [bf16(tok, full) for _ in plan]
    sizes = {d: tok * sum(item[2] == d for item in plan) for d in replicas}
    for d in replicas:
        out_shape += [bf16(2, sizes[d], ff)] * 2
    if 0 in replicas:
        out_shape.append(jax.ShapeDtypeStruct((sizes[0], 2), jnp.int32))
        out_shape.append(jax.ShapeDtypeStruct((sizes[0], 2), jnp.float32))
    hid = [value for d in replicas for value in hiddens[d]]
    count = len(plan) * tok
    made = pl.pallas_call(
        functools.partial(block_kernel, plan, len(blocks), n_dp, n_ex, top),
        in_specs=[pl.BlockSpec(memory_space=pltpu.SMEM)] + [vmem] * (len(blocks) + len(hid) + 2),
        out_specs=[vmem] * len(out_shape),
        out_shape=out_shape,
        compiler_params=pltpu.CompilerParams(vmem_limit_bytes=VMEM_BYTES),
        cost_estimate=pl.CostEstimate(
            flops=8 * count * ff * width,
            bytes_accessed=4 * ff * width + 4 * count * (full + ff),
            transcendentals=0,
        ),
        name="block_product",
    )(meta, *blocks, *hid, w_own, w_sib)
    parts = made[: len(plan)]
    rest = made[len(plan) :]
    scaled = {d: rest[2 * i] for i, d in enumerate(replicas)}
    back = {d: rest[2 * i + 1] for i, d in enumerate(replicas)}
    return parts, scaled, back, rest[2 * len(replicas) :]


def spread_kernel(sizes, *refs):
    n_parts = len(sizes[0])
    index, prob = refs[:n_parts], refs[n_parts : 2 * n_parts]
    backs = list(refs[2 * n_parts : -2])
    outs = refs[-2:]
    slots = outs[0].shape[0]
    slot = jnp.concatenate([ref[...] for ref in index], axis=0)
    weight = jnp.concatenate([ref[...] for ref in prob], axis=0)
    lane = lax.broadcasted_iota(jnp.int32, (slot.shape[0], slots), 1)
    for x, out in enumerate(outs):
        back, at = None, 0
        for pieces in sizes:
            value = jnp.concatenate([ref[x] for ref in backs[at : at + len(pieces)]], axis=0)
            at += len(pieces)
            value = value.astype(jnp.float32)
            back = value if back is None else back + value
        pick = (lane == slot[:, x : x + 1]).astype(jnp.bfloat16)
        mine = (back * weight[:, x : x + 1]).astype(jnp.bfloat16)
        out[...] = dot(pick, mine, 0, 0).astype(jnp.bfloat16)


def spread_product(index, prob, backs, slots):
    sizes = [[part.shape[1] for part in parts] for parts in backs]
    ff = backs[0][0].shape[2]
    rows = sum(sizes[0])
    flat = [part for parts in backs for part in parts]
    vmem = pl.BlockSpec(memory_space=pltpu.VMEM)
    return pl.pallas_call(
        functools.partial(spread_kernel, sizes),
        in_specs=[vmem] * (2 * len(index) + len(flat)),
        out_specs=[vmem] * 2,
        out_shape=[jax.ShapeDtypeStruct((slots, ff), jnp.bfloat16)] * 2,
        compiler_params=pltpu.CompilerParams(vmem_limit_bytes=VMEM_BYTES),
        cost_estimate=pl.CostEstimate(
            flops=4 * rows * slots * ff,
            bytes_accessed=4 * (1 + len(backs)) * rows * ff,
            transcendentals=0,
        ),
        name="spread_product",
    )(*index, *prob, *flat)


def weight_kernel(n_refs, n_scaled, layout, *refs):
    blocks, scaleds, more = refs[:n_refs], refs[n_refs : n_refs + n_scaled], refs[n_refs + n_scaled : -2]
    out, turned = refs[-2:]

    @pl.when(pl.program_id(0) == 0)
    def _():
        turned[...] = jnp.concatenate([ref[0] for ref in scaleds], axis=0).T

    rows = jnp.concatenate([blocks[where][place] for where, place in layout], axis=0)
    total = dot(turned[...], rows, 1, 0)
    for ref in more:
        total = total + ref[...].astype(jnp.float32)
    out[...] = total.astype(out.dtype)


def weight_product(blocks, layout, scaleds, x, dtype, width, *more):
    tok = blocks[0].shape[1]
    ff = scaleds[0].shape[2]
    rows = len(layout) * tok
    tile = 512 if width >= 2048 else 256
    return pl.pallas_call(
        functools.partial(weight_kernel, len(blocks), len(scaleds), layout),
        grid=(width // tile,),
        in_specs=[pl.BlockSpec(block.shape[:2] + (tile,), lambda i: (0, 0, i)) for block in blocks]
        + [
            pl.BlockSpec((1,) + value.shape[1:], lambda i: (x, 0, 0), pipeline_mode=pl.Buffered(1))
            for value in scaleds
        ]
        + [pl.BlockSpec((ff, tile), lambda i: (0, i)) for _ in more],
        out_specs=pl.BlockSpec((ff, tile), lambda i: (0, i)),
        out_shape=jax.ShapeDtypeStruct((ff, width), dtype),
        scratch_shapes=[pltpu.VMEM((ff, rows), jnp.bfloat16)],
        compiler_params=pltpu.CompilerParams(vmem_limit_bytes=VMEM_BYTES),
        cost_estimate=pl.CostEstimate(
            flops=2 * rows * width * ff,
            bytes_accessed=2 * rows * (width + ff) + 4 * ff * width,
            transcendentals=0,
        ),
        name="weight_product",
    )(*blocks, *scaleds, *more)


def body(ring):
    chips = len(ring)
    half = chips // 2
    offsets = [0]
    for step in range(1, half):
        offsets += [-step, step]
    offsets.append(half)
    place_of = {chip: at for at, chip in enumerate(ring)}
    meta_table = np.asarray(
        [
            [e, e ^ 1] + [2 * ring[(place_of[e // 2] + off) % chips] + e % 2 for off in offsets]
            for e in range(2 * chips)
        ],
        np.int32,
    )

    def along(step):
        return [
            (2 * ring[at] + core, 2 * ring[(at + step) % chips] + core)
            for at in range(chips)
            for core in range(2)
        ]

    forward, backward = along(1), along(-1)
    sibling = [(e, e ^ 1) for e in range(2 * chips)]

    def shards(expert_ids, route_probs, expert_hidden, down_weight, out_grad):
        tok, top = expert_ids.shape
        n_dp = lax.axis_size("dp")
        n_ex = lax.axis_size("expert")
        cap = expert_hidden.shape[3]
        slots = cap * n_ex
        ff = down_weight.shape[1]
        width = down_weight.shape[2]
        weight = down_weight[0]
        replica = lax.axis_index("dp")
        expert = lax.axis_index("expert")
        per = n_dp // 2
        meta = lax.dynamic_index_in_dim(jnp.asarray(meta_table), expert, 0, keepdims=False)

        def shift(value, step):
            return lax.ppermute(value, "dp", [(i, (i + step) % n_dp) for i in range(n_dp)])

        def ring_send(value, step):
            return lax.ppermute(value, "expert", forward if step > 0 else backward)

        def swap(value):
            return lax.ppermute(value, "expert", sibling)

        room = 128 * -(-max(4 * top, 2 * n_ex) // 128)
        narrow = lambda value: lax.reduce_precision(value, 8, 7)
        high = narrow(route_probs)
        middle = narrow(route_probs - high)
        low = route_probs - high - middle
        routes = jnp.concatenate([expert_ids.astype(jnp.float32), high, middle, low], axis=1)
        routes = jnp.pad(routes.astype(jnp.bfloat16), ((0, 0), (0, room - 4 * top)))

        def width_shard(d):
            at = ((replica + d) % n_dp) * width
            return jnp.concatenate([lax.dynamic_slice_in_dim(out_grad, at, width, axis=1), routes], axis=1)

        blocks = {0: jnp.stack([width_shard(0)] + [shift(width_shard(d), d) for d in range(1, n_dp)])}

        sibling_weight = swap(weight)
        hidden = expert_hidden[0, 0].transpose(1, 0, 2).reshape(slots, ff)
        hiddens = [hidden] + [shift(hidden, d) for d in range(1, n_dp)]
        hiddens = [(value, swap(value)) for value in hiddens]

        parts, scaleds, layout, facts = {}, [], [], []
        own_back, sent_back = [], [[] for _ in range(1, n_dp)]
        refs = []

        def work(items, *done):
            used, plan = [], []
            for off, d in items:
                value = blocks[off][d // per] if off == half else blocks[off]
                if not any(value is other for other in used):
                    used.append(value)
                where = [value is other for other in used].index(True)
                plan.append((where, d % per if off == half else d, d, offsets.index(off)))
            if done:
                gated = [after(used[0], *done)] + used[1:]
            else:
                gated = used
            made, scaled, back, fact = block_product(
                tuple(plan), meta, gated, hiddens, weight, sibling_weight, n_ex, top
            )
            for item, part in zip(items, made):
                parts[item] = part
            for d in sorted(scaled):
                scaleds.append(scaled[d])
                for (off, e), (where, place, _, _) in zip(items, plan):
                    if e == d:
                        if not any(used[where] is other for other in refs):
                            refs.append(used[where])
                        layout.append(([used[where] is other for other in refs].index(True), place))
                if d == 0:
                    own_back.append(back[0])
                    facts.append(fact)
                else:
                    sent_back[d - 1].append(shift(back[d], -d))
            return made[0]

        both = lambda offs: [(off, d) for d in range(n_dp) for off in offs]
        gate = ()
        for step in range(1, half):
            sent = blocks[1 - step], blocks[step - 1]
            if gate:
                sent = after(sent[0], *gate), after(sent[1], *gate)
            blocks[-step] = ring_send(sent[0], 1)
            blocks[step] = ring_send(sent[1], -1)
            if step == 1:
                following = [(off, 0) for off in offsets[:3]]
            elif step == 2:
                following = [(off, d) for d in range(n_dp) for off in offsets[:5] if d > 0 or off not in offsets[:3]]
            else:
                following = both([-step, step])
            if step == half - 1:
                break
            if step > 1:
                gate = (ready,)
            ready = work(following)
        sent = after(blocks[1 - half][:per], ready), after(blocks[half - 1][per:], ready)
        blocks[half] = [ring_send(sent[0], 1), ring_send(sent[1], -1)]
        ready = work(following)
        work(both([half]), ready)

        carry = {}

        def hop_on(hop, *done):
            for direction in (1, -1):
                off = half if hop == half else hop * direction
                group = range(n_dp)
                if hop == half:
                    group = range(per) if direction == 1 else range(per, n_dp)
                first = 0 if direction == 1 else per
                values = []
                for d in group:
                    value = parts[off, d]
                    if hop == half - 1 and 0 <= d - first < per:
                        value = value.astype(jnp.float32) + carry[direction][d - first].astype(jnp.float32)
                    elif hop < half - 1:
                        value = value.astype(jnp.float32) + carry[direction][d].astype(jnp.float32)
                    values.append(value.astype(jnp.bfloat16))
                carry[direction] = ring_send(after(jnp.stack(values), *done), direction)
            return carry[1], carry[-1]

        first = hop_on(half)
        other = weight_product(
            [after(refs[0], parts[half, n_dp - 1])] + refs[1:], layout, scaleds, 1, jnp.bfloat16, width
        )
        swapped = swap(other)
        second = hop_on(half - 1, other)
        spread, spread_other = spread_product(
            [after(facts[0][0], *first)] + [fact[0] for fact in facts[1:]],
            [fact[1] for fact in facts],
            [own_back] + sent_back,
            slots,
        )
        spread_swapped = swap(spread_other)
        for hop in range(half - 2, 1, -1):
            hop_on(hop, spread)
        weight_grad = weight_product(
            [after(refs[0], *second)] + refs[1:], layout, scaleds, 0, jnp.float32, width, swapped
        )
        hop_on(1, weight_grad)
        hidden_grad = spread + spread_swapped
        hidden_grad = hidden_grad.reshape(cap, n_ex, ff).transpose(1, 0, 2)[None, None]

        layer_out = jnp.zeros((tok, n_dp * width), jnp.bfloat16)
        inner = jnp.zeros((tok, n_ex), jnp.float32)
        for d in reversed(range(n_dp)):
            total = parts[0, d].astype(jnp.float32)
            total = total + carry[1][d].astype(jnp.float32) + carry[-1][d].astype(jnp.float32)
            total = total.astype(jnp.bfloat16)
            piece = total if d == 0 else shift(total, -d)
            layer_out = lax.dynamic_update_slice_in_dim(
                layer_out, piece[:, :width], ((replica + d) % n_dp) * width, axis=1
            )
            found = piece[:, width:].astype(jnp.float32)
            inner = inner + found[:, :n_ex] + found[:, n_ex : 2 * n_ex]

        mine = expert_ids[:, :, None] == jnp.arange(n_ex, dtype=jnp.int32)
        prob_grad = jnp.sum(jnp.where(mine, inner[:, None, :], 0.0), axis=2)
        return (layer_out, prob_grad, hidden_grad, weight_grad[None])

    return shards


def solution(mesh):
    placed = (
        P(("dp", "expert"), None),
        P(("dp", "expert"), None),
        P("dp", "expert", None, None, None),
        P("expert", None, "dp"),
        P(("dp", "expert"), None),
    )
    return jax.shard_map(
        body(chip_ring(mesh)),
        mesh=mesh,
        in_specs=placed,
        out_specs=(
            P(("dp", "expert"), None),
            P(("dp", "expert"), None),
            P("dp", "expert", None, None, None),
            P("expert", None, "dp"),
        ),
        check_vma=False,
    )
```

```python
import functools

import jax
import jax.numpy as jnp
import numpy as np
from jax import lax
from jax.experimental import pallas as pl
from jax.experimental.pallas import tpu as pltpu
from jax.sharding import PartitionSpec as P

MIB = 1024 * 1024


def kernel_memory(rows):
    return pltpu.CompilerParams(vmem_limit_bytes=(20 if rows <= 1024 else 48) * MIB)


def dot(a, b, ca, cb):
    return lax.dot_general(a, b, (((ca,), (cb,)), ((), ())), preferred_element_type=jnp.float32)


def after(value, *done):
    return lax.optimization_barrier((value, *done))[0]


def chip_ring(mesh):
    chips = mesh.shape["expert"] // 2
    devices = mesh.devices.reshape(mesh.shape["dp"], -1)
    if not hasattr(devices[0, 0], "coords"):
        return list(range(chips))
    at = [tuple(devices[0, 2 * chip].coords)[1:] for chip in range(chips)]
    rows = max(z for _, z in at) + 1
    cols = max(y for y, _ in at) + 1
    if rows * cols != chips or rows % 2:
        return list(range(chips))
    walk = [(0, z) for z in range(rows)]
    for step, z in enumerate(reversed(range(rows))):
        span = range(1, cols)
        walk += [(y, z) for y in (span if step % 2 == 0 else reversed(span))]
    return [at.index(place) for place in walk]


def pack_kernel(top, where, ids, probs, grads, *outs):
    tok = grads.shape[0]
    width = grads.shape[1] // len(outs)
    room = outs[0].shape[1] - width
    row = lax.broadcasted_iota(jnp.int32, (tok, tok), 0)
    col = lax.broadcasted_iota(jnp.int32, (tok, tok), 1)
    same = (row == col).astype(jnp.float32)

    def columns(value):
        return lax.dot_general(
            same,
            value,
            (((1,), (1,)), ((), ())),
            precision=lax.Precision.HIGHEST,
            preferred_element_type=jnp.float32,
        )

    prob = columns(probs[...])
    high = prob.astype(jnp.bfloat16)
    middle = (prob - high.astype(jnp.float32)).astype(jnp.bfloat16)
    low = (prob - high.astype(jnp.float32) - middle.astype(jnp.float32)).astype(jnp.bfloat16)
    named = columns(ids[...].astype(jnp.float32)).astype(jnp.bfloat16)
    blank = jnp.zeros((tok, room - 4 * top), jnp.bfloat16)
    routes = jnp.concatenate([named, high, middle, low, blank], axis=1)
    for d, out in enumerate(outs):
        at = lax.rem(where[0] + d, len(outs)) * width
        out[:, :width] = grads[:, pl.ds(pl.multiple_of(at, 128), width)]
        out[:, width:] = routes


def pack(where, ids, probs, grads, n_dp, room):
    top, tok = ids.shape
    width = grads.shape[1] // n_dp
    vmem = pl.BlockSpec(memory_space=pltpu.VMEM)
    return pl.pallas_call(
        functools.partial(pack_kernel, top),
        in_specs=[pl.BlockSpec(memory_space=pltpu.SMEM)] + [vmem] * 3,
        out_specs=[vmem] * n_dp,
        out_shape=[jax.ShapeDtypeStruct((tok, width + room), jnp.bfloat16)] * n_dp,
        compiler_params=kernel_memory(tok),
        name="pack",
    )(where, ids, probs, grads)


def sum_kernel(starts, n_out, *refs):
    outs = refs[-n_out:]
    at = 0
    for out, (n_rows, arrives) in zip(outs, starts):
        carry = refs[at + n_rows] if arrives else None
        for i in range(n_rows):
            value = refs[at + i][...]
            if carry is not None and arrives[0] <= i < arrives[1]:
                value = value.astype(jnp.float32) + carry[i - arrives[0]].astype(jnp.float32)
            out[i] = value.astype(jnp.bfloat16)
        at += n_rows + (1 if arrives else 0)


def sums(jobs):
    tok, full = jobs[0][0][0].shape
    flat, starts, shapes = [], [], []
    for parts, carry, first, last in jobs:
        flat += list(parts) + [carry]
        starts.append((len(parts), (first, last)))
        shapes.append(jax.ShapeDtypeStruct((len(parts), tok, full), jnp.bfloat16))
    vmem = pl.BlockSpec(memory_space=pltpu.VMEM)
    return pl.pallas_call(
        functools.partial(sum_kernel, tuple(starts), len(shapes)),
        in_specs=[vmem] * len(flat),
        out_specs=[vmem] * len(shapes),
        out_shape=shapes,
        compiler_params=kernel_memory(tok),
        name="sums",
    )(*flat)


def close_kernel(n_dp, *refs):
    parts, (one, two), outs = refs[:n_dp], refs[n_dp : n_dp + 2], refs[n_dp + 2 :]
    for d, out in enumerate(outs):
        value = parts[d][...].astype(jnp.float32) + one[d].astype(jnp.float32)
        out[...] = (value + two[d].astype(jnp.float32)).astype(jnp.bfloat16)


def close(parts, one, two):
    vmem = pl.BlockSpec(memory_space=pltpu.VMEM)
    return pl.pallas_call(
        functools.partial(close_kernel, len(parts)),
        in_specs=[vmem] * (len(parts) + 2),
        out_specs=[vmem] * len(parts),
        out_shape=[jax.ShapeDtypeStruct(part.shape, jnp.bfloat16) for part in parts],
        compiler_params=kernel_memory(parts[0].shape[0]),
        name="close",
    )(*parts, one, two)


def home_kernel(n_ex, where, ids, *refs):
    pieces, (layer, prob) = refs[:-2], refs[-2:]
    n_dp = len(pieces)
    tok, top = ids.shape
    width = layer.shape[1] // n_dp
    inner = jnp.zeros((tok, n_ex), jnp.float32)
    for d, piece in enumerate(pieces):
        at = lax.rem(where[0] + d, n_dp) * width
        layer[:, pl.ds(pl.multiple_of(at, 128), width)] = piece[:, :width]
        more = piece[:, width:].astype(jnp.float32)
        inner = inner + more[:, :n_ex] + more[:, n_ex : 2 * n_ex]
    lane = lax.broadcasted_iota(jnp.int32, (tok, n_ex), 1)
    for k in range(top):
        mine = lane == ids[:, k : k + 1]
        prob[:, k : k + 1] = jnp.sum(jnp.where(mine, inner, 0.0), axis=1, keepdims=True)


def home(where, ids, pieces, width, n_ex):
    tok, top = ids.shape
    vmem = pl.BlockSpec(memory_space=pltpu.VMEM)
    return pl.pallas_call(
        functools.partial(home_kernel, n_ex),
        in_specs=[pl.BlockSpec(memory_space=pltpu.SMEM)] + [vmem] * (1 + len(pieces)),
        out_specs=[vmem] * 2,
        out_shape=[
            jax.ShapeDtypeStruct((tok, len(pieces) * width), jnp.bfloat16),
            jax.ShapeDtypeStruct((tok, top), jnp.float32),
        ],
        compiler_params=kernel_memory(tok),
        name="home",
    )(where, ids, *pieces)


def block_kernel(plan, refs_in, n_dp, n_ex, top, *refs):
    meta = refs[0]
    blocks = refs[1 : 1 + refs_in]
    at = 1 + refs_in
    replicas = sorted({item[2] for item in plan})
    hid = {d: refs[at + 2 * i : at + 2 * i + 2] for i, d in enumerate(replicas)}
    at += 2 * len(replicas)
    weights = refs[at : at + 2]
    at += 2
    parts = refs[at : at + len(plan)]
    at += len(plan)
    outs = {d: refs[at + 2 * i : at + 2 * i + 2] for i, d in enumerate(replicas)}
    at += 2 * len(replicas)
    index, prob = refs[at : at + 2] if 0 in replicas else (None, None)

    _, tok, full = blocks[0].shape
    ff, width = weights[0].shape
    slots = hid[replicas[0]][0].shape[0]
    count = len(plan) * tok
    rows = [blocks[where][place] for where, place, _, _ in plan]
    routes = jnp.concatenate([row[:, width:] for row in rows], axis=0).astype(jnp.float32)
    named = routes[:, :top]
    chance = routes[:, top : 2 * top] + routes[:, 2 * top : 3 * top] + routes[:, 3 * top : 4 * top]
    row = lax.broadcasted_iota(jnp.int32, (tok, tok), 0)
    col = lax.broadcasted_iota(jnp.int32, (tok, tok), 1)
    earlier = (col < row).astype(jnp.float32)
    lane = lax.broadcasted_iota(jnp.int32, (tok, slots), 1)
    spans = {d: [i for i, item in enumerate(plan) if item[2] == d] for d in replicas}
    helds, scaleds = [], []
    for x in range(2):
        mine = named == meta[x].astype(jnp.float32)
        here = jnp.sum(jnp.where(mine, chance, 0.0), axis=1, keepdims=True)
        taken = jnp.broadcast_to((here > 0.0).astype(jnp.float32), (count, 128))
        held = []
        for d in replicas:
            picks = []
            for n, i in enumerate(spans[d]):
                span = slice(i * tok, (i + 1) * tok)
                position = dot(earlier, taken[span], 1, 0)[:, :1].astype(jnp.int32)
                slot = jnp.where(here[span] > 0.0, position * n_ex + meta[2 + plan[i][3]], -1)
                picks.append((lane == slot).astype(jnp.bfloat16))
                if d == 0:
                    index[n * tok : (n + 1) * tok, x : x + 1] = slot
                    prob[n * tok : (n + 1) * tok, x : x + 1] = here[span]
            held.append(dot(jnp.concatenate(picks, axis=0), hid[d][x][...], 1, 0))
        held = jnp.concatenate(held, axis=0)
        scaled = (held * here).astype(jnp.bfloat16)
        base = 0
        for d in replicas:
            size = len(spans[d]) * tok
            outs[d][0][x] = scaled[base : base + size]
            base += size
        helds.append(held)
        scaleds.append(scaled)

    tile = 512
    for step in range(width // tile):
        cols = slice(step * tile, (step + 1) * tile)
        value = dot(scaleds[0], weights[0][:, cols], 1, 0) + dot(scaleds[1], weights[1][:, cols], 1, 0)
        value = value.astype(jnp.bfloat16)
        for i, out in enumerate(parts):
            out[:, cols] = value[i * tok : (i + 1) * tok]

    lhs = jnp.concatenate([row[:, :width] for row in rows], axis=0)
    lane = lax.broadcasted_iota(jnp.int32, (count, full - width), 1)
    extra = jnp.zeros((count, full - width), jnp.float32)
    for x in range(2):
        inner = jnp.zeros((count, 1), jnp.float32)
        step_ff = 256
        for step in range(ff // step_ff):
            cols = slice(step * step_ff, (step + 1) * step_ff)
            value = dot(lhs, weights[x][cols, :], 1, 1)
            inner = inner + jnp.sum(value * helds[x][:, cols], axis=1, keepdims=True)
            value = value.astype(jnp.bfloat16)
            base = 0
            for d in replicas:
                size = len(spans[d]) * tok
                outs[d][1][x, :, cols] = value[base : base + size]
                base += size
        high = inner.astype(jnp.bfloat16).astype(jnp.float32)
        extra = jnp.where(lane == meta[x], high, extra)
        extra = jnp.where(lane == meta[x] + n_ex, inner - high, extra)
    extra = extra.astype(jnp.bfloat16)
    for i, out in enumerate(parts):
        out[:, width:] = extra[i * tok : (i + 1) * tok]


def block_product(plan, meta, blocks, hiddens, w_own, w_sib, n_ex, top):
    n_dp = len(hiddens)
    _, tok, full = blocks[0].shape
    ff, width = w_own.shape
    slots = hiddens[0][0].shape[0]
    replicas = sorted({item[2] for item in plan})
    vmem = pl.BlockSpec(memory_space=pltpu.VMEM)
    bf16 = lambda *shape: jax.ShapeDtypeStruct(shape, jnp.bfloat16)
    out_shape = [bf16(tok, full) for _ in plan]
    sizes = {d: tok * sum(item[2] == d for item in plan) for d in replicas}
    for d in replicas:
        out_shape += [bf16(2, sizes[d], ff)] * 2
    if 0 in replicas:
        out_shape.append(jax.ShapeDtypeStruct((sizes[0], 2), jnp.int32))
        out_shape.append(jax.ShapeDtypeStruct((sizes[0], 2), jnp.float32))
    hid = [value for d in replicas for value in hiddens[d]]
    count = len(plan) * tok
    chips_rows = n_ex * tok * n_dp // 2
    made = pl.pallas_call(
        functools.partial(block_kernel, plan, len(blocks), n_dp, n_ex, top),
        in_specs=[pl.BlockSpec(memory_space=pltpu.SMEM)] + [vmem] * (len(blocks) + len(hid) + 2),
        out_specs=[vmem] * len(out_shape),
        out_shape=out_shape,
        compiler_params=kernel_memory(chips_rows),
        cost_estimate=pl.CostEstimate(
            flops=8 * count * ff * width,
            bytes_accessed=4 * ff * width + 4 * count * (full + ff),
            transcendentals=0,
        ),
        name="block_product",
    )(meta, *blocks, *hid, w_own, w_sib)
    parts = made[: len(plan)]
    rest = made[len(plan) :]
    scaled = {d: rest[2 * i] for i, d in enumerate(replicas)}
    back = {d: rest[2 * i + 1] for i, d in enumerate(replicas)}
    return parts, scaled, back, rest[2 * len(replicas) :]


def spread_kernel(sizes, *refs):
    n_parts = len(sizes[0])
    index, prob = refs[:n_parts], refs[n_parts : 2 * n_parts]
    backs = list(refs[2 * n_parts : -2])
    outs = refs[-2:]
    slots = outs[0].shape[0]
    slot = jnp.concatenate([ref[...] for ref in index], axis=0)
    weight = jnp.concatenate([ref[...] for ref in prob], axis=0)
    lane = lax.broadcasted_iota(jnp.int32, (slot.shape[0], slots), 1)
    for x, out in enumerate(outs):
        back, at = None, 0
        for pieces in sizes:
            value = jnp.concatenate([ref[x] for ref in backs[at : at + len(pieces)]], axis=0)
            at += len(pieces)
            value = value.astype(jnp.float32)
            back = value if back is None else back + value
        pick = (lane == slot[:, x : x + 1]).astype(jnp.bfloat16)
        mine = (back * weight[:, x : x + 1]).astype(jnp.bfloat16)
        out[...] = dot(pick, mine, 0, 0).astype(jnp.bfloat16)


def spread_product(index, prob, backs, slots):
    sizes = [[part.shape[1] for part in parts] for parts in backs]
    ff = backs[0][0].shape[2]
    rows = sum(sizes[0])
    flat = [part for parts in backs for part in parts]
    vmem = pl.BlockSpec(memory_space=pltpu.VMEM)
    return pl.pallas_call(
        functools.partial(spread_kernel, sizes),
        in_specs=[vmem] * (2 * len(index) + len(flat)),
        out_specs=[vmem] * 2,
        out_shape=[jax.ShapeDtypeStruct((slots, ff), jnp.bfloat16)] * 2,
        compiler_params=kernel_memory(rows * len(backs)),
        cost_estimate=pl.CostEstimate(
            flops=4 * rows * slots * ff,
            bytes_accessed=4 * (1 + len(backs)) * rows * ff,
            transcendentals=0,
        ),
        name="spread_product",
    )(*index, *prob, *flat)


def weight_kernel(n_refs, n_scaled, layout, *refs):
    blocks, scaleds, more = refs[:n_refs], refs[n_refs : n_refs + n_scaled], refs[n_refs + n_scaled : -2]
    out, turned = refs[-2:]

    @pl.when(pl.program_id(0) == 0)
    def _():
        turned[...] = jnp.concatenate([ref[0] for ref in scaleds], axis=0).T

    rows = jnp.concatenate([blocks[where][place] for where, place in layout], axis=0)
    total = dot(turned[...], rows, 1, 0)
    for ref in more:
        total = total + ref[...].astype(jnp.float32)
    out[...] = total.astype(out.dtype)


def weight_product(blocks, layout, scaleds, x, dtype, width, *more):
    tok = blocks[0].shape[1]
    ff = scaleds[0].shape[2]
    rows = len(layout) * tok
    tile = 512 if width >= 2048 else 256
    return pl.pallas_call(
        functools.partial(weight_kernel, len(blocks), len(scaleds), layout),
        grid=(width // tile,),
        in_specs=[pl.BlockSpec(block.shape[:2] + (tile,), lambda i: (0, 0, i)) for block in blocks]
        + [
            pl.BlockSpec((1,) + value.shape[1:], lambda i: (x, 0, 0), pipeline_mode=pl.Buffered(1))
            for value in scaleds
        ]
        + [pl.BlockSpec((ff, tile), lambda i: (0, i)) for _ in more],
        out_specs=pl.BlockSpec((ff, tile), lambda i: (0, i)),
        out_shape=jax.ShapeDtypeStruct((ff, width), dtype),
        scratch_shapes=[pltpu.VMEM((ff, rows), jnp.bfloat16)],
        compiler_params=kernel_memory(rows),
        cost_estimate=pl.CostEstimate(
            flops=2 * rows * width * ff,
            bytes_accessed=2 * rows * (width + ff) + 4 * ff * width,
            transcendentals=0,
        ),
        name="weight_product",
    )(*blocks, *scaleds, *more)


def body(ring):
    chips = len(ring)
    half = chips // 2
    offsets = [0]
    for step in range(1, half):
        offsets += [-step, step]
    offsets.append(half)
    place_of = {chip: at for at, chip in enumerate(ring)}
    meta_table = np.asarray(
        [
            [e, e ^ 1] + [2 * ring[(place_of[e // 2] + off) % chips] + e % 2 for off in offsets]
            for e in range(2 * chips)
        ],
        np.int32,
    )

    def along(step):
        return [
            (2 * ring[at] + core, 2 * ring[(at + step) % chips] + core)
            for at in range(chips)
            for core in range(2)
        ]

    forward, backward = along(1), along(-1)
    sibling = [(e, e ^ 1) for e in range(2 * chips)]

    def shards(expert_ids, route_probs, expert_hidden, down_weight, out_grad):
        tok, top = expert_ids.shape
        n_dp = lax.axis_size("dp")
        n_ex = lax.axis_size("expert")
        cap = expert_hidden.shape[3]
        slots = cap * n_ex
        ff = down_weight.shape[1]
        width = down_weight.shape[2]
        weight = down_weight[0]
        replica = lax.axis_index("dp")
        expert = lax.axis_index("expert")
        per = n_dp // 2
        meta = lax.dynamic_index_in_dim(jnp.asarray(meta_table), expert, 0, keepdims=False)

        def shift(value, step):
            return lax.ppermute(value, "dp", [(i, (i + step) % n_dp) for i in range(n_dp)])

        def ring_send(value, step):
            return lax.ppermute(value, "expert", forward if step > 0 else backward)

        def swap(value):
            return lax.ppermute(value, "expert", sibling)

        room = 128 * -(-max(4 * top, 2 * n_ex) // 128)
        where = replica.reshape(1).astype(jnp.int32)
        packed = pack(where, expert_ids.T, route_probs.T, out_grad, n_dp, room)
        blocks = {0: jnp.stack([packed[0]] + [shift(packed[d], d) for d in range(1, n_dp)])}

        sibling_weight = swap(weight)
        hidden = expert_hidden[0, 0].transpose(1, 0, 2).reshape(slots, ff)
        hiddens = [(hidden, swap(hidden))]
        for d in range(1, n_dp):
            value = shift(after(hidden, blocks[0]), d)
            hiddens.append((value, None))

        parts, scaleds, layout, facts = {}, [], [], []
        own_back, sent_back = [], [[] for _ in range(1, n_dp)]
        refs = []

        def work(items, *done):
            used, plan = [], []
            for off, d in items:
                value = blocks[off][d // per] if off == half else blocks[off]
                if not any(value is other for other in used):
                    used.append(value)
                where = [value is other for other in used].index(True)
                plan.append((where, d % per if off == half else d, d, offsets.index(off)))
            if done:
                gated = [after(used[0], *done)] + used[1:]
            else:
                gated = used
            made, scaled, back, fact = block_product(
                tuple(plan), meta, gated, hiddens, weight, sibling_weight, n_ex, top
            )
            for item, part in zip(items, made):
                parts[item] = part
            for d in sorted(scaled):
                scaleds.append(scaled[d])
                for (off, e), (where, place, _, _) in zip(items, plan):
                    if e == d:
                        if not any(used[where] is other for other in refs):
                            refs.append(used[where])
                        layout.append(([used[where] is other for other in refs].index(True), place))
                if d == 0:
                    own_back.append(back[0])
                    facts.append(fact)
                else:
                    sent_back[d - 1].append(shift(back[d], -d))
            return made[0]

        both = lambda offs: [(off, d) for d in range(n_dp) for off in offs]
        gate = ()
        for step in range(1, half):
            sent = blocks[1 - step], blocks[step - 1]
            if gate:
                sent = after(sent[0], *gate), after(sent[1], *gate)
            blocks[-step] = ring_send(sent[0], 1)
            blocks[step] = ring_send(sent[1], -1)
            if step == 1:
                following = [(off, 0) for off in offsets[:3]]
            elif step == 2:
                following = [(off, d) for d in range(n_dp) for off in offsets[:5] if d > 0 or off not in offsets[:3]]
            else:
                following = both([-step, step])
            if step == half - 1:
                break
            if step > 1:
                gate = (ready,)
            if step == 2:
                for d in range(1, n_dp):
                    value = hiddens[d][0]
                    hiddens[d] = value, swap(after(value, blocks[-step], blocks[step], ready))
            ready = work(following)
        sent = after(blocks[1 - half], ready)[:per], after(blocks[half - 1], ready)[per:]
        blocks[half] = [ring_send(sent[0], 1), ring_send(sent[1], -1)]
        ready = work(following)
        work(both([half]), ready)

        carry = {}

        def hop_on(hop, *done):
            every = range(n_dp)
            if hop == half:
                values = [jnp.stack([parts[half, d] for d in every[:per]])]
                values.append(jnp.stack([parts[half, d] for d in every[per:]]))
            else:
                first, last = ((0, per), (per, n_dp)) if hop == half - 1 else ((0, n_dp), (0, n_dp))
                values = sums(
                    [
                        ([parts[hop, d] for d in every], carry[1], *first),
                        ([parts[-hop, d] for d in every], carry[-1], *last),
                    ]
                )
            values = [after(value, *done) for value in values]
            carry[1] = ring_send(values[0], 1)
            carry[-1] = ring_send(values[1], -1)
            sending[:] = values
            return carry[1], carry[-1]

        sending = []
        hop_on(half)
        second = hop_on(half - 1)
        other = weight_product(
            [after(refs[0], *sending, *[value for sent in sent_back for value in sent[:-1]])] + refs[1:], layout, scaleds, 1, jnp.bfloat16, width
        )
        swapped = swap(after(other, *second))
        third = hop_on(half - 2, other)
        spread, spread_other = spread_product(
            [after(facts[0][0], *second)] + [fact[0] for fact in facts[1:]],
            [fact[1] for fact in facts],
            [own_back] + sent_back,
            slots,
        )
        hidden_grad = spread + swap(spread_other)
        hidden_grad = hidden_grad.reshape(cap, n_ex, ff).transpose(1, 0, 2)[None, None]
        for hop in range(half - 3, 0, -1):
            hop_on(hop, spread)
        weight_grad = weight_product(
            [after(refs[0], *third)] + refs[1:], layout, scaleds, 0, jnp.float32, width, swapped
        )
        totals = close([after(parts[0, 0], weight_grad)] + [parts[0, d] for d in range(1, n_dp)], carry[1], carry[-1])
        pieces = [totals[0]] + [shift(totals[d], -d) for d in range(1, n_dp)]
        layer_out, prob_grad = home(where, expert_ids, pieces, width, n_ex)
        return (layer_out, prob_grad, hidden_grad, weight_grad[None])

    return shards


def solution(mesh):
    placed = (
        P(("dp", "expert"), None),
        P(("dp", "expert"), None),
        P("dp", "expert", None, None, None),
        P("expert", None, "dp"),
        P(("dp", "expert"), None),
    )
    return jax.shard_map(
        body(chip_ring(mesh)),
        mesh=mesh,
        in_specs=placed,
        out_specs=(
            P(("dp", "expert"), None),
            P(("dp", "expert"), None),
            P("dp", "expert", None, None, None),
            P("expert", None, "dp"),
        ),
        check_vma=False,
    )
```

```python
import functools

import jax
import jax.numpy as jnp
import numpy as np
from jax import lax
from jax.experimental import pallas as pl
from jax.experimental.pallas import tpu as pltpu
from jax.sharding import PartitionSpec as P

MIB = 1024 * 1024


def kernel_memory(rows):
    return pltpu.CompilerParams(vmem_limit_bytes=(20 if rows <= 1024 else 48) * MIB)


def dot(a, b, ca, cb):
    return lax.dot_general(a, b, (((ca,), (cb,)), ((), ())), preferred_element_type=jnp.float32)


def after(value, *done):
    return lax.optimization_barrier((value, *done))[0]


def chip_ring(mesh):
    chips = mesh.shape["expert"] // 2
    devices = mesh.devices.reshape(mesh.shape["dp"], -1)
    if not hasattr(devices[0, 0], "coords"):
        return list(range(chips))
    at = [tuple(devices[0, 2 * chip].coords)[1:] for chip in range(chips)]
    rows = max(z for _, z in at) + 1
    cols = max(y for y, _ in at) + 1
    if rows * cols != chips or rows % 2:
        return list(range(chips))
    walk = [(0, z) for z in range(rows)]
    for step, z in enumerate(reversed(range(rows))):
        span = range(1, cols)
        walk += [(y, z) for y in (span if step % 2 == 0 else reversed(span))]
    return [at.index(place) for place in walk]


def pack_kernel(top, where, ids, probs, grads, *outs):
    tok = grads.shape[0]
    width = grads.shape[1] // len(outs)
    room = outs[0].shape[1] - width
    row = lax.broadcasted_iota(jnp.int32, (tok, tok), 0)
    col = lax.broadcasted_iota(jnp.int32, (tok, tok), 1)
    same = (row == col).astype(jnp.float32)

    def columns(value):
        return lax.dot_general(
            same,
            value,
            (((1,), (1,)), ((), ())),
            precision=lax.Precision.HIGHEST,
            preferred_element_type=jnp.float32,
        )

    prob = columns(probs[...])
    high = prob.astype(jnp.bfloat16)
    middle = (prob - high.astype(jnp.float32)).astype(jnp.bfloat16)
    low = (prob - high.astype(jnp.float32) - middle.astype(jnp.float32)).astype(jnp.bfloat16)
    named = columns(ids[...].astype(jnp.float32)).astype(jnp.bfloat16)
    blank = jnp.zeros((tok, room - 4 * top), jnp.bfloat16)
    routes = jnp.concatenate([named, high, middle, low, blank], axis=1)
    for d, out in enumerate(outs):
        at = lax.rem(where[0] + d, len(outs)) * width
        out[:, :width] = grads[:, pl.ds(pl.multiple_of(at, 128), width)]
        out[:, width:] = routes


def pack(where, ids, probs, grads, n_dp, room):
    top, tok = ids.shape
    width = grads.shape[1] // n_dp
    vmem = pl.BlockSpec(memory_space=pltpu.VMEM)
    return pl.pallas_call(
        functools.partial(pack_kernel, top),
        in_specs=[pl.BlockSpec(memory_space=pltpu.SMEM)] + [vmem] * 3,
        out_specs=[vmem] * n_dp,
        out_shape=[jax.ShapeDtypeStruct((tok, width + room), jnp.bfloat16)] * n_dp,
        compiler_params=kernel_memory(tok),
        name="pack",
    )(where, ids, probs, grads)


def sum_kernel(starts, n_out, *refs):
    outs = refs[-n_out:]
    at = 0
    for out, (n_rows, arrives) in zip(outs, starts):
        carry = refs[at + n_rows] if arrives else None
        for i in range(n_rows):
            value = refs[at + i][...]
            if carry is not None and arrives[0] <= i < arrives[1]:
                value = value.astype(jnp.float32) + carry[i - arrives[0]].astype(jnp.float32)
            out[i] = value.astype(jnp.bfloat16)
        at += n_rows + (1 if arrives else 0)


def sums(jobs):
    tok, full = jobs[0][0][0].shape
    flat, starts, shapes = [], [], []
    for parts, carry, first, last in jobs:
        flat += list(parts) + [carry]
        starts.append((len(parts), (first, last)))
        shapes.append(jax.ShapeDtypeStruct((len(parts), tok, full), jnp.bfloat16))
    vmem = pl.BlockSpec(memory_space=pltpu.VMEM)
    return pl.pallas_call(
        functools.partial(sum_kernel, tuple(starts), len(shapes)),
        in_specs=[vmem] * len(flat),
        out_specs=[vmem] * len(shapes),
        out_shape=shapes,
        compiler_params=kernel_memory(tok),
        name="sums",
    )(*flat)


def close_kernel(n_dp, *refs):
    parts, (one, two), outs = refs[:n_dp], refs[n_dp : n_dp + 2], refs[n_dp + 2 :]
    for d, out in enumerate(outs):
        value = parts[d][...].astype(jnp.float32) + one[d].astype(jnp.float32)
        out[...] = (value + two[d].astype(jnp.float32)).astype(jnp.bfloat16)


def close(parts, one, two):
    vmem = pl.BlockSpec(memory_space=pltpu.VMEM)
    return pl.pallas_call(
        functools.partial(close_kernel, len(parts)),
        in_specs=[vmem] * (len(parts) + 2),
        out_specs=[vmem] * len(parts),
        out_shape=[jax.ShapeDtypeStruct(part.shape, jnp.bfloat16) for part in parts],
        compiler_params=kernel_memory(parts[0].shape[0]),
        name="close",
    )(*parts, one, two)


def home_kernel(n_ex, where, ids, *refs):
    pieces, (layer, prob) = refs[:-2], refs[-2:]
    n_dp = len(pieces)
    tok, top = ids.shape
    width = layer.shape[1] // n_dp
    inner = jnp.zeros((tok, n_ex), jnp.float32)
    for d, piece in enumerate(pieces):
        at = lax.rem(where[0] + d, n_dp) * width
        layer[:, pl.ds(pl.multiple_of(at, 128), width)] = piece[:, :width]
        more = piece[:, width:].astype(jnp.float32)
        inner = inner + more[:, :n_ex] + more[:, n_ex : 2 * n_ex]
    lane = lax.broadcasted_iota(jnp.int32, (tok, n_ex), 1)
    for k in range(top):
        mine = lane == ids[:, k : k + 1]
        prob[:, k : k + 1] = jnp.sum(jnp.where(mine, inner, 0.0), axis=1, keepdims=True)


def home(where, ids, pieces, width, n_ex):
    tok, top = ids.shape
    vmem = pl.BlockSpec(memory_space=pltpu.VMEM)
    return pl.pallas_call(
        functools.partial(home_kernel, n_ex),
        in_specs=[pl.BlockSpec(memory_space=pltpu.SMEM)] + [vmem] * (1 + len(pieces)),
        out_specs=[vmem] * 2,
        out_shape=[
            jax.ShapeDtypeStruct((tok, len(pieces) * width), jnp.bfloat16),
            jax.ShapeDtypeStruct((tok, top), jnp.float32),
        ],
        compiler_params=kernel_memory(tok),
        name="home",
    )(where, ids, *pieces)


def block_kernel(plan, refs_in, n_dp, n_ex, top, *refs):
    meta = refs[0]
    blocks = refs[1 : 1 + refs_in]
    at = 1 + refs_in
    replicas = sorted({item[2] for item in plan})
    hid = {d: refs[at + 2 * i : at + 2 * i + 2] for i, d in enumerate(replicas)}
    at += 2 * len(replicas)
    weights = refs[at : at + 2]
    at += 2
    parts = refs[at : at + len(plan)]
    at += len(plan)
    outs = {d: refs[at + 2 * i : at + 2 * i + 2] for i, d in enumerate(replicas)}
    at += 2 * len(replicas)
    index, prob = refs[at : at + 2] if 0 in replicas else (None, None)

    _, tok, full = blocks[0].shape
    ff, width = weights[0].shape
    slots = hid[replicas[0]][0].shape[0]
    count = len(plan) * tok
    rows = [blocks[where][place] for where, place, _, _ in plan]
    routes = jnp.concatenate([row[:, width:] for row in rows], axis=0).astype(jnp.float32)
    named = routes[:, :top]
    chance = routes[:, top : 2 * top] + routes[:, 2 * top : 3 * top] + routes[:, 3 * top : 4 * top]
    row = lax.broadcasted_iota(jnp.int32, (tok, tok), 0)
    col = lax.broadcasted_iota(jnp.int32, (tok, tok), 1)
    earlier = (col < row).astype(jnp.float32)
    lane = lax.broadcasted_iota(jnp.int32, (tok, slots), 1)
    spans = {d: [i for i, item in enumerate(plan) if item[2] == d] for d in replicas}
    helds, scaleds = [], []
    for x in range(2):
        mine = named == meta[x].astype(jnp.float32)
        here = jnp.sum(jnp.where(mine, chance, 0.0), axis=1, keepdims=True)
        taken = jnp.broadcast_to((here > 0.0).astype(jnp.float32), (count, 128))
        held = []
        for d in replicas:
            picks = []
            for n, i in enumerate(spans[d]):
                span = slice(i * tok, (i + 1) * tok)
                position = dot(earlier, taken[span], 1, 0)[:, :1].astype(jnp.int32)
                slot = jnp.where(here[span] > 0.0, position * n_ex + meta[2 + plan[i][3]], -1)
                picks.append((lane == slot).astype(jnp.bfloat16))
                if d == 0:
                    index[n * tok : (n + 1) * tok, x : x + 1] = slot
                    prob[n * tok : (n + 1) * tok, x : x + 1] = here[span]
            held.append(dot(jnp.concatenate(picks, axis=0), hid[d][x][...], 1, 0))
        held = jnp.concatenate(held, axis=0)
        scaled = (held * here).astype(jnp.bfloat16)
        base = 0
        for d in replicas:
            size = len(spans[d]) * tok
            outs[d][0][x] = scaled[base : base + size]
            base += size
        helds.append(held)
        scaleds.append(scaled)

    tile = 512
    for step in range(width // tile):
        cols = slice(step * tile, (step + 1) * tile)
        value = dot(scaleds[0], weights[0][:, cols], 1, 0) + dot(scaleds[1], weights[1][:, cols], 1, 0)
        value = value.astype(jnp.bfloat16)
        for i, out in enumerate(parts):
            out[:, cols] = value[i * tok : (i + 1) * tok]

    lhs = jnp.concatenate([row[:, :width] for row in rows], axis=0)
    lane = lax.broadcasted_iota(jnp.int32, (count, full - width), 1)
    extra = jnp.zeros((count, full - width), jnp.float32)
    for x in range(2):
        inner = jnp.zeros((count, 1), jnp.float32)
        step_ff = 256
        for step in range(ff // step_ff):
            cols = slice(step * step_ff, (step + 1) * step_ff)
            value = dot(lhs, weights[x][cols, :], 1, 1)
            inner = inner + jnp.sum(value * helds[x][:, cols], axis=1, keepdims=True)
            value = value.astype(jnp.bfloat16)
            base = 0
            for d in replicas:
                size = len(spans[d]) * tok
                outs[d][1][x, :, cols] = value[base : base + size]
                base += size
        high = inner.astype(jnp.bfloat16).astype(jnp.float32)
        extra = jnp.where(lane == meta[x], high, extra)
        extra = jnp.where(lane == meta[x] + n_ex, inner - high, extra)
    extra = extra.astype(jnp.bfloat16)
    for i, out in enumerate(parts):
        out[:, width:] = extra[i * tok : (i + 1) * tok]


def block_product(plan, meta, blocks, hiddens, w_own, w_sib, n_ex, top):
    n_dp = len(hiddens)
    _, tok, full = blocks[0].shape
    ff, width = w_own.shape
    slots = hiddens[0][0].shape[0]
    replicas = sorted({item[2] for item in plan})
    vmem = pl.BlockSpec(memory_space=pltpu.VMEM)
    bf16 = lambda *shape: jax.ShapeDtypeStruct(shape, jnp.bfloat16)
    out_shape = [bf16(tok, full) for _ in plan]
    sizes = {d: tok * sum(item[2] == d for item in plan) for d in replicas}
    for d in replicas:
        out_shape += [bf16(2, sizes[d], ff)] * 2
    if 0 in replicas:
        out_shape.append(jax.ShapeDtypeStruct((sizes[0], 2), jnp.int32))
        out_shape.append(jax.ShapeDtypeStruct((sizes[0], 2), jnp.float32))
    hid = [value for d in replicas for value in hiddens[d]]
    count = len(plan) * tok
    chips_rows = n_ex * tok * n_dp // 2
    made = pl.pallas_call(
        functools.partial(block_kernel, plan, len(blocks), n_dp, n_ex, top),
        in_specs=[pl.BlockSpec(memory_space=pltpu.SMEM)] + [vmem] * (len(blocks) + len(hid) + 2),
        out_specs=[vmem] * len(out_shape),
        out_shape=out_shape,
        compiler_params=kernel_memory(chips_rows),
        cost_estimate=pl.CostEstimate(
            flops=8 * count * ff * width,
            bytes_accessed=4 * ff * width + 4 * count * (full + ff),
            transcendentals=0,
        ),
        name="block_product",
    )(meta, *blocks, *hid, w_own, w_sib)
    parts = made[: len(plan)]
    rest = made[len(plan) :]
    scaled = {d: rest[2 * i] for i, d in enumerate(replicas)}
    back = {d: rest[2 * i + 1] for i, d in enumerate(replicas)}
    return parts, scaled, back, rest[2 * len(replicas) :]


def spread_kernel(sizes, *refs):
    n_parts = len(sizes[0])
    index, prob = refs[:n_parts], refs[n_parts : 2 * n_parts]
    backs = list(refs[2 * n_parts : -2])
    outs = refs[-2:]
    slots = outs[0].shape[0]
    slot = jnp.concatenate([ref[...] for ref in index], axis=0)
    weight = jnp.concatenate([ref[...] for ref in prob], axis=0)
    lane = lax.broadcasted_iota(jnp.int32, (slot.shape[0], slots), 1)
    for x, out in enumerate(outs):
        back, at = None, 0
        for pieces in sizes:
            value = jnp.concatenate([ref[x] for ref in backs[at : at + len(pieces)]], axis=0)
            at += len(pieces)
            value = value.astype(jnp.float32)
            back = value if back is None else back + value
        pick = (lane == slot[:, x : x + 1]).astype(jnp.bfloat16)
        mine = (back * weight[:, x : x + 1]).astype(jnp.bfloat16)
        out[...] = dot(pick, mine, 0, 0).astype(jnp.bfloat16)


def spread_product(index, prob, backs, slots):
    sizes = [[part.shape[1] for part in parts] for parts in backs]
    ff = backs[0][0].shape[2]
    rows = sum(sizes[0])
    flat = [part for parts in backs for part in parts]
    vmem = pl.BlockSpec(memory_space=pltpu.VMEM)
    return pl.pallas_call(
        functools.partial(spread_kernel, sizes),
        in_specs=[vmem] * (2 * len(index) + len(flat)),
        out_specs=[vmem] * 2,
        out_shape=[jax.ShapeDtypeStruct((slots, ff), jnp.bfloat16)] * 2,
        compiler_params=kernel_memory(rows * len(backs)),
        cost_estimate=pl.CostEstimate(
            flops=4 * rows * slots * ff,
            bytes_accessed=4 * (1 + len(backs)) * rows * ff,
            transcendentals=0,
        ),
        name="spread_product",
    )(*index, *prob, *flat)


def weight_kernel(n_refs, n_scaled, layout, *refs):
    blocks, scaleds, more = refs[:n_refs], refs[n_refs : n_refs + n_scaled], refs[n_refs + n_scaled : -2]
    out, turned = refs[-2:]

    @pl.when(pl.program_id(0) == 0)
    def _():
        turned[...] = jnp.concatenate([ref[0] for ref in scaleds], axis=0).T

    rows = jnp.concatenate([blocks[where][place] for where, place in layout], axis=0)
    total = dot(turned[...], rows, 1, 0)
    for ref in more:
        total = total + ref[...].astype(jnp.float32)
    out[...] = total.astype(out.dtype)


def weight_product(blocks, layout, scaleds, x, dtype, width, *more):
    tok = blocks[0].shape[1]
    ff = scaleds[0].shape[2]
    rows = len(layout) * tok
    tile = 512 if width >= 2048 else 256
    return pl.pallas_call(
        functools.partial(weight_kernel, len(blocks), len(scaleds), layout),
        grid=(width // tile,),
        in_specs=[pl.BlockSpec(block.shape[:2] + (tile,), lambda i: (0, 0, i)) for block in blocks]
        + [
            pl.BlockSpec((1,) + value.shape[1:], lambda i: (x, 0, 0), pipeline_mode=pl.Buffered(1))
            for value in scaleds
        ]
        + [pl.BlockSpec((ff, tile), lambda i: (0, i)) for _ in more],
        out_specs=pl.BlockSpec((ff, tile), lambda i: (0, i)),
        out_shape=jax.ShapeDtypeStruct((ff, width), dtype),
        scratch_shapes=[pltpu.VMEM((ff, rows), jnp.bfloat16)],
        compiler_params=kernel_memory(rows),
        cost_estimate=pl.CostEstimate(
            flops=2 * rows * width * ff,
            bytes_accessed=2 * rows * (width + ff) + 4 * ff * width,
            transcendentals=0,
        ),
        name="weight_product",
    )(*blocks, *scaleds, *more)


def body(ring):
    chips = len(ring)
    half = chips // 2
    offsets = [0]
    for step in range(1, half):
        offsets += [-step, step]
    offsets.append(half)
    place_of = {chip: at for at, chip in enumerate(ring)}
    meta_table = np.asarray(
        [
            [e, e ^ 1] + [2 * ring[(place_of[e // 2] + off) % chips] + e % 2 for off in offsets]
            for e in range(2 * chips)
        ],
        np.int32,
    )

    def along(step):
        return [
            (2 * ring[at] + core, 2 * ring[(at + step) % chips] + core)
            for at in range(chips)
            for core in range(2)
        ]

    forward, backward = along(1), along(-1)
    sibling = [(e, e ^ 1) for e in range(2 * chips)]

    def shards(expert_ids, route_probs, expert_hidden, down_weight, out_grad):
        tok, top = expert_ids.shape
        n_dp = lax.axis_size("dp")
        n_ex = lax.axis_size("expert")
        cap = expert_hidden.shape[3]
        slots = cap * n_ex
        ff = down_weight.shape[1]
        width = down_weight.shape[2]
        weight = down_weight[0]
        replica = lax.axis_index("dp")
        expert = lax.axis_index("expert")
        per = n_dp // 2
        meta = lax.dynamic_index_in_dim(jnp.asarray(meta_table), expert, 0, keepdims=False)

        def shift(value, step):
            return lax.ppermute(value, "dp", [(i, (i + step) % n_dp) for i in range(n_dp)])

        def ring_send(value, step):
            return lax.ppermute(value, "expert", forward if step > 0 else backward)

        def swap(value):
            return lax.ppermute(value, "expert", sibling)

        room = 128 * -(-max(4 * top, 2 * n_ex) // 128)
        where = replica.reshape(1).astype(jnp.int32)
        packed = pack(where, expert_ids.T, route_probs.T, out_grad, n_dp, room)
        seeds = [packed[0]] + [shift(packed[d], d) for d in range(1, n_dp)]
        blocks = {0: [jnp.stack(seeds[:per]), jnp.stack(seeds[per:])]}

        sibling_weight = swap(weight)
        hidden = expert_hidden[0, 0].transpose(1, 0, 2).reshape(slots, ff)
        hiddens = [(hidden, swap(hidden))]

        parts, scaleds, layout, facts = {}, [], [], []
        own_back, sent_back = [], [[] for _ in range(1, n_dp)]
        refs = []

        def work(items, *done):
            used, plan = [], []
            for off, d in items:
                value = blocks[off][d // per]
                if not any(value is other for other in used):
                    used.append(value)
                where = [value is other for other in used].index(True)
                plan.append((where, d % per, d, offsets.index(off)))
            if done:
                gated = [after(used[0], *done)] + used[1:]
            else:
                gated = used
            made, scaled, back, fact = block_product(
                tuple(plan), meta, gated, hiddens, weight, sibling_weight, n_ex, top
            )
            for item, part in zip(items, made):
                parts[item] = part
            for d in sorted(scaled):
                scaleds.append(scaled[d])
                for (off, e), (where, place, _, _) in zip(items, plan):
                    if e == d:
                        if not any(used[where] is other for other in refs):
                            refs.append(used[where])
                        layout.append(([used[where] is other for other in refs].index(True), place))
                if d == 0:
                    own_back.append(back[0])
                    facts.append(fact)
                else:
                    sent_back[d - 1].append(shift(back[d], -d))
            return made[0]

        near = offsets[: 2 * min(2, half - 1) + 1]
        for step in range(1, half):
            sent = blocks[1 - step][0], blocks[step - 1][0]
            if step == 2:
                sent = after(sent[0], *seeds[1:]), after(sent[1], *seeds[1:])
            if step > 2:
                gate = blocks[2 - step][1], blocks[step - 2][1]
                sent = after(sent[0], *gate), after(sent[1], *gate)
            blocks[-step], blocks[step] = [ring_send(sent[0], 1)], [ring_send(sent[1], -1)]
            blocks[-step].append(ring_send(blocks[1 - step][1], 1))
            blocks[step].append(ring_send(blocks[step - 1][1], -1))
            if step == 1:
                for d in range(1, n_dp):
                    value = shift(after(hidden, *seeds[1:], blocks[-1][0], blocks[1][0]), d)
                    hiddens.append((value, None))
            if step == min(2, half - 1):
                ready = work([(off, 0) for off in near])
        gate = blocks[2 - half][1], blocks[half - 2][1], ready
        blocks[half] = [
            ring_send(after(blocks[1 - half][0], *gate), 1),
            ring_send(after(blocks[half - 1][1], ready), -1),
        ]
        for d in range(1, n_dp):
            value = hiddens[d][0]
            hiddens[d] = value, swap(after(value, *gate, blocks[1 - half][0], blocks[half - 1][0]))
        later = [[(off, d) for off in near for d in range(1, n_dp)]]
        later.append([(off, d) for off in offsets for d in range(n_dp) if off not in near])
        for items in later:
            for at in range(0, len(items), 12):
                ready = work(sorted(items[at : at + 12], key=lambda item: item[1]), ready)

        carry = {}

        def hop_on(hop, *done):
            every = range(n_dp)
            if hop == half:
                values = [jnp.stack([parts[half, d] for d in every[:per]])]
                values.append(jnp.stack([parts[half, d] for d in every[per:]]))
            else:
                first, last = ((0, per), (per, n_dp)) if hop == half - 1 else ((0, n_dp), (0, n_dp))
                values = sums(
                    [
                        ([parts[hop, d] for d in every], carry[1], *first),
                        ([parts[-hop, d] for d in every], carry[-1], *last),
                    ]
                )
            values = [after(value, *done) for value in values]
            carry[1] = ring_send(values[0], 1)
            carry[-1] = ring_send(values[1], -1)
            sending[:] = values
            return carry[1], carry[-1]

        sending = []
        hop_on(half)
        second = hop_on(half - 1)
        other = weight_product(
            [after(refs[0], *sending, *[value for sent in sent_back for value in sent[:-1]])] + refs[1:], layout, scaleds, 1, jnp.bfloat16, width
        )
        swapped = swap(after(other, *second))
        third = hop_on(half - 2, other, *[sent[-1] for sent in sent_back])
        spread, spread_other = spread_product(
            [after(facts[0][0], *second)] + [fact[0] for fact in facts[1:]],
            [fact[1] for fact in facts],
            [own_back] + sent_back,
            slots,
        )
        hidden_grad = spread + swap(spread_other)
        hidden_grad = hidden_grad.reshape(cap, n_ex, ff).transpose(1, 0, 2)[None, None]
        for hop in range(half - 3, 0, -1):
            hop_on(hop, spread)
        weight_grad = weight_product(
            [after(refs[0], *third)] + refs[1:], layout, scaleds, 0, jnp.float32, width, swapped
        )
        totals = close([after(parts[0, 0], weight_grad)] + [parts[0, d] for d in range(1, n_dp)], carry[1], carry[-1])
        pieces = [totals[0]] + [shift(totals[d], -d) for d in range(1, n_dp)]
        layer_out, prob_grad = home(where, expert_ids, pieces, width, n_ex)
        return (layer_out, prob_grad, hidden_grad, weight_grad[None])

    return shards


def solution(mesh):
    placed = (
        P(("dp", "expert"), None),
        P(("dp", "expert"), None),
        P("dp", "expert", None, None, None),
        P("expert", None, "dp"),
        P(("dp", "expert"), None),
    )
    return jax.shard_map(
        body(chip_ring(mesh)),
        mesh=mesh,
        in_specs=placed,
        out_specs=(
            P(("dp", "expert"), None),
            P(("dp", "expert"), None),
            P("dp", "expert", None, None, None),
            P("expert", None, "dp"),
        ),
        check_vma=False,
    )
```

```python
import functools

import jax
import jax.numpy as jnp
import numpy as np
from jax import lax
from jax.experimental import pallas as pl
from jax.experimental.pallas import tpu as pltpu
from jax.sharding import PartitionSpec as P

MIB = 1024 * 1024


def kernel_memory(rows):
    return pltpu.CompilerParams(vmem_limit_bytes=(20 if rows <= 1024 else 48) * MIB)


def dot(a, b, ca, cb):
    return lax.dot_general(a, b, (((ca,), (cb,)), ((), ())), preferred_element_type=jnp.float32)


def after(value, *done):
    return lax.optimization_barrier((value, *done))[0]


def chip_ring(mesh):
    chips = mesh.shape["expert"] // 2
    devices = mesh.devices.reshape(mesh.shape["dp"], -1)
    if not hasattr(devices[0, 0], "coords"):
        return list(range(chips))
    at = [tuple(devices[0, 2 * chip].coords)[1:] for chip in range(chips)]
    rows = max(z for _, z in at) + 1
    cols = max(y for y, _ in at) + 1
    if rows * cols != chips or rows % 2:
        return list(range(chips))
    walk = [(0, z) for z in range(rows)]
    for step, z in enumerate(reversed(range(rows))):
        span = range(1, cols)
        walk += [(y, z) for y in (span if step % 2 == 0 else reversed(span))]
    return [at.index(place) for place in walk]


def pack_kernel(top, n_out, where, ids_in, probs_in, grads_in, *refs):
    outs, (ids, probs, grads, sems) = refs[:n_out], refs[n_out:]
    copies = [
        pltpu.make_async_copy(source, target, sems.at[i])
        for i, (source, target) in enumerate([(ids_in, ids), (probs_in, probs), (grads_in, grads)])
    ]
    for copy in copies:
        copy.start()
    for copy in copies:
        copy.wait()
    tok = grads.shape[0]
    width = grads.shape[1] // len(outs)
    room = outs[0].shape[1] - width
    row = lax.broadcasted_iota(jnp.int32, (tok, tok), 0)
    col = lax.broadcasted_iota(jnp.int32, (tok, tok), 1)
    same = (row == col).astype(jnp.float32)

    def columns(value):
        return lax.dot_general(
            same,
            value,
            (((1,), (1,)), ((), ())),
            precision=lax.Precision.HIGHEST,
            preferred_element_type=jnp.float32,
        )

    prob = columns(probs[...])
    high = prob.astype(jnp.bfloat16)
    middle = (prob - high.astype(jnp.float32)).astype(jnp.bfloat16)
    low = (prob - high.astype(jnp.float32) - middle.astype(jnp.float32)).astype(jnp.bfloat16)
    named = columns(ids[...].astype(jnp.float32)).astype(jnp.bfloat16)
    blank = jnp.zeros((tok, room - 4 * top), jnp.bfloat16)
    routes = jnp.concatenate([named, high, middle, low, blank], axis=1)
    for d, out in enumerate(outs):
        at = lax.rem(where[0] + d, len(outs)) * width
        out[:, :width] = grads[:, pl.ds(pl.multiple_of(at, 128), width)]
        out[:, width:] = routes


def pack(where, ids, probs, grads, n_dp, room):
    top, tok = ids.shape
    width = grads.shape[1] // n_dp
    vmem = pl.BlockSpec(memory_space=pltpu.VMEM)
    return pl.pallas_call(
        functools.partial(pack_kernel, top, n_dp),
        in_specs=[pl.BlockSpec(memory_space=pltpu.SMEM)] + [pl.BlockSpec(memory_space=pl.ANY)] * 3,
        out_specs=[vmem] * n_dp,
        out_shape=[jax.ShapeDtypeStruct((tok, width + room), jnp.bfloat16)] * n_dp,
        scratch_shapes=[
            pltpu.VMEM(ids.shape, ids.dtype),
            pltpu.VMEM(probs.shape, probs.dtype),
            pltpu.VMEM(grads.shape, grads.dtype),
            pltpu.SemaphoreType.DMA((3,)),
        ],
        compiler_params=kernel_memory(tok),
        name="pack",
    )(where, ids, probs, grads)


def turn_kernel(value, out):
    rows, cols = value.shape
    step = 256
    for i in range(rows // step):
        for j in range(cols // step):
            tile = value[i * step : (i + 1) * step, j * step : (j + 1) * step]
            out[j * step : (j + 1) * step, i * step : (i + 1) * step] = tile.T


def turn(value):
    rows, cols = value.shape
    vmem = pl.BlockSpec(memory_space=pltpu.VMEM)
    return pl.pallas_call(
        turn_kernel,
        in_specs=[vmem],
        out_specs=vmem,
        out_shape=jax.ShapeDtypeStruct((cols, rows), value.dtype),
        compiler_params=kernel_memory(rows),
        cost_estimate=pl.CostEstimate(flops=0, bytes_accessed=4 * rows * cols, transcendentals=0),
        name="turn",
    )(value)


def sum_kernel(starts, n_out, *refs):
    outs = refs[-n_out:]
    at = 0
    for out, (n_rows, arrives) in zip(outs, starts):
        carry = refs[at + n_rows] if arrives else None
        for i in range(n_rows):
            value = refs[at + i][...]
            if carry is not None and arrives[0] <= i < arrives[1]:
                value = value.astype(jnp.float32) + carry[i - arrives[0]].astype(jnp.float32)
            out[i] = value.astype(jnp.bfloat16)
        at += n_rows + (1 if arrives else 0)


def sums(jobs):
    tok, full = jobs[0][0][0].shape
    flat, starts, shapes = [], [], []
    for parts, carry, first, last in jobs:
        flat += list(parts) + [carry]
        starts.append((len(parts), (first, last)))
        shapes.append(jax.ShapeDtypeStruct((len(parts), tok, full), jnp.bfloat16))
    vmem = pl.BlockSpec(memory_space=pltpu.VMEM)
    return pl.pallas_call(
        functools.partial(sum_kernel, tuple(starts), len(shapes)),
        in_specs=[vmem] * len(flat),
        out_specs=[vmem] * len(shapes),
        out_shape=shapes,
        compiler_params=kernel_memory(tok),
        name="sums",
    )(*flat)


def close_kernel(n_dp, *refs):
    parts, (one, two), outs = refs[:n_dp], refs[n_dp : n_dp + 2], refs[n_dp + 2 :]
    for d, out in enumerate(outs):
        value = parts[d][...].astype(jnp.float32) + one[d].astype(jnp.float32)
        out[...] = (value + two[d].astype(jnp.float32)).astype(jnp.bfloat16)


def close(parts, one, two):
    vmem = pl.BlockSpec(memory_space=pltpu.VMEM)
    return pl.pallas_call(
        functools.partial(close_kernel, len(parts)),
        in_specs=[vmem] * (len(parts) + 2),
        out_specs=[vmem] * len(parts),
        out_shape=[jax.ShapeDtypeStruct(part.shape, jnp.bfloat16) for part in parts],
        compiler_params=kernel_memory(parts[0].shape[0]),
        name="close",
    )(*parts, one, two)


def home_kernel(n_ex, where, ids, *refs):
    pieces, (layer, prob) = refs[:-2], refs[-2:]
    n_dp = len(pieces)
    tok, top = ids.shape
    width = layer.shape[1] // n_dp
    inner = jnp.zeros((tok, n_ex), jnp.float32)
    for d, piece in enumerate(pieces):
        at = lax.rem(where[0] + d, n_dp) * width
        layer[:, pl.ds(pl.multiple_of(at, 128), width)] = piece[:, :width]
        more = piece[:, width:].astype(jnp.float32)
        inner = inner + more[:, :n_ex] + more[:, n_ex : 2 * n_ex]
    lane = lax.broadcasted_iota(jnp.int32, (tok, n_ex), 1)
    for k in range(top):
        mine = lane == ids[:, k : k + 1]
        prob[:, k : k + 1] = jnp.sum(jnp.where(mine, inner, 0.0), axis=1, keepdims=True)


def home(where, ids, pieces, width, n_ex):
    tok, top = ids.shape
    vmem = pl.BlockSpec(memory_space=pltpu.VMEM)
    return pl.pallas_call(
        functools.partial(home_kernel, n_ex),
        in_specs=[pl.BlockSpec(memory_space=pltpu.SMEM)] + [vmem] * (1 + len(pieces)),
        out_specs=[vmem] * 2,
        out_shape=[
            jax.ShapeDtypeStruct((tok, len(pieces) * width), jnp.bfloat16),
            jax.ShapeDtypeStruct((tok, top), jnp.float32),
        ],
        compiler_params=kernel_memory(tok),
        name="home",
    )(where, ids, *pieces)


def block_kernel(plan, refs_in, n_dp, n_ex, top, *refs):
    meta = refs[0]
    blocks = refs[1 : 1 + refs_in]
    at = 1 + refs_in
    replicas = sorted({item[2] for item in plan})
    hid = {d: refs[at + 2 * i : at + 2 * i + 2] for i, d in enumerate(replicas)}
    at += 2 * len(replicas)
    weights, turned = refs[at : at + 2], refs[at + 2 : at + 4]
    at += 4
    parts = refs[at : at + len(plan)]
    at += len(plan)
    outs = {d: refs[at + 2 * i : at + 2 * i + 2] for i, d in enumerate(replicas)}
    at += 2 * len(replicas)
    index, prob = refs[at : at + 2] if 0 in replicas else (None, None)

    _, tok, full = blocks[0].shape
    ff, width = weights[0].shape
    slots = hid[replicas[0]][0].shape[0]
    count = len(plan) * tok
    rows = [blocks[where][place] for where, place, _, _ in plan]
    routes = jnp.concatenate([row[:, width:] for row in rows], axis=0).astype(jnp.float32)
    named = routes[:, :top]
    chance = routes[:, top : 2 * top] + routes[:, 2 * top : 3 * top] + routes[:, 3 * top : 4 * top]
    row = lax.broadcasted_iota(jnp.int32, (tok, tok), 0)
    col = lax.broadcasted_iota(jnp.int32, (tok, tok), 1)
    earlier = (col < row).astype(jnp.float32)
    lane = lax.broadcasted_iota(jnp.int32, (tok, slots), 1)
    spans = {d: [i for i, item in enumerate(plan) if item[2] == d] for d in replicas}
    helds, scaleds = [], []
    for x in range(2):
        mine = named == meta[x].astype(jnp.float32)
        here = jnp.sum(jnp.where(mine, chance, 0.0), axis=1, keepdims=True)
        taken = jnp.broadcast_to((here > 0.0).astype(jnp.float32), (count, 128))
        held = []
        for d in replicas:
            picks = []
            for n, i in enumerate(spans[d]):
                span = slice(i * tok, (i + 1) * tok)
                position = dot(earlier, taken[span], 1, 0)[:, :1].astype(jnp.int32)
                slot = jnp.where(here[span] > 0.0, position * n_ex + meta[2 + plan[i][3]], -1)
                picks.append((lane == slot).astype(jnp.bfloat16))
                if d == 0:
                    index[n * tok : (n + 1) * tok, x : x + 1] = slot
                    prob[n * tok : (n + 1) * tok, x : x + 1] = here[span]
            held.append(dot(jnp.concatenate(picks, axis=0), hid[d][x][...], 1, 0))
        held = jnp.concatenate(held, axis=0)
        scaled = (held * here).astype(jnp.bfloat16)
        base = 0
        for d in replicas:
            size = len(spans[d]) * tok
            outs[d][0][x] = scaled[base : base + size]
            base += size
        helds.append(held)
        scaleds.append(scaled)

    tile = 512
    for step in range(width // tile):
        cols = slice(step * tile, (step + 1) * tile)
        value = dot(scaleds[0], weights[0][:, cols], 1, 0) + dot(scaleds[1], weights[1][:, cols], 1, 0)
        value = value.astype(jnp.bfloat16)
        for i, out in enumerate(parts):
            out[:, cols] = value[i * tok : (i + 1) * tok]

    lhs = jnp.concatenate([row[:, :width] for row in rows], axis=0)
    lane = lax.broadcasted_iota(jnp.int32, (count, full - width), 1)
    extra = jnp.zeros((count, full - width), jnp.float32)
    for x in range(2):
        inner = jnp.zeros((count, 1), jnp.float32)
        step_ff = 256
        for step in range(ff // step_ff):
            cols = slice(step * step_ff, (step + 1) * step_ff)
            value = dot(lhs, turned[x][:, cols], 1, 0)
            inner = inner + jnp.sum(value * helds[x][:, cols], axis=1, keepdims=True)
            value = value.astype(jnp.bfloat16)
            base = 0
            for d in replicas:
                size = len(spans[d]) * tok
                outs[d][1][x, :, cols] = value[base : base + size]
                base += size
        high = inner.astype(jnp.bfloat16).astype(jnp.float32)
        extra = jnp.where(lane == meta[x], high, extra)
        extra = jnp.where(lane == meta[x] + n_ex, inner - high, extra)
    extra = extra.astype(jnp.bfloat16)
    for i, out in enumerate(parts):
        out[:, width:] = extra[i * tok : (i + 1) * tok]


def block_product(plan, meta, blocks, hiddens, weights, n_ex, top):
    n_dp = len(hiddens)
    _, tok, full = blocks[0].shape
    ff, width = weights[0].shape
    slots = hiddens[0][0].shape[0]
    replicas = sorted({item[2] for item in plan})
    vmem = pl.BlockSpec(memory_space=pltpu.VMEM)
    bf16 = lambda *shape: jax.ShapeDtypeStruct(shape, jnp.bfloat16)
    out_shape = [bf16(tok, full) for _ in plan]
    sizes = {d: tok * sum(item[2] == d for item in plan) for d in replicas}
    for d in replicas:
        out_shape += [bf16(2, sizes[d], ff)] * 2
    if 0 in replicas:
        out_shape.append(jax.ShapeDtypeStruct((sizes[0], 2), jnp.int32))
        out_shape.append(jax.ShapeDtypeStruct((sizes[0], 2), jnp.float32))
    hid = [value for d in replicas for value in hiddens[d]]
    count = len(plan) * tok
    chips_rows = n_ex * tok * n_dp // 2
    made = pl.pallas_call(
        functools.partial(block_kernel, plan, len(blocks), n_dp, n_ex, top),
        in_specs=[pl.BlockSpec(memory_space=pltpu.SMEM)] + [vmem] * (len(blocks) + len(hid) + 4),
        out_specs=[vmem] * len(out_shape),
        out_shape=out_shape,
        compiler_params=kernel_memory(chips_rows),
        cost_estimate=pl.CostEstimate(
            flops=8 * count * ff * width,
            bytes_accessed=4 * ff * width + 4 * count * (full + ff),
            transcendentals=0,
        ),
        name="block_product",
    )(meta, *blocks, *hid, *weights)
    parts = made[: len(plan)]
    rest = made[len(plan) :]
    scaled = {d: rest[2 * i] for i, d in enumerate(replicas)}
    back = {d: rest[2 * i + 1] for i, d in enumerate(replicas)}
    return parts, scaled, back, rest[2 * len(replicas) :]


def spread_kernel(sizes, *refs):
    n_parts = len(sizes[0])
    index, prob = refs[:n_parts], refs[n_parts : 2 * n_parts]
    backs = list(refs[2 * n_parts : -2])
    outs = refs[-2:]
    slots = outs[0].shape[0]
    slot = jnp.concatenate([ref[...] for ref in index], axis=0)
    weight = jnp.concatenate([ref[...] for ref in prob], axis=0)
    lane = lax.broadcasted_iota(jnp.int32, (slot.shape[0], slots), 1)
    for x, out in enumerate(outs):
        back, at = None, 0
        for pieces in sizes:
            value = jnp.concatenate([ref[x] for ref in backs[at : at + len(pieces)]], axis=0)
            at += len(pieces)
            value = value.astype(jnp.float32)
            back = value if back is None else back + value
        pick = (lane == slot[:, x : x + 1]).astype(jnp.bfloat16)
        mine = (back * weight[:, x : x + 1]).astype(jnp.bfloat16)
        out[...] = dot(pick, mine, 0, 0).astype(jnp.bfloat16)


def spread_product(index, prob, backs, slots):
    sizes = [[part.shape[1] for part in parts] for parts in backs]
    ff = backs[0][0].shape[2]
    rows = sum(sizes[0])
    flat = [part for parts in backs for part in parts]
    vmem = pl.BlockSpec(memory_space=pltpu.VMEM)
    return pl.pallas_call(
        functools.partial(spread_kernel, sizes),
        in_specs=[vmem] * (2 * len(index) + len(flat)),
        out_specs=[vmem] * 2,
        out_shape=[jax.ShapeDtypeStruct((slots, ff), jnp.bfloat16)] * 2,
        compiler_params=kernel_memory(rows * len(backs)),
        cost_estimate=pl.CostEstimate(
            flops=4 * rows * slots * ff,
            bytes_accessed=4 * (1 + len(backs)) * rows * ff,
            transcendentals=0,
        ),
        name="spread_product",
    )(*index, *prob, *flat)


def weight_kernel(n_refs, n_scaled, layout, *refs):
    blocks, scaleds, more = refs[:n_refs], refs[n_refs : n_refs + n_scaled], refs[n_refs + n_scaled : -2]
    out, turned = refs[-2:]

    @pl.when(pl.program_id(0) == 0)
    def _():
        turned[...] = jnp.concatenate([ref[0] for ref in scaleds], axis=0).T

    rows = jnp.concatenate([blocks[where][place] for where, place in layout], axis=0)
    total = dot(turned[...], rows, 1, 0)
    for ref in more:
        total = total + ref[...].astype(jnp.float32)
    out[...] = total.astype(out.dtype)


def weight_product(blocks, layout, scaleds, x, dtype, width, *more):
    tok = blocks[0].shape[1]
    ff = scaleds[0].shape[2]
    rows = len(layout) * tok
    tile = 512 if width >= 2048 else 256
    return pl.pallas_call(
        functools.partial(weight_kernel, len(blocks), len(scaleds), layout),
        grid=(width // tile,),
        in_specs=[pl.BlockSpec(block.shape[:2] + (tile,), lambda i: (0, 0, i)) for block in blocks]
        + [
            pl.BlockSpec((1,) + value.shape[1:], lambda i: (x, 0, 0), pipeline_mode=pl.Buffered(1))
            for value in scaleds
        ]
        + [pl.BlockSpec((ff, tile), lambda i: (0, i)) for _ in more],
        out_specs=pl.BlockSpec((ff, tile), lambda i: (0, i)),
        out_shape=jax.ShapeDtypeStruct((ff, width), dtype),
        scratch_shapes=[pltpu.VMEM((ff, rows), jnp.bfloat16)],
        compiler_params=kernel_memory(rows),
        cost_estimate=pl.CostEstimate(
            flops=2 * rows * width * ff,
            bytes_accessed=2 * rows * (width + ff) + 4 * ff * width,
            transcendentals=0,
        ),
        name="weight_product",
    )(*blocks, *scaleds, *more)


def body(ring):
    chips = len(ring)
    half = chips // 2
    offsets = [0]
    for step in range(1, half):
        offsets += [-step, step]
    offsets.append(half)
    place_of = {chip: at for at, chip in enumerate(ring)}
    meta_table = np.asarray(
        [
            [e, e ^ 1] + [2 * ring[(place_of[e // 2] + off) % chips] + e % 2 for off in offsets]
            for e in range(2 * chips)
        ],
        np.int32,
    )

    def along(step):
        return [
            (2 * ring[at] + core, 2 * ring[(at + step) % chips] + core)
            for at in range(chips)
            for core in range(2)
        ]

    forward, backward = along(1), along(-1)
    sibling = [(e, e ^ 1) for e in range(2 * chips)]

    def shards(expert_ids, route_probs, expert_hidden, down_weight, out_grad):
        tok, top = expert_ids.shape
        n_dp = lax.axis_size("dp")
        n_ex = lax.axis_size("expert")
        cap = expert_hidden.shape[3]
        slots = cap * n_ex
        ff = down_weight.shape[1]
        width = down_weight.shape[2]
        weight = down_weight[0]
        replica = lax.axis_index("dp")
        expert = lax.axis_index("expert")
        per = n_dp // 2
        meta = lax.dynamic_index_in_dim(jnp.asarray(meta_table), expert, 0, keepdims=False)

        def shift(value, step):
            return lax.ppermute(value, "dp", [(i, (i + step) % n_dp) for i in range(n_dp)])

        def ring_send(value, step):
            return lax.ppermute(value, "expert", forward if step > 0 else backward)

        def swap(value):
            return lax.ppermute(value, "expert", sibling)

        room = 128 * -(-max(4 * top, 2 * n_ex) // 128)
        where = replica.reshape(1).astype(jnp.int32)
        packed = pack(where, expert_ids.T, route_probs.T, out_grad, n_dp, room)
        blocks = {0: jnp.stack([packed[0]] + [shift(packed[d], d) for d in range(1, n_dp)])}

        sibling_weight = swap(weight)
        weights = [weight, sibling_weight, turn(weight), turn(sibling_weight)]
        hidden = expert_hidden[0, 0].transpose(1, 0, 2).reshape(slots, ff)
        hiddens = [(hidden, swap(hidden))]
        for d in range(1, n_dp):
            value = shift(after(hidden, blocks[0]), d)
            hiddens.append((value, None))

        parts, scaleds, layout, facts = {}, [], [], []
        own_back, sent_back = [], [[] for _ in range(1, n_dp)]
        refs = []

        def work(items, *done):
            used, plan = [], []
            for off, d in items:
                value = blocks[off][d // per] if off == half else blocks[off]
                if not any(value is other for other in used):
                    used.append(value)
                where = [value is other for other in used].index(True)
                plan.append((where, d % per if off == half else d, d, offsets.index(off)))
            if done:
                gated = [after(used[0], *done)] + used[1:]
            else:
                gated = used
            made, scaled, back, fact = block_product(
                tuple(plan), meta, gated, hiddens, weights, n_ex, top
            )
            for item, part in zip(items, made):
                parts[item] = part
            for d in sorted(scaled):
                scaleds.append(scaled[d])
                for (off, e), (where, place, _, _) in zip(items, plan):
                    if e == d:
                        if not any(used[where] is other for other in refs):
                            refs.append(used[where])
                        layout.append(([used[where] is other for other in refs].index(True), place))
                if d == 0:
                    own_back.append(back[0])
                    facts.append(fact)
                else:
                    sent_back[d - 1].append(shift(back[d], -d))
            return made[0]

        both = lambda offs: [(off, d) for d in range(n_dp) for off in offs]
        gate = tuple(weights[2:])
        for step in range(1, half):
            sent = blocks[1 - step], blocks[step - 1]
            if step > 1:
                sent = after(sent[0], *gate), after(sent[1], *gate)
            blocks[-step] = ring_send(sent[0], 1)
            blocks[step] = ring_send(sent[1], -1)
            if step == 1:
                following = [(off, 0) for off in offsets[:3]]
            elif step == 2:
                following = [(off, d) for d in range(n_dp) for off in offsets[:5] if d > 0 or off not in offsets[:3]]
            else:
                following = both([-step, step])
            if step == half - 1:
                break
            if step > 1:
                gate = (ready,)
            if step == 2:
                for d in range(1, n_dp):
                    value = hiddens[d][0]
                    hiddens[d] = value, swap(after(value, blocks[-step], blocks[step], ready))
            ready = work(following)
        sent = after(blocks[1 - half], ready)[:per], after(blocks[half - 1], ready)[per:]
        blocks[half] = [ring_send(sent[0], 1), ring_send(sent[1], -1)]
        ready = work(following)
        work(both([half]), ready)

        carry = {}

        def hop_on(hop, *done):
            every = range(n_dp)
            if hop == half:
                values = [jnp.stack([parts[half, d] for d in every[:per]])]
                values.append(jnp.stack([parts[half, d] for d in every[per:]]))
            else:
                first, last = ((0, per), (per, n_dp)) if hop == half - 1 else ((0, n_dp), (0, n_dp))
                values = sums([([parts[hop, d] for d in every], carry[1], *first)])
                values += sums([([parts[-hop, d] for d in every], carry[-1], *last)])
            values = [after(value, *done) for value in values]
            carry[1] = ring_send(values[0], 1)
            carry[-1] = ring_send(values[1], -1)
            sending[:] = values
            return carry[1], carry[-1]

        sending = []
        hop_on(half)
        second = hop_on(half - 1)
        other = weight_product(
            [after(refs[0], *sending, *[value for sent in sent_back for value in sent])] + refs[1:], layout, scaleds, 1, jnp.bfloat16, width
        )
        swapped = swap(after(other, *second))
        third = hop_on(half - 2, other)
        spread, spread_other = spread_product(
            [after(facts[0][0], *second)] + [fact[0] for fact in facts[1:]],
            [fact[1] for fact in facts],
            [own_back] + sent_back,
            slots,
        )
        hidden_grad = spread + swap(spread_other)
        hidden_grad = hidden_grad.reshape(cap, n_ex, ff).transpose(1, 0, 2)[None, None]
        for hop in range(half - 3, 0, -1):
            hop_on(hop, spread)
        weight_grad = weight_product(
            [after(refs[0], *third)] + refs[1:], layout, scaleds, 0, jnp.float32, width, swapped
        )
        totals = close([after(parts[0, 0], weight_grad)] + [parts[0, d] for d in range(1, n_dp)], carry[1], carry[-1])
        pieces = [totals[0]] + [shift(totals[d], -d) for d in range(1, n_dp)]
        layer_out, prob_grad = home(where, expert_ids, pieces, width, n_ex)
        return (layer_out, prob_grad, hidden_grad, weight_grad[None])

    return shards


def solution(mesh):
    placed = (
        P(("dp", "expert"), None),
        P(("dp", "expert"), None),
        P("dp", "expert", None, None, None),
        P("expert", None, "dp"),
        P(("dp", "expert"), None),
    )
    return jax.shard_map(
        body(chip_ring(mesh)),
        mesh=mesh,
        in_specs=placed,
        out_specs=(
            P(("dp", "expert"), None),
            P(("dp", "expert"), None),
            P("dp", "expert", None, None, None),
            P("expert", None, "dp"),
        ),
        check_vma=False,
    )
```

```python
import functools

import jax
import jax.numpy as jnp
import numpy as np
from jax import lax
from jax.experimental import pallas as pl
from jax.experimental.pallas import tpu as pltpu
from jax.sharding import PartitionSpec as P

MIB = 1024 * 1024


def kernel_memory(rows):
    return pltpu.CompilerParams(vmem_limit_bytes=(20 if rows <= 1024 else 48) * MIB)


def dot(a, b, ca, cb):
    return lax.dot_general(a, b, (((ca,), (cb,)), ((), ())), preferred_element_type=jnp.float32)


def after(value, *done):
    return lax.optimization_barrier((value, *done))[0]


def chip_ring(mesh):
    chips = mesh.shape["expert"] // 2
    devices = mesh.devices.reshape(mesh.shape["dp"], -1)
    if not hasattr(devices[0, 0], "coords"):
        return list(range(chips))
    at = [tuple(devices[0, 2 * chip].coords)[1:] for chip in range(chips)]
    rows = max(z for _, z in at) + 1
    cols = max(y for y, _ in at) + 1
    if rows * cols != chips or rows % 2:
        return list(range(chips))
    walk = [(0, z) for z in range(rows)]
    for step, z in enumerate(reversed(range(rows))):
        span = range(1, cols)
        walk += [(y, z) for y in (span if step % 2 == 0 else reversed(span))]
    return [at.index(place) for place in walk]


def pack_kernel(top, n_out, where, ids_in, probs_in, grads_in, *refs):
    outs, (ids, probs, grads, sems) = refs[:n_out], refs[n_out:]
    copies = [
        pltpu.make_async_copy(source, target, sems.at[i])
        for i, (source, target) in enumerate([(ids_in, ids), (probs_in, probs), (grads_in, grads)])
    ]
    for copy in copies:
        copy.start()
    for copy in copies:
        copy.wait()
    tok = grads.shape[0]
    width = grads.shape[1] // len(outs)
    room = outs[0].shape[1] - width
    row = lax.broadcasted_iota(jnp.int32, (tok, tok), 0)
    col = lax.broadcasted_iota(jnp.int32, (tok, tok), 1)
    same = (row == col).astype(jnp.float32)

    def columns(value):
        return lax.dot_general(
            same,
            value,
            (((1,), (1,)), ((), ())),
            precision=lax.Precision.HIGHEST,
            preferred_element_type=jnp.float32,
        )

    prob = columns(probs[...])
    high = prob.astype(jnp.bfloat16)
    middle = (prob - high.astype(jnp.float32)).astype(jnp.bfloat16)
    low = (prob - high.astype(jnp.float32) - middle.astype(jnp.float32)).astype(jnp.bfloat16)
    named = columns(ids[...].astype(jnp.float32)).astype(jnp.bfloat16)
    blank = jnp.zeros((tok, room - 4 * top), jnp.bfloat16)
    routes = jnp.concatenate([named, high, middle, low, blank], axis=1)
    for d, out in enumerate(outs):
        at = lax.rem(where[0] + d, len(outs)) * width
        out[:, :width] = grads[:, pl.ds(pl.multiple_of(at, 128), width)]
        out[:, width:] = routes


def pack(where, ids, probs, grads, n_dp, room):
    top, tok = ids.shape
    width = grads.shape[1] // n_dp
    vmem = pl.BlockSpec(memory_space=pltpu.VMEM)
    return pl.pallas_call(
        functools.partial(pack_kernel, top, n_dp),
        in_specs=[pl.BlockSpec(memory_space=pltpu.SMEM)] + [pl.BlockSpec(memory_space=pltpu.HBM)] * 3,
        out_specs=[vmem] * n_dp,
        out_shape=[jax.ShapeDtypeStruct((tok, width + room), jnp.bfloat16)] * n_dp,
        scratch_shapes=[
            pltpu.VMEM(ids.shape, ids.dtype),
            pltpu.VMEM(probs.shape, probs.dtype),
            pltpu.VMEM(grads.shape, grads.dtype),
            pltpu.SemaphoreType.DMA((3,)),
        ],
        compiler_params=kernel_memory(tok),
        name="pack",
    )(where, ids, probs, grads)


def sum_kernel(starts, n_out, *refs):
    outs = refs[-n_out:]
    at = 0
    for out, (n_rows, arrives) in zip(outs, starts):
        carry = refs[at + n_rows] if arrives else None
        for i in range(n_rows):
            value = refs[at + i][...]
            if carry is not None and arrives[0] <= i < arrives[1]:
                value = value.astype(jnp.float32) + carry[i - arrives[0]].astype(jnp.float32)
            out[i] = value.astype(jnp.bfloat16)
        at += n_rows + (1 if arrives else 0)


def sums(jobs):
    tok, full = jobs[0][0][0].shape
    flat, starts, shapes = [], [], []
    for parts, carry, first, last in jobs:
        flat += list(parts) + [carry]
        starts.append((len(parts), (first, last)))
        shapes.append(jax.ShapeDtypeStruct((len(parts), tok, full), jnp.bfloat16))
    vmem = pl.BlockSpec(memory_space=pltpu.VMEM)
    return pl.pallas_call(
        functools.partial(sum_kernel, tuple(starts), len(shapes)),
        in_specs=[vmem] * len(flat),
        out_specs=[vmem] * len(shapes),
        out_shape=shapes,
        compiler_params=kernel_memory(tok),
        name="sums",
    )(*flat)


def close_kernel(n_dp, *refs):
    parts, (one, two), outs = refs[:n_dp], refs[n_dp : n_dp + 2], refs[n_dp + 2 :]
    for d, out in enumerate(outs):
        value = parts[d][...].astype(jnp.float32) + one[d].astype(jnp.float32)
        out[...] = (value + two[d].astype(jnp.float32)).astype(jnp.bfloat16)


def close(parts, one, two):
    vmem = pl.BlockSpec(memory_space=pltpu.VMEM)
    return pl.pallas_call(
        functools.partial(close_kernel, len(parts)),
        in_specs=[vmem] * (len(parts) + 2),
        out_specs=[vmem] * len(parts),
        out_shape=[jax.ShapeDtypeStruct(part.shape, jnp.bfloat16) for part in parts],
        compiler_params=kernel_memory(parts[0].shape[0]),
        name="close",
    )(*parts, one, two)


def home_kernel(n_ex, where, ids, *refs):
    pieces, (layer, prob) = refs[:-2], refs[-2:]
    n_dp = len(pieces)
    tok, top = ids.shape
    width = layer.shape[1] // n_dp
    inner = jnp.zeros((tok, n_ex), jnp.float32)
    for d, piece in enumerate(pieces):
        at = lax.rem(where[0] + d, n_dp) * width
        layer[:, pl.ds(pl.multiple_of(at, 128), width)] = piece[:, :width]
        more = piece[:, width:].astype(jnp.float32)
        inner = inner + more[:, :n_ex] + more[:, n_ex : 2 * n_ex]
    lane = lax.broadcasted_iota(jnp.int32, (tok, n_ex), 1)
    for k in range(top):
        mine = lane == ids[:, k : k + 1]
        prob[:, k : k + 1] = jnp.sum(jnp.where(mine, inner, 0.0), axis=1, keepdims=True)


def home(where, ids, pieces, width, n_ex):
    tok, top = ids.shape
    vmem = pl.BlockSpec(memory_space=pltpu.VMEM)
    return pl.pallas_call(
        functools.partial(home_kernel, n_ex),
        in_specs=[pl.BlockSpec(memory_space=pltpu.SMEM)] + [vmem] * (1 + len(pieces)),
        out_specs=[vmem] * 2,
        out_shape=[
            jax.ShapeDtypeStruct((tok, len(pieces) * width), jnp.bfloat16),
            jax.ShapeDtypeStruct((tok, top), jnp.float32),
        ],
        compiler_params=kernel_memory(tok),
        name="home",
    )(where, ids, *pieces)


def block_kernel(plan, refs_in, n_dp, n_ex, top, *refs):
    meta = refs[0]
    blocks = refs[1 : 1 + refs_in]
    at = 1 + refs_in
    replicas = sorted({item[2] for item in plan})
    hid = {d: refs[at + 2 * i : at + 2 * i + 2] for i, d in enumerate(replicas)}
    at += 2 * len(replicas)
    weights = refs[at : at + 2]
    at += 2
    parts = refs[at : at + len(plan)]
    at += len(plan)
    outs = {d: refs[at + 2 * i : at + 2 * i + 2] for i, d in enumerate(replicas)}
    at += 2 * len(replicas)
    index, prob = refs[at : at + 2] if 0 in replicas else (None, None)

    _, tok, full = blocks[0].shape
    ff, width = weights[0].shape
    slots = hid[replicas[0]][0].shape[0]
    count = len(plan) * tok
    rows = [blocks[where][place] for where, place, _, _ in plan]
    routes = jnp.concatenate([row[:, width:] for row in rows], axis=0).astype(jnp.float32)
    named = routes[:, :top]
    chance = routes[:, top : 2 * top] + routes[:, 2 * top : 3 * top] + routes[:, 3 * top : 4 * top]
    row = lax.broadcasted_iota(jnp.int32, (tok, tok), 0)
    col = lax.broadcasted_iota(jnp.int32, (tok, tok), 1)
    earlier = (col < row).astype(jnp.float32)
    lane = lax.broadcasted_iota(jnp.int32, (tok, slots), 1)
    spans = {d: [i for i, item in enumerate(plan) if item[2] == d] for d in replicas}
    helds, scaleds = [], []
    for x in range(2):
        mine = named == meta[x].astype(jnp.float32)
        here = jnp.sum(jnp.where(mine, chance, 0.0), axis=1, keepdims=True)
        taken = jnp.broadcast_to((here > 0.0).astype(jnp.float32), (count, 128))
        held = []
        for d in replicas:
            picks = []
            for n, i in enumerate(spans[d]):
                span = slice(i * tok, (i + 1) * tok)
                position = dot(earlier, taken[span], 1, 0)[:, :1].astype(jnp.int32)
                slot = jnp.where(here[span] > 0.0, position * n_ex + meta[2 + plan[i][3]], -1)
                picks.append((lane == slot).astype(jnp.bfloat16))
                if d == 0:
                    index[n * tok : (n + 1) * tok, x : x + 1] = slot
                    prob[n * tok : (n + 1) * tok, x : x + 1] = here[span]
            held.append(dot(jnp.concatenate(picks, axis=0), hid[d][x][...], 1, 0))
        held = jnp.concatenate(held, axis=0)
        scaled = (held * here).astype(jnp.bfloat16)
        base = 0
        for d in replicas:
            size = len(spans[d]) * tok
            outs[d][0][x] = scaled[base : base + size]
            base += size
        helds.append(held)
        scaleds.append(scaled)

    tile = 512
    for step in range(width // tile):
        cols = slice(step * tile, (step + 1) * tile)
        value = dot(scaleds[0], weights[0][:, cols], 1, 0) + dot(scaleds[1], weights[1][:, cols], 1, 0)
        value = value.astype(jnp.bfloat16)
        for i, out in enumerate(parts):
            out[:, cols] = value[i * tok : (i + 1) * tok]

    lhs = jnp.concatenate([row[:, :width] for row in rows], axis=0)
    lane = lax.broadcasted_iota(jnp.int32, (count, full - width), 1)
    extra = jnp.zeros((count, full - width), jnp.float32)
    for x in range(2):
        inner = jnp.zeros((count, 1), jnp.float32)
        step_ff = 256
        for step in range(ff // step_ff):
            cols = slice(step * step_ff, (step + 1) * step_ff)
            value = dot(lhs, weights[x][cols, :], 1, 1)
            inner = inner + jnp.sum(value * helds[x][:, cols], axis=1, keepdims=True)
            value = value.astype(jnp.bfloat16)
            base = 0
            for d in replicas:
                size = len(spans[d]) * tok
                outs[d][1][x, :, cols] = value[base : base + size]
                base += size
        high = inner.astype(jnp.bfloat16).astype(jnp.float32)
        extra = jnp.where(lane == meta[x], high, extra)
        extra = jnp.where(lane == meta[x] + n_ex, inner - high, extra)
    extra = extra.astype(jnp.bfloat16)
    for i, out in enumerate(parts):
        out[:, width:] = extra[i * tok : (i + 1) * tok]


def block_product(plan, meta, blocks, hiddens, w_own, w_sib, n_ex, top):
    n_dp = len(hiddens)
    _, tok, full = blocks[0].shape
    ff, width = w_own.shape
    slots = hiddens[0][0].shape[0]
    replicas = sorted({item[2] for item in plan})
    vmem = pl.BlockSpec(memory_space=pltpu.VMEM)
    bf16 = lambda *shape: jax.ShapeDtypeStruct(shape, jnp.bfloat16)
    out_shape = [bf16(tok, full) for _ in plan]
    sizes = {d: tok * sum(item[2] == d for item in plan) for d in replicas}
    for d in replicas:
        out_shape += [bf16(2, sizes[d], ff)] * 2
    if 0 in replicas:
        out_shape.append(jax.ShapeDtypeStruct((sizes[0], 2), jnp.int32))
        out_shape.append(jax.ShapeDtypeStruct((sizes[0], 2), jnp.float32))
    hid = [value for d in replicas for value in hiddens[d]]
    count = len(plan) * tok
    chips_rows = n_ex * tok * n_dp // 2
    made = pl.pallas_call(
        functools.partial(block_kernel, plan, len(blocks), n_dp, n_ex, top),
        in_specs=[pl.BlockSpec(memory_space=pltpu.SMEM)] + [vmem] * (len(blocks) + len(hid) + 2),
        out_specs=[vmem] * len(out_shape),
        out_shape=out_shape,
        compiler_params=kernel_memory(chips_rows),
        cost_estimate=pl.CostEstimate(
            flops=8 * count * ff * width,
            bytes_accessed=4 * ff * width + 4 * count * (full + ff),
            transcendentals=0,
        ),
        name="block_product",
    )(meta, *blocks, *hid, w_own, w_sib)
    parts = made[: len(plan)]
    rest = made[len(plan) :]
    scaled = {d: rest[2 * i] for i, d in enumerate(replicas)}
    back = {d: rest[2 * i + 1] for i, d in enumerate(replicas)}
    return parts, scaled, back, rest[2 * len(replicas) :]


def spread_kernel(sizes, *refs):
    n_parts = len(sizes[0])
    index, prob = refs[:n_parts], refs[n_parts : 2 * n_parts]
    backs = list(refs[2 * n_parts : -2])
    outs = refs[-2:]
    slots = outs[0].shape[0]
    slot = jnp.concatenate([ref[...] for ref in index], axis=0)
    weight = jnp.concatenate([ref[...] for ref in prob], axis=0)
    lane = lax.broadcasted_iota(jnp.int32, (slot.shape[0], slots), 1)
    for x, out in enumerate(outs):
        back, at = None, 0
        for pieces in sizes:
            value = jnp.concatenate([ref[x] for ref in backs[at : at + len(pieces)]], axis=0)
            at += len(pieces)
            value = value.astype(jnp.float32)
            back = value if back is None else back + value
        pick = (lane == slot[:, x : x + 1]).astype(jnp.bfloat16)
        mine = (back * weight[:, x : x + 1]).astype(jnp.bfloat16)
        out[...] = dot(pick, mine, 0, 0).astype(jnp.bfloat16)


def spread_product(index, prob, backs, slots):
    sizes = [[part.shape[1] for part in parts] for parts in backs]
    ff = backs[0][0].shape[2]
    rows = sum(sizes[0])
    flat = [part for parts in backs for part in parts]
    vmem = pl.BlockSpec(memory_space=pltpu.VMEM)
    return pl.pallas_call(
        functools.partial(spread_kernel, sizes),
        in_specs=[vmem] * (2 * len(index) + len(flat)),
        out_specs=[vmem] * 2,
        out_shape=[jax.ShapeDtypeStruct((slots, ff), jnp.bfloat16)] * 2,
        compiler_params=kernel_memory(rows * len(backs)),
        cost_estimate=pl.CostEstimate(
            flops=4 * rows * slots * ff,
            bytes_accessed=4 * (1 + len(backs)) * rows * ff,
            transcendentals=0,
        ),
        name="spread_product",
    )(*index, *prob, *flat)


def weight_kernel(n_refs, n_scaled, layout, *refs):
    blocks, scaleds, more = refs[:n_refs], refs[n_refs : n_refs + n_scaled], refs[n_refs + n_scaled : -2]
    out, turned = refs[-2:]

    @pl.when(pl.program_id(0) == 0)
    def _():
        turned[...] = jnp.concatenate([ref[0] for ref in scaleds], axis=0).T

    rows = jnp.concatenate([blocks[where][place] for where, place in layout], axis=0)
    total = dot(turned[...], rows, 1, 0)
    for ref in more:
        total = total + ref[...].astype(jnp.float32)
    out[...] = total.astype(out.dtype)


def weight_product(blocks, layout, scaleds, x, dtype, width, *more):
    tok = blocks[0].shape[1]
    ff = scaleds[0].shape[2]
    rows = len(layout) * tok
    tile = 512 if width >= 2048 else 256
    return pl.pallas_call(
        functools.partial(weight_kernel, len(blocks), len(scaleds), layout),
        grid=(width // tile,),
        in_specs=[pl.BlockSpec(block.shape[:2] + (tile,), lambda i: (0, 0, i)) for block in blocks]
        + [
            pl.BlockSpec((1,) + value.shape[1:], lambda i: (x, 0, 0), pipeline_mode=pl.Buffered(1))
            for value in scaleds
        ]
        + [pl.BlockSpec((ff, tile), lambda i: (0, i)) for _ in more],
        out_specs=pl.BlockSpec((ff, tile), lambda i: (0, i)),
        out_shape=jax.ShapeDtypeStruct((ff, width), dtype),
        scratch_shapes=[pltpu.VMEM((ff, rows), jnp.bfloat16)],
        compiler_params=kernel_memory(rows),
        cost_estimate=pl.CostEstimate(
            flops=2 * rows * width * ff,
            bytes_accessed=2 * rows * (width + ff) + 4 * ff * width,
            transcendentals=0,
        ),
        name="weight_product",
    )(*blocks, *scaleds, *more)


def body(ring):
    chips = len(ring)
    half = chips // 2
    offsets = [0]
    for step in range(1, half):
        offsets += [-step, step]
    offsets.append(half)
    place_of = {chip: at for at, chip in enumerate(ring)}
    meta_table = np.asarray(
        [
            [e, e ^ 1] + [2 * ring[(place_of[e // 2] + off) % chips] + e % 2 for off in offsets]
            for e in range(2 * chips)
        ],
        np.int32,
    )

    def along(step):
        return [
            (2 * ring[at] + core, 2 * ring[(at + step) % chips] + core)
            for at in range(chips)
            for core in range(2)
        ]

    forward, backward = along(1), along(-1)
    sibling = [(e, e ^ 1) for e in range(2 * chips)]

    def shards(expert_ids, route_probs, expert_hidden, down_weight, out_grad):
        tok, top = expert_ids.shape
        n_dp = lax.axis_size("dp")
        n_ex = lax.axis_size("expert")
        cap = expert_hidden.shape[3]
        slots = cap * n_ex
        ff = down_weight.shape[1]
        width = down_weight.shape[2]
        weight = down_weight[0]
        replica = lax.axis_index("dp")
        expert = lax.axis_index("expert")
        per = n_dp // 2
        meta = lax.dynamic_index_in_dim(jnp.asarray(meta_table), expert, 0, keepdims=False)

        def shift(value, step):
            return lax.ppermute(value, "dp", [(i, (i + step) % n_dp) for i in range(n_dp)])

        def ring_send(value, step):
            return lax.ppermute(value, "expert", forward if step > 0 else backward)

        def swap(value):
            return lax.ppermute(value, "expert", sibling)

        room = 128 * -(-max(4 * top, 2 * n_ex) // 128)
        where = replica.reshape(1).astype(jnp.int32)
        packed = pack(where, expert_ids.T, route_probs.T, out_grad, n_dp, room)
        seeds = [packed[0]] + [shift(packed[d], d) for d in range(1, n_dp)]
        blocks = {0: [jnp.stack(seeds[:per]), jnp.stack(seeds[per:])]}
        halves = {step: [ring_send(value, step) for value in blocks[0]] for step in (1, -1)}

        sibling_weight = swap(weight)
        hidden = expert_hidden[0, 0].transpose(1, 0, 2).reshape(slots, ff)
        hiddens = [(hidden, swap(hidden))]
        for d in range(1, n_dp):
            value = shift(after(hidden, *seeds[1:], halves[1][0], halves[-1][0]), d)
            hiddens.append((value, None))

        parts, scaleds, layout, facts = {}, [], [], []
        own_back, sent_back = [], [[] for _ in range(1, n_dp)]
        refs = []

        def work(items, *done):
            used, plan = [], []
            for off, d in items:
                value = blocks[off][d // per] if off in (0, half) else blocks[off]
                if not any(value is other for other in used):
                    used.append(value)
                where = [value is other for other in used].index(True)
                plan.append((where, d % per if off in (0, half) else d, d, offsets.index(off)))
            if done:
                gated = [after(used[0], *done)] + used[1:]
            else:
                gated = used
            made, scaled, back, fact = block_product(
                tuple(plan), meta, gated, hiddens, weight, sibling_weight, n_ex, top
            )
            for item, part in zip(items, made):
                parts[item] = part
            for d in sorted(scaled):
                scaleds.append(scaled[d])
                for (off, e), (where, place, _, _) in zip(items, plan):
                    if e == d:
                        if not any(used[where] is other for other in refs):
                            refs.append(used[where])
                        layout.append(([used[where] is other for other in refs].index(True), place))
                if d == 0:
                    own_back.append(back[0])
                    facts.append(fact)
                else:
                    sent_back[d - 1].append(shift(back[d], -d))
            return made[0]

        both = lambda offs: [(off, d) for d in range(n_dp) for off in offs]
        gate = ()
        for step in range(1, half):
            if step == 1:
                blocks[-1] = jnp.concatenate(halves[1], axis=0)
                blocks[1] = jnp.concatenate(halves[-1], axis=0)
            else:
                sent = blocks[1 - step], blocks[step - 1]
                if gate:
                    sent = after(sent[0], *gate), after(sent[1], *gate)
                blocks[-step] = ring_send(sent[0], 1)
                blocks[step] = ring_send(sent[1], -1)
            if step == 1:
                following = [(off, 0) for off in offsets[:3]]
            elif step == 2:
                following = [(off, d) for d in range(n_dp) for off in offsets[:5] if d > 0 or off not in offsets[:3]]
            else:
                following = both([-step, step])
            if step == half - 1:
                break
            if step > 1:
                gate = (ready,)
            if step == 2:
                for d in range(1, n_dp):
                    value = hiddens[d][0]
                    hiddens[d] = value, swap(after(value, blocks[-step], blocks[step], ready))
            ready = work(following)
        sent = after(blocks[1 - half], ready)[:per], after(blocks[half - 1], ready)[per:]
        blocks[half] = [ring_send(sent[0], 1), ring_send(sent[1], -1)]
        ready = work(following)
        work(both([half]), ready)

        carry = {}

        def hop_on(hop, *done):
            every = range(n_dp)
            if hop == half:
                values = [jnp.stack([parts[half, d] for d in every[:per]])]
                values.append(jnp.stack([parts[half, d] for d in every[per:]]))
            else:
                first, last = ((0, per), (per, n_dp)) if hop == half - 1 else ((0, n_dp), (0, n_dp))
                values = sums([([parts[hop, d] for d in every], carry[1], *first)])
                values += sums([([parts[-hop, d] for d in every], carry[-1], *last)])
            values = [after(value, *done) for value in values]
            carry[1] = ring_send(values[0], 1)
            carry[-1] = ring_send(values[1], -1)
            sending[:] = values
            return carry[1], carry[-1]

        sending = []
        hop_on(half)
        second = hop_on(half - 1)
        other = weight_product(
            [after(refs[0], *sending, *[value for sent in sent_back for value in sent])] + refs[1:], layout, scaleds, 1, jnp.bfloat16, width
        )
        swapped = swap(after(other, *second))
        third = hop_on(half - 2, other)
        spread, spread_other = spread_product(
            [after(facts[0][0], *second)] + [fact[0] for fact in facts[1:]],
            [fact[1] for fact in facts],
            [own_back] + sent_back,
            slots,
        )
        hidden_grad = spread + swap(spread_other)
        hidden_grad = hidden_grad.reshape(cap, n_ex, ff).transpose(1, 0, 2)[None, None]
        for hop in range(half - 3, 0, -1):
            hop_on(hop, spread)
        weight_grad = weight_product(
            [after(refs[0], *third)] + refs[1:], layout, scaleds, 0, jnp.float32, width, swapped
        )
        totals = close([after(parts[0, 0], weight_grad)] + [parts[0, d] for d in range(1, n_dp)], carry[1], carry[-1])
        pieces = [totals[0]] + [shift(totals[d], -d) for d in range(1, n_dp)]
        layer_out, prob_grad = home(where, expert_ids, pieces, width, n_ex)
        return (layer_out, prob_grad, hidden_grad, weight_grad[None])

    return shards


def solution(mesh):
    placed = (
        P(("dp", "expert"), None),
        P(("dp", "expert"), None),
        P("dp", "expert", None, None, None),
        P("expert", None, "dp"),
        P(("dp", "expert"), None),
    )
    return jax.shard_map(
        body(chip_ring(mesh)),
        mesh=mesh,
        in_specs=placed,
        out_specs=(
            P(("dp", "expert"), None),
            P(("dp", "expert"), None),
            P("dp", "expert", None, None, None),
            P("expert", None, "dp"),
        ),
        check_vma=False,
    )
```

```python
import functools

import jax
import jax.numpy as jnp
import numpy as np
from jax import lax
from jax.experimental import pallas as pl
from jax.experimental.pallas import tpu as pltpu
from jax.sharding import PartitionSpec as P

MIB = 1024 * 1024


def kernel_memory(rows):
    return pltpu.CompilerParams(vmem_limit_bytes=(20 if rows <= 1024 else 48) * MIB)


def dot(a, b, ca, cb):
    return lax.dot_general(a, b, (((ca,), (cb,)), ((), ())), preferred_element_type=jnp.float32)


def after(value, *done):
    return lax.optimization_barrier((value, *done))[0]


def chip_ring(mesh):
    chips = mesh.shape["expert"] // 2
    devices = mesh.devices.reshape(mesh.shape["dp"], -1)
    if not hasattr(devices[0, 0], "coords"):
        return list(range(chips))
    at = [tuple(devices[0, 2 * chip].coords)[1:] for chip in range(chips)]
    rows = max(z for _, z in at) + 1
    cols = max(y for y, _ in at) + 1
    if rows * cols != chips or rows % 2:
        return list(range(chips))
    walk = [(0, z) for z in range(rows)]
    for step, z in enumerate(reversed(range(rows))):
        span = range(1, cols)
        walk += [(y, z) for y in (span if step % 2 == 0 else reversed(span))]
    return [at.index(place) for place in walk]


def pack_kernel(top, n_out, where, ids_in, probs_in, grads_in, *refs):
    outs, (ids, probs, grads, sems) = refs[:n_out], refs[n_out:]
    copies = [
        pltpu.make_async_copy(source, target, sems.at[i])
        for i, (source, target) in enumerate([(ids_in, ids), (probs_in, probs), (grads_in, grads)])
    ]
    for copy in copies:
        copy.start()
    for copy in copies:
        copy.wait()
    tok = grads.shape[0]
    width = grads.shape[1] // len(outs)
    room = outs[0].shape[1] - width
    row = lax.broadcasted_iota(jnp.int32, (tok, tok), 0)
    col = lax.broadcasted_iota(jnp.int32, (tok, tok), 1)
    same = (row == col).astype(jnp.float32)

    def columns(value):
        return lax.dot_general(
            same,
            value,
            (((1,), (1,)), ((), ())),
            precision=lax.Precision.HIGHEST,
            preferred_element_type=jnp.float32,
        )

    prob = columns(probs[...])
    high = prob.astype(jnp.bfloat16)
    middle = (prob - high.astype(jnp.float32)).astype(jnp.bfloat16)
    low = (prob - high.astype(jnp.float32) - middle.astype(jnp.float32)).astype(jnp.bfloat16)
    named = columns(ids[...].astype(jnp.float32)).astype(jnp.bfloat16)
    blank = jnp.zeros((tok, room - 4 * top), jnp.bfloat16)
    routes = jnp.concatenate([named, high, middle, low, blank], axis=1)
    for d, out in enumerate(outs):
        at = lax.rem(where[0] + d, len(outs)) * width
        out[:, :width] = grads[:, pl.ds(pl.multiple_of(at, 128), width)]
        out[:, width:] = routes


def pack(where, ids, probs, grads, n_dp, room):
    top, tok = ids.shape
    width = grads.shape[1] // n_dp
    vmem = pl.BlockSpec(memory_space=pltpu.VMEM)
    return pl.pallas_call(
        functools.partial(pack_kernel, top, n_dp),
        in_specs=[pl.BlockSpec(memory_space=pltpu.SMEM)] + [pl.BlockSpec(memory_space=pltpu.HBM)] * 3,
        out_specs=[vmem] * n_dp,
        out_shape=[jax.ShapeDtypeStruct((tok, width + room), jnp.bfloat16)] * n_dp,
        scratch_shapes=[
            pltpu.VMEM(ids.shape, ids.dtype),
            pltpu.VMEM(probs.shape, probs.dtype),
            pltpu.VMEM(grads.shape, grads.dtype),
            pltpu.SemaphoreType.DMA((3,)),
        ],
        compiler_params=kernel_memory(tok),
        name="pack",
    )(where, ids, probs, grads)


def sum_kernel(starts, n_out, *refs):
    outs = refs[-n_out:]
    at = 0
    for out, (n_rows, arrives) in zip(outs, starts):
        carry = refs[at + n_rows] if arrives else None
        for i in range(n_rows):
            value = refs[at + i][...]
            if carry is not None and arrives[0] <= i < arrives[1]:
                value = value.astype(jnp.float32) + carry[i - arrives[0]].astype(jnp.float32)
            out[i] = value.astype(jnp.bfloat16)
        at += n_rows + (1 if arrives else 0)


def sums(jobs):
    tok, full = jobs[0][0][0].shape
    flat, starts, shapes = [], [], []
    for parts, carry, first, last in jobs:
        flat += list(parts) + [carry]
        starts.append((len(parts), (first, last)))
        shapes.append(jax.ShapeDtypeStruct((len(parts), tok, full), jnp.bfloat16))
    vmem = pl.BlockSpec(memory_space=pltpu.VMEM)
    return pl.pallas_call(
        functools.partial(sum_kernel, tuple(starts), len(shapes)),
        in_specs=[vmem] * len(flat),
        out_specs=[vmem] * len(shapes),
        out_shape=shapes,
        compiler_params=kernel_memory(tok),
        name="sums",
    )(*flat)


def close_kernel(n_dp, *refs):
    parts, (one, two), outs = refs[:n_dp], refs[n_dp : n_dp + 2], refs[n_dp + 2 :]
    for d, out in enumerate(outs):
        value = parts[d][...].astype(jnp.float32) + one[d].astype(jnp.float32)
        out[...] = (value + two[d].astype(jnp.float32)).astype(jnp.bfloat16)


def close(parts, one, two):
    vmem = pl.BlockSpec(memory_space=pltpu.VMEM)
    return pl.pallas_call(
        functools.partial(close_kernel, len(parts)),
        in_specs=[vmem] * (len(parts) + 2),
        out_specs=[vmem] * len(parts),
        out_shape=[jax.ShapeDtypeStruct(part.shape, jnp.bfloat16) for part in parts],
        compiler_params=kernel_memory(parts[0].shape[0]),
        name="close",
    )(*parts, one, two)


def home_kernel(n_ex, where, ids, *refs):
    pieces, (layer, prob) = refs[:-2], refs[-2:]
    n_dp = len(pieces)
    tok, top = ids.shape
    width = layer.shape[1] // n_dp
    inner = jnp.zeros((tok, n_ex), jnp.float32)
    for d, piece in enumerate(pieces):
        at = lax.rem(where[0] + d, n_dp) * width
        layer[:, pl.ds(pl.multiple_of(at, 128), width)] = piece[:, :width]
        more = piece[:, width:].astype(jnp.float32)
        inner = inner + more[:, :n_ex] + more[:, n_ex : 2 * n_ex]
    lane = lax.broadcasted_iota(jnp.int32, (tok, n_ex), 1)
    for k in range(top):
        mine = lane == ids[:, k : k + 1]
        prob[:, k : k + 1] = jnp.sum(jnp.where(mine, inner, 0.0), axis=1, keepdims=True)


def home(where, ids, pieces, width, n_ex):
    tok, top = ids.shape
    vmem = pl.BlockSpec(memory_space=pltpu.VMEM)
    return pl.pallas_call(
        functools.partial(home_kernel, n_ex),
        in_specs=[pl.BlockSpec(memory_space=pltpu.SMEM)] + [vmem] * (1 + len(pieces)),
        out_specs=[vmem] * 2,
        out_shape=[
            jax.ShapeDtypeStruct((tok, len(pieces) * width), jnp.bfloat16),
            jax.ShapeDtypeStruct((tok, top), jnp.float32),
        ],
        compiler_params=kernel_memory(tok),
        name="home",
    )(where, ids, *pieces)


def block_kernel(plan, refs_in, n_dp, n_ex, top, *refs):
    meta = refs[0]
    blocks = refs[1 : 1 + refs_in]
    at = 1 + refs_in
    replicas = sorted({item[2] for item in plan})
    hid = {d: refs[at + 2 * i : at + 2 * i + 2] for i, d in enumerate(replicas)}
    at += 2 * len(replicas)
    weights = refs[at : at + 2]
    at += 2
    parts = refs[at : at + len(plan)]
    at += len(plan)
    outs = {d: refs[at + 2 * i : at + 2 * i + 2] for i, d in enumerate(replicas)}
    at += 2 * len(replicas)
    index, prob = refs[at : at + 2] if 0 in replicas else (None, None)

    _, tok, full = blocks[0].shape
    ff, width = weights[0].shape
    slots = hid[replicas[0]][0].shape[0]
    count = len(plan) * tok
    rows = [blocks[where][place] for where, place, _, _ in plan]
    routes = jnp.concatenate([row[:, width:] for row in rows], axis=0).astype(jnp.float32)
    named = routes[:, :top]
    chance = routes[:, top : 2 * top] + routes[:, 2 * top : 3 * top] + routes[:, 3 * top : 4 * top]
    row = lax.broadcasted_iota(jnp.int32, (tok, tok), 0)
    col = lax.broadcasted_iota(jnp.int32, (tok, tok), 1)
    earlier = (col < row).astype(jnp.float32)
    lane = lax.broadcasted_iota(jnp.int32, (tok, slots), 1)
    spans = {d: [i for i, item in enumerate(plan) if item[2] == d] for d in replicas}
    helds, scaleds = [], []
    for x in range(2):
        mine = named == meta[x].astype(jnp.float32)
        here = jnp.sum(jnp.where(mine, chance, 0.0), axis=1, keepdims=True)
        taken = jnp.broadcast_to((here > 0.0).astype(jnp.float32), (count, 128))
        held = []
        for d in replicas:
            picks = []
            for n, i in enumerate(spans[d]):
                span = slice(i * tok, (i + 1) * tok)
                position = dot(earlier, taken[span], 1, 0)[:, :1].astype(jnp.int32)
                slot = jnp.where(here[span] > 0.0, position * n_ex + meta[2 + plan[i][3]], -1)
                picks.append((lane == slot).astype(jnp.bfloat16))
                if d == 0:
                    index[n * tok : (n + 1) * tok, x : x + 1] = slot
                    prob[n * tok : (n + 1) * tok, x : x + 1] = here[span]
            held.append(dot(jnp.concatenate(picks, axis=0), hid[d][x][...], 1, 0))
        held = jnp.concatenate(held, axis=0)
        scaled = (held * here).astype(jnp.bfloat16)
        base = 0
        for d in replicas:
            size = len(spans[d]) * tok
            outs[d][0][x] = scaled[base : base + size]
            base += size
        helds.append(held)
        scaleds.append(scaled)

    tile = 512
    for step in range(width // tile):
        cols = slice(step * tile, (step + 1) * tile)
        value = dot(scaleds[0], weights[0][:, cols], 1, 0) + dot(scaleds[1], weights[1][:, cols], 1, 0)
        value = value.astype(jnp.bfloat16)
        for i, out in enumerate(parts):
            out[:, cols] = value[i * tok : (i + 1) * tok]

    lhs = jnp.concatenate([row[:, :width] for row in rows], axis=0)
    lane = lax.broadcasted_iota(jnp.int32, (count, full - width), 1)
    extra = jnp.zeros((count, full - width), jnp.float32)
    for x in range(2):
        inner = jnp.zeros((count, 1), jnp.float32)
        step_ff = 256
        for step in range(ff // step_ff):
            cols = slice(step * step_ff, (step + 1) * step_ff)
            value = dot(lhs, weights[x][cols, :], 1, 1)
            inner = inner + jnp.sum(value * helds[x][:, cols], axis=1, keepdims=True)
            value = value.astype(jnp.bfloat16)
            base = 0
            for d in replicas:
                size = len(spans[d]) * tok
                outs[d][1][x, :, cols] = value[base : base + size]
                base += size
        high = inner.astype(jnp.bfloat16).astype(jnp.float32)
        extra = jnp.where(lane == meta[x], high, extra)
        extra = jnp.where(lane == meta[x] + n_ex, inner - high, extra)
    extra = extra.astype(jnp.bfloat16)
    for i, out in enumerate(parts):
        out[:, width:] = extra[i * tok : (i + 1) * tok]


def block_product(plan, meta, blocks, hiddens, w_own, w_sib, n_ex, top):
    n_dp = len(hiddens)
    _, tok, full = blocks[0].shape
    ff, width = w_own.shape
    slots = hiddens[0][0].shape[0]
    replicas = sorted({item[2] for item in plan})
    vmem = pl.BlockSpec(memory_space=pltpu.VMEM)
    bf16 = lambda *shape: jax.ShapeDtypeStruct(shape, jnp.bfloat16)
    out_shape = [bf16(tok, full) for _ in plan]
    sizes = {d: tok * sum(item[2] == d for item in plan) for d in replicas}
    for d in replicas:
        out_shape += [bf16(2, sizes[d], ff)] * 2
    if 0 in replicas:
        out_shape.append(jax.ShapeDtypeStruct((sizes[0], 2), jnp.int32))
        out_shape.append(jax.ShapeDtypeStruct((sizes[0], 2), jnp.float32))
    hid = [value for d in replicas for value in hiddens[d]]
    count = len(plan) * tok
    chips_rows = n_ex * tok * n_dp // 2
    made = pl.pallas_call(
        functools.partial(block_kernel, plan, len(blocks), n_dp, n_ex, top),
        in_specs=[pl.BlockSpec(memory_space=pltpu.SMEM)] + [vmem] * (len(blocks) + len(hid) + 2),
        out_specs=[vmem] * len(out_shape),
        out_shape=out_shape,
        compiler_params=kernel_memory(chips_rows),
        cost_estimate=pl.CostEstimate(
            flops=8 * count * ff * width,
            bytes_accessed=4 * ff * width + 4 * count * (full + ff),
            transcendentals=0,
        ),
        name="block_product",
    )(meta, *blocks, *hid, w_own, w_sib)
    parts = made[: len(plan)]
    rest = made[len(plan) :]
    scaled = {d: rest[2 * i] for i, d in enumerate(replicas)}
    back = {d: rest[2 * i + 1] for i, d in enumerate(replicas)}
    return parts, scaled, back, rest[2 * len(replicas) :]


def spread_kernel(sizes, *refs):
    n_parts = len(sizes[0])
    index, prob = refs[:n_parts], refs[n_parts : 2 * n_parts]
    backs = list(refs[2 * n_parts : -2])
    outs = refs[-2:]
    slots = outs[0].shape[0]
    slot = jnp.concatenate([ref[...] for ref in index], axis=0)
    weight = jnp.concatenate([ref[...] for ref in prob], axis=0)
    lane = lax.broadcasted_iota(jnp.int32, (slot.shape[0], slots), 1)
    for x, out in enumerate(outs):
        back, at = None, 0
        for pieces in sizes:
            value = jnp.concatenate([ref[x] for ref in backs[at : at + len(pieces)]], axis=0)
            at += len(pieces)
            value = value.astype(jnp.float32)
            back = value if back is None else back + value
        pick = (lane == slot[:, x : x + 1]).astype(jnp.bfloat16)
        mine = (back * weight[:, x : x + 1]).astype(jnp.bfloat16)
        out[...] = dot(pick, mine, 0, 0).astype(jnp.bfloat16)


def spread_product(index, prob, backs, slots):
    sizes = [[part.shape[1] for part in parts] for parts in backs]
    ff = backs[0][0].shape[2]
    rows = sum(sizes[0])
    flat = [part for parts in backs for part in parts]
    vmem = pl.BlockSpec(memory_space=pltpu.VMEM)
    return pl.pallas_call(
        functools.partial(spread_kernel, sizes),
        in_specs=[vmem] * (2 * len(index) + len(flat)),
        out_specs=[vmem] * 2,
        out_shape=[jax.ShapeDtypeStruct((slots, ff), jnp.bfloat16)] * 2,
        compiler_params=kernel_memory(rows * len(backs)),
        cost_estimate=pl.CostEstimate(
            flops=4 * rows * slots * ff,
            bytes_accessed=4 * (1 + len(backs)) * rows * ff,
            transcendentals=0,
        ),
        name="spread_product",
    )(*index, *prob, *flat)


def weight_kernel(n_refs, n_scaled, layout, *refs):
    blocks, scaleds, more = refs[:n_refs], refs[n_refs : n_refs + n_scaled], refs[n_refs + n_scaled : -2]
    out, turned = refs[-2:]

    @pl.when(pl.program_id(0) == 0)
    def _():
        turned[...] = jnp.concatenate([ref[0] for ref in scaleds], axis=0).T

    rows = jnp.concatenate([blocks[where][place] for where, place in layout], axis=0)
    total = dot(turned[...], rows, 1, 0)
    for ref in more:
        total = total + ref[...].astype(jnp.float32)
    out[...] = total.astype(out.dtype)


def weight_product(blocks, layout, scaleds, x, dtype, width, *more):
    tok = blocks[0].shape[1]
    ff = scaleds[0].shape[2]
    rows = len(layout) * tok
    tile = 512 if width >= 2048 else 256
    return pl.pallas_call(
        functools.partial(weight_kernel, len(blocks), len(scaleds), layout),
        grid=(width // tile,),
        in_specs=[pl.BlockSpec(block.shape[:2] + (tile,), lambda i: (0, 0, i)) for block in blocks]
        + [
            pl.BlockSpec((1,) + value.shape[1:], lambda i: (x, 0, 0), pipeline_mode=pl.Buffered(1))
            for value in scaleds
        ]
        + [pl.BlockSpec((ff, tile), lambda i: (0, i)) for _ in more],
        out_specs=pl.BlockSpec((ff, tile), lambda i: (0, i)),
        out_shape=jax.ShapeDtypeStruct((ff, width), dtype),
        scratch_shapes=[pltpu.VMEM((ff, rows), jnp.bfloat16)],
        compiler_params=kernel_memory(rows),
        cost_estimate=pl.CostEstimate(
            flops=2 * rows * width * ff,
            bytes_accessed=2 * rows * (width + ff) + 4 * ff * width,
            transcendentals=0,
        ),
        name="weight_product",
    )(*blocks, *scaleds, *more)


def body(ring):
    chips = len(ring)
    half = chips // 2
    offsets = [0]
    for step in range(1, half):
        offsets += [-step, step]
    offsets.append(half)
    place_of = {chip: at for at, chip in enumerate(ring)}
    meta_table = np.asarray(
        [
            [e, e ^ 1] + [2 * ring[(place_of[e // 2] + off) % chips] + e % 2 for off in offsets]
            for e in range(2 * chips)
        ],
        np.int32,
    )

    def along(step):
        return [
            (2 * ring[at] + core, 2 * ring[(at + step) % chips] + core)
            for at in range(chips)
            for core in range(2)
        ]

    forward, backward = along(1), along(-1)
    sibling = [(e, e ^ 1) for e in range(2 * chips)]

    def shards(expert_ids, route_probs, expert_hidden, down_weight, out_grad):
        tok, top = expert_ids.shape
        n_dp = lax.axis_size("dp")
        n_ex = lax.axis_size("expert")
        cap = expert_hidden.shape[3]
        slots = cap * n_ex
        ff = down_weight.shape[1]
        width = down_weight.shape[2]
        weight = down_weight[0]
        replica = lax.axis_index("dp")
        expert = lax.axis_index("expert")
        per = n_dp // 2
        meta = lax.dynamic_index_in_dim(jnp.asarray(meta_table), expert, 0, keepdims=False)

        def shift(value, step):
            return lax.ppermute(value, "dp", [(i, (i + step) % n_dp) for i in range(n_dp)])

        def ring_send(value, step):
            return lax.ppermute(value, "expert", forward if step > 0 else backward)

        def swap(value):
            return lax.ppermute(value, "expert", sibling)

        room = 128 * -(-max(4 * top, 2 * n_ex) // 128)
        where = replica.reshape(1).astype(jnp.int32)
        packed = pack(where, expert_ids.T, route_probs.T, out_grad, n_dp, room)
        seeds = [packed[0]] + [shift(packed[d], d) for d in range(1, n_dp)]
        blocks = {0: [jnp.stack(seeds[:per]), jnp.stack(seeds[per:])]}
        halves = {step: [ring_send(value, step) for value in blocks[0]] for step in (1, -1)}

        sibling_weight = swap(weight)
        hidden = expert_hidden[0, 0].transpose(1, 0, 2).reshape(slots, ff)
        hiddens = [(hidden, swap(hidden))]
        for d in range(1, n_dp):
            value = shift(after(hidden, *seeds[1:], halves[1][0], halves[-1][0]), d)
            hiddens.append((value, None))

        parts, scaleds, layout, facts = {}, [], [], []
        own_back, sent_back = [], [[] for _ in range(1, n_dp)]
        refs = []

        def work(items, *done):
            used, plan = [], []
            for off, d in items:
                value = blocks[off][d // per] if off in (0, half) else blocks[off]
                if not any(value is other for other in used):
                    used.append(value)
                where = [value is other for other in used].index(True)
                plan.append((where, d % per if off in (0, half) else d, d, offsets.index(off)))
            if done:
                gated = [after(used[0], *done)] + used[1:]
            else:
                gated = used
            made, scaled, back, fact = block_product(
                tuple(plan), meta, gated, hiddens, weight, sibling_weight, n_ex, top
            )
            for item, part in zip(items, made):
                parts[item] = part
            for d in sorted(scaled):
                scaleds.append(scaled[d])
                for (off, e), (where, place, _, _) in zip(items, plan):
                    if e == d:
                        if not any(used[where] is other for other in refs):
                            refs.append(used[where])
                        layout.append(([used[where] is other for other in refs].index(True), place))
                if d == 0:
                    own_back.append(back[0])
                    facts.append(fact)
                    continue
                sent_back[d - 1].append(shift(after(back[d], *blocks.get(half, ())), -d))
            return made[0]

        near = offsets[: 2 * min(2, half - 1) + 1]
        for step in range(1, half):
            if step == 1:
                blocks[-1] = jnp.concatenate(halves[1], axis=0)
                blocks[1] = jnp.concatenate(halves[-1], axis=0)
            else:
                blocks[-step] = ring_send(blocks[1 - step], 1)
                blocks[step] = ring_send(blocks[step - 1], -1)
            if step == min(2, half - 1):
                ready = work([(off, 0) for off in near])
        arrived = blocks[1 - half], blocks[half - 1]
        sent = after(arrived[0], ready)[:per], after(arrived[1], ready)[per:]
        blocks[half] = [ring_send(sent[0], 1), ring_send(sent[1], -1)]
        for d in range(1, n_dp):
            value = hiddens[d][0]
            hiddens[d] = value, swap(after(value, ready, *arrived))
        later = [[(off, d) for off in near for d in range(1, n_dp)]]
        later.append([(off, d) for off in offsets for d in range(n_dp) if off not in near])
        for items in later:
            for at in range(0, len(items), 12):
                ready = work(sorted(items[at : at + 12], key=lambda item: item[1]), ready)

        carry = {}

        def hop_on(hop, *done):
            every = range(n_dp)
            if hop == half:
                values = [jnp.stack([parts[half, d] for d in every[:per]])]
                values.append(jnp.stack([parts[half, d] for d in every[per:]]))
            else:
                first, last = ((0, per), (per, n_dp)) if hop == half - 1 else ((0, n_dp), (0, n_dp))
                values = sums([([parts[hop, d] for d in every], carry[1], *first)])
                values += sums([([parts[-hop, d] for d in every], carry[-1], *last)])
            values = [after(value, *done) for value in values]
            carry[1] = ring_send(values[0], 1)
            carry[-1] = ring_send(values[1], -1)
            sending[:] = values
            return carry[1], carry[-1]

        sending = []
        hop_on(half)
        second = hop_on(half - 1)
        other = weight_product(
            [after(refs[0], *sending, *[sent[0] for sent in sent_back])] + refs[1:], layout, scaleds, 1, jnp.bfloat16, width
        )
        swapped = swap(after(other, *second, *[sent[-1] for sent in sent_back]))
        third = hop_on(half - 2, other)
        spread, spread_other = spread_product(
            [after(facts[0][0], *second)] + [fact[0] for fact in facts[1:]],
            [fact[1] for fact in facts],
            [own_back] + sent_back,
            slots,
        )
        hidden_grad = spread + swap(spread_other)
        hidden_grad = hidden_grad.reshape(cap, n_ex, ff).transpose(1, 0, 2)[None, None]
        for hop in range(half - 3, 0, -1):
            hop_on(hop, spread)
        weight_grad = weight_product(
            [after(refs[0], *third)] + refs[1:], layout, scaleds, 0, jnp.float32, width, swapped
        )
        totals = close([after(parts[0, 0], weight_grad)] + [parts[0, d] for d in range(1, n_dp)], carry[1], carry[-1])
        pieces = [totals[0]] + [shift(totals[d], -d) for d in range(1, n_dp)]
        layer_out, prob_grad = home(where, expert_ids, pieces, width, n_ex)
        return (layer_out, prob_grad, hidden_grad, weight_grad[None])

    return shards


def solution(mesh):
    placed = (
        P(("dp", "expert"), None),
        P(("dp", "expert"), None),
        P("dp", "expert", None, None, None),
        P("expert", None, "dp"),
        P(("dp", "expert"), None),
    )
    return jax.shard_map(
        body(chip_ring(mesh)),
        mesh=mesh,
        in_specs=placed,
        out_specs=(
            P(("dp", "expert"), None),
            P(("dp", "expert"), None),
            P("dp", "expert", None, None, None),
            P("expert", None, "dp"),
        ),
        check_vma=False,
    )
```

```python
import functools

import jax
import jax.numpy as jnp
import numpy as np
from jax import lax
from jax.experimental import pallas as pl
from jax.experimental.pallas import tpu as pltpu
from jax.sharding import PartitionSpec as P

MIB = 1024 * 1024


def kernel_memory(rows):
    return pltpu.CompilerParams(vmem_limit_bytes=(20 if rows <= 1024 else 48) * MIB)


def dot(a, b, ca, cb):
    return lax.dot_general(a, b, (((ca,), (cb,)), ((), ())), preferred_element_type=jnp.float32)


def after(value, *done):
    return lax.optimization_barrier((value, *done))[0]


def chip_ring(mesh):
    chips = mesh.shape["expert"] // 2
    devices = mesh.devices.reshape(mesh.shape["dp"], -1)
    if not hasattr(devices[0, 0], "coords"):
        return list(range(chips))
    at = [tuple(devices[0, 2 * chip].coords)[1:] for chip in range(chips)]
    rows = max(z for _, z in at) + 1
    cols = max(y for y, _ in at) + 1
    if rows * cols != chips or rows % 2:
        return list(range(chips))
    walk = [(0, z) for z in range(rows)]
    for step, z in enumerate(reversed(range(rows))):
        span = range(1, cols)
        walk += [(y, z) for y in (span if step % 2 == 0 else reversed(span))]
    return [at.index(place) for place in walk]


def pack_kernel(top, n_out, where, ids_in, probs_in, grads_in, *refs):
    outs, (ids, probs, grads, sems) = refs[:n_out], refs[n_out:]
    copies = [
        pltpu.make_async_copy(source, target, sems.at[i])
        for i, (source, target) in enumerate([(ids_in, ids), (probs_in, probs), (grads_in, grads)])
    ]
    for copy in copies:
        copy.start()
    for copy in copies:
        copy.wait()
    tok = grads.shape[0]
    width = grads.shape[1] // len(outs)
    room = outs[0].shape[1] - width
    row = lax.broadcasted_iota(jnp.int32, (tok, tok), 0)
    col = lax.broadcasted_iota(jnp.int32, (tok, tok), 1)
    same = (row == col).astype(jnp.float32)

    def columns(value):
        return lax.dot_general(
            same,
            value,
            (((1,), (1,)), ((), ())),
            precision=lax.Precision.HIGHEST,
            preferred_element_type=jnp.float32,
        )

    prob = columns(probs[...])
    high = prob.astype(jnp.bfloat16)
    middle = (prob - high.astype(jnp.float32)).astype(jnp.bfloat16)
    low = (prob - high.astype(jnp.float32) - middle.astype(jnp.float32)).astype(jnp.bfloat16)
    named = columns(ids[...].astype(jnp.float32)).astype(jnp.bfloat16)
    blank = jnp.zeros((tok, room - 4 * top), jnp.bfloat16)
    routes = jnp.concatenate([named, high, middle, low, blank], axis=1)
    for d, out in enumerate(outs):
        at = lax.rem(where[0] + d, len(outs)) * width
        out[:, :width] = grads[:, pl.ds(pl.multiple_of(at, 128), width)]
        out[:, width:] = routes


def pack(where, ids, probs, grads, n_dp, room):
    top, tok = ids.shape
    width = grads.shape[1] // n_dp
    vmem = pl.BlockSpec(memory_space=pltpu.VMEM)
    return pl.pallas_call(
        functools.partial(pack_kernel, top, n_dp),
        in_specs=[pl.BlockSpec(memory_space=pltpu.SMEM)] + [pl.BlockSpec(memory_space=pltpu.HBM)] * 3,
        out_specs=[vmem] * n_dp,
        out_shape=[jax.ShapeDtypeStruct((tok, width + room), jnp.bfloat16)] * n_dp,
        scratch_shapes=[
            pltpu.VMEM(ids.shape, ids.dtype),
            pltpu.VMEM(probs.shape, probs.dtype),
            pltpu.VMEM(grads.shape, grads.dtype),
            pltpu.SemaphoreType.DMA((3,)),
        ],
        compiler_params=kernel_memory(tok),
        name="pack",
    )(where, ids, probs, grads)


def sum_kernel(starts, n_out, *refs):
    outs = refs[-n_out:]
    at = 0
    for out, (n_rows, arrives) in zip(outs, starts):
        carry = refs[at + n_rows] if arrives else None
        for i in range(n_rows):
            value = refs[at + i][...]
            if carry is not None and arrives[0] <= i < arrives[1]:
                value = value.astype(jnp.float32) + carry[i - arrives[0]].astype(jnp.float32)
            out[i] = value.astype(jnp.bfloat16)
        at += n_rows + (1 if arrives else 0)


def sums(jobs):
    tok, full = jobs[0][0][0].shape
    flat, starts, shapes = [], [], []
    for parts, carry, first, last in jobs:
        flat += list(parts) + [carry]
        starts.append((len(parts), (first, last)))
        shapes.append(jax.ShapeDtypeStruct((len(parts), tok, full), jnp.bfloat16))
    vmem = pl.BlockSpec(memory_space=pltpu.VMEM)
    return pl.pallas_call(
        functools.partial(sum_kernel, tuple(starts), len(shapes)),
        in_specs=[vmem] * len(flat),
        out_specs=[vmem] * len(shapes),
        out_shape=shapes,
        compiler_params=kernel_memory(tok),
        name="sums",
    )(*flat)


def close_kernel(n_dp, *refs):
    parts, (one, two), outs = refs[:n_dp], refs[n_dp : n_dp + 2], refs[n_dp + 2 :]
    for d, out in enumerate(outs):
        value = parts[d][...].astype(jnp.float32) + one[d].astype(jnp.float32)
        out[...] = (value + two[d].astype(jnp.float32)).astype(jnp.bfloat16)


def close(parts, one, two):
    vmem = pl.BlockSpec(memory_space=pltpu.VMEM)
    return pl.pallas_call(
        functools.partial(close_kernel, len(parts)),
        in_specs=[vmem] * (len(parts) + 2),
        out_specs=[vmem] * len(parts),
        out_shape=[jax.ShapeDtypeStruct(part.shape, jnp.bfloat16) for part in parts],
        compiler_params=kernel_memory(parts[0].shape[0]),
        name="close",
    )(*parts, one, two)


def home_kernel(n_ex, where, ids, *refs):
    pieces, (layer, prob) = refs[:-2], refs[-2:]
    n_dp = len(pieces)
    top, tok = ids.shape
    width = layer.shape[1] // n_dp
    inner = jnp.zeros((tok, n_ex), jnp.float32)
    for d, piece in enumerate(pieces):
        at = lax.rem(where[0] + d, n_dp) * width
        layer[:, pl.ds(pl.multiple_of(at, 128), width)] = piece[:, :width]
        more = piece[:, width:].astype(jnp.float32)
        inner = inner + more[:, :n_ex] + more[:, n_ex : 2 * n_ex]
    row = lax.broadcasted_iota(jnp.int32, (n_ex, n_ex), 0)
    col = lax.broadcasted_iota(jnp.int32, (n_ex, n_ex), 1)
    inner = lax.dot_general(
        (row == col).astype(jnp.float32),
        inner,
        (((1,), (1,)), ((), ())),
        precision=lax.Precision.HIGHEST,
        preferred_element_type=jnp.float32,
    )
    row = lax.broadcasted_iota(jnp.int32, (n_ex, tok), 0)
    for k in range(top):
        mine = row == ids[k : k + 1, :]
        prob[k : k + 1, :] = jnp.sum(jnp.where(mine, inner, 0.0), axis=0, keepdims=True)


def home(where, ids, pieces, width, n_ex):
    top, tok = ids.shape
    vmem = pl.BlockSpec(memory_space=pltpu.VMEM)
    return pl.pallas_call(
        functools.partial(home_kernel, n_ex),
        in_specs=[pl.BlockSpec(memory_space=pltpu.SMEM)] + [vmem] * (1 + len(pieces)),
        out_specs=[vmem] * 2,
        out_shape=[
            jax.ShapeDtypeStruct((tok, len(pieces) * width), jnp.bfloat16),
            jax.ShapeDtypeStruct((top, tok), jnp.float32),
        ],
        compiler_params=kernel_memory(tok),
        name="home",
    )(where, ids, *pieces)


def block_kernel(plan, refs_in, n_dp, n_ex, top, *refs):
    meta = refs[0]
    blocks = refs[1 : 1 + refs_in]
    at = 1 + refs_in
    replicas = sorted({item[2] for item in plan})
    hid = {d: refs[at + 2 * i : at + 2 * i + 2] for i, d in enumerate(replicas)}
    at += 2 * len(replicas)
    weights = refs[at : at + 2]
    at += 2
    parts = refs[at : at + len(plan)]
    at += len(plan)
    outs = {d: refs[at + 2 * i : at + 2 * i + 2] for i, d in enumerate(replicas)}
    at += 2 * len(replicas)
    index, prob = refs[at : at + 2] if 0 in replicas else (None, None)

    _, tok, full = blocks[0].shape
    ff, width = weights[0].shape
    slots = hid[replicas[0]][0].shape[0]
    count = len(plan) * tok
    rows = [blocks[where][place] for where, place, _, _ in plan]
    routes = jnp.concatenate([row[:, width:] for row in rows], axis=0).astype(jnp.float32)
    named = routes[:, :top]
    chance = routes[:, top : 2 * top] + routes[:, 2 * top : 3 * top] + routes[:, 3 * top : 4 * top]
    row = lax.broadcasted_iota(jnp.int32, (tok, tok), 0)
    col = lax.broadcasted_iota(jnp.int32, (tok, tok), 1)
    earlier = (col < row).astype(jnp.float32)
    lane = lax.broadcasted_iota(jnp.int32, (tok, slots), 1)
    spans = {d: [i for i, item in enumerate(plan) if item[2] == d] for d in replicas}
    helds, scaleds = [], []
    for x in range(2):
        mine = named == meta[x].astype(jnp.float32)
        here = jnp.sum(jnp.where(mine, chance, 0.0), axis=1, keepdims=True)
        taken = jnp.broadcast_to((here > 0.0).astype(jnp.float32), (count, 128))
        held = []
        for d in replicas:
            picks = []
            for n, i in enumerate(spans[d]):
                span = slice(i * tok, (i + 1) * tok)
                position = dot(earlier, taken[span], 1, 0)[:, :1].astype(jnp.int32)
                slot = jnp.where(here[span] > 0.0, position * n_ex + meta[2 + plan[i][3]], -1)
                picks.append((lane == slot).astype(jnp.bfloat16))
                if d == 0:
                    index[n * tok : (n + 1) * tok, x : x + 1] = slot
                    prob[n * tok : (n + 1) * tok, x : x + 1] = here[span]
            held.append(dot(jnp.concatenate(picks, axis=0), hid[d][x][...], 1, 0))
        held = jnp.concatenate(held, axis=0)
        scaled = (held * here).astype(jnp.bfloat16)
        base = 0
        for d in replicas:
            size = len(spans[d]) * tok
            outs[d][0][x] = scaled[base : base + size]
            base += size
        helds.append(held)
        scaleds.append(scaled)

    tile = 512
    for step in range(width // tile):
        cols = slice(step * tile, (step + 1) * tile)
        value = dot(scaleds[0], weights[0][:, cols], 1, 0) + dot(scaleds[1], weights[1][:, cols], 1, 0)
        value = value.astype(jnp.bfloat16)
        for i, out in enumerate(parts):
            out[:, cols] = value[i * tok : (i + 1) * tok]

    lhs = jnp.concatenate([row[:, :width] for row in rows], axis=0)
    lane = lax.broadcasted_iota(jnp.int32, (count, full - width), 1)
    extra = jnp.zeros((count, full - width), jnp.float32)
    for x in range(2):
        inner = jnp.zeros((count, 1), jnp.float32)
        step_ff = 256
        for step in range(ff // step_ff):
            cols = slice(step * step_ff, (step + 1) * step_ff)
            value = dot(lhs, weights[x][cols, :], 1, 1)
            inner = inner + jnp.sum(value * helds[x][:, cols], axis=1, keepdims=True)
            value = value.astype(jnp.bfloat16)
            base = 0
            for d in replicas:
                size = len(spans[d]) * tok
                outs[d][1][x, :, cols] = value[base : base + size]
                base += size
        high = inner.astype(jnp.bfloat16).astype(jnp.float32)
        extra = jnp.where(lane == meta[x], high, extra)
        extra = jnp.where(lane == meta[x] + n_ex, inner - high, extra)
    extra = extra.astype(jnp.bfloat16)
    for i, out in enumerate(parts):
        out[:, width:] = extra[i * tok : (i + 1) * tok]


def block_product(plan, meta, blocks, hiddens, w_own, w_sib, n_ex, top):
    n_dp = len(hiddens)
    _, tok, full = blocks[0].shape
    ff, width = w_own.shape
    slots = hiddens[0][0].shape[0]
    replicas = sorted({item[2] for item in plan})
    vmem = pl.BlockSpec(memory_space=pltpu.VMEM)
    bf16 = lambda *shape: jax.ShapeDtypeStruct(shape, jnp.bfloat16)
    out_shape = [bf16(tok, full) for _ in plan]
    sizes = {d: tok * sum(item[2] == d for item in plan) for d in replicas}
    for d in replicas:
        out_shape += [bf16(2, sizes[d], ff)] * 2
    if 0 in replicas:
        out_shape.append(jax.ShapeDtypeStruct((sizes[0], 2), jnp.int32))
        out_shape.append(jax.ShapeDtypeStruct((sizes[0], 2), jnp.float32))
    hid = [value for d in replicas for value in hiddens[d]]
    count = len(plan) * tok
    chips_rows = n_ex * tok * n_dp // 2
    made = pl.pallas_call(
        functools.partial(block_kernel, plan, len(blocks), n_dp, n_ex, top),
        in_specs=[pl.BlockSpec(memory_space=pltpu.SMEM)] + [vmem] * (len(blocks) + len(hid) + 2),
        out_specs=[vmem] * len(out_shape),
        out_shape=out_shape,
        compiler_params=kernel_memory(chips_rows),
        cost_estimate=pl.CostEstimate(
            flops=8 * count * ff * width,
            bytes_accessed=4 * ff * width + 4 * count * (full + ff),
            transcendentals=0,
        ),
        name="block_product",
    )(meta, *blocks, *hid, w_own, w_sib)
    parts = made[: len(plan)]
    rest = made[len(plan) :]
    scaled = {d: rest[2 * i] for i, d in enumerate(replicas)}
    back = {d: rest[2 * i + 1] for i, d in enumerate(replicas)}
    return parts, scaled, back, rest[2 * len(replicas) :]


def spread_kernel(sizes, *refs):
    n_parts = len(sizes[0])
    index, prob = refs[:n_parts], refs[n_parts : 2 * n_parts]
    backs = list(refs[2 * n_parts : -2])
    outs = refs[-2:]
    slots = outs[0].shape[0]
    slot = jnp.concatenate([ref[...] for ref in index], axis=0)
    weight = jnp.concatenate([ref[...] for ref in prob], axis=0)
    lane = lax.broadcasted_iota(jnp.int32, (slot.shape[0], slots), 1)
    for x, out in enumerate(outs):
        back, at = None, 0
        for pieces in sizes:
            value = jnp.concatenate([ref[x] for ref in backs[at : at + len(pieces)]], axis=0)
            at += len(pieces)
            value = value.astype(jnp.float32)
            back = value if back is None else back + value
        pick = (lane == slot[:, x : x + 1]).astype(jnp.bfloat16)
        mine = (back * weight[:, x : x + 1]).astype(jnp.bfloat16)
        out[...] = dot(pick, mine, 0, 0).astype(jnp.bfloat16)


def spread_product(index, prob, backs, slots):
    sizes = [[part.shape[1] for part in parts] for parts in backs]
    ff = backs[0][0].shape[2]
    rows = sum(sizes[0])
    flat = [part for parts in backs for part in parts]
    vmem = pl.BlockSpec(memory_space=pltpu.VMEM)
    return pl.pallas_call(
        functools.partial(spread_kernel, sizes),
        in_specs=[vmem] * (2 * len(index) + len(flat)),
        out_specs=[vmem] * 2,
        out_shape=[jax.ShapeDtypeStruct((slots, ff), jnp.bfloat16)] * 2,
        compiler_params=kernel_memory(rows * len(backs)),
        cost_estimate=pl.CostEstimate(
            flops=4 * rows * slots * ff,
            bytes_accessed=4 * (1 + len(backs)) * rows * ff,
            transcendentals=0,
        ),
        name="spread_product",
    )(*index, *prob, *flat)


def weight_kernel(n_refs, n_scaled, layout, *refs):
    blocks, scaleds, more = refs[:n_refs], refs[n_refs : n_refs + n_scaled], refs[n_refs + n_scaled : -2]
    out, turned = refs[-2:]

    @pl.when(pl.program_id(0) == 0)
    def _():
        turned[...] = jnp.concatenate([ref[0] for ref in scaleds], axis=0).T

    rows = jnp.concatenate([blocks[where][place] for where, place in layout], axis=0)
    total = dot(turned[...], rows, 1, 0)
    for ref in more:
        total = total + ref[...].astype(jnp.float32)
    out[...] = total.astype(out.dtype)


def weight_product(blocks, layout, scaleds, x, dtype, width, *more):
    tok = blocks[0].shape[1]
    ff = scaleds[0].shape[2]
    rows = len(layout) * tok
    tile = 512 if width >= 2048 else 256
    return pl.pallas_call(
        functools.partial(weight_kernel, len(blocks), len(scaleds), layout),
        grid=(width // tile,),
        in_specs=[pl.BlockSpec(block.shape[:2] + (tile,), lambda i: (0, 0, i)) for block in blocks]
        + [
            pl.BlockSpec((1,) + value.shape[1:], lambda i: (x, 0, 0), pipeline_mode=pl.Buffered(1))
            for value in scaleds
        ]
        + [pl.BlockSpec((ff, tile), lambda i: (0, i)) for _ in more],
        out_specs=pl.BlockSpec((ff, tile), lambda i: (0, i)),
        out_shape=jax.ShapeDtypeStruct((ff, width), dtype),
        scratch_shapes=[pltpu.VMEM((ff, rows), jnp.bfloat16)],
        compiler_params=kernel_memory(rows),
        cost_estimate=pl.CostEstimate(
            flops=2 * rows * width * ff,
            bytes_accessed=2 * rows * (width + ff) + 4 * ff * width,
            transcendentals=0,
        ),
        name="weight_product",
    )(*blocks, *scaleds, *more)


def body(ring):
    chips = len(ring)
    half = chips // 2
    offsets = [0]
    for step in range(1, half):
        offsets += [-step, step]
    offsets.append(half)
    place_of = {chip: at for at, chip in enumerate(ring)}
    meta_table = np.asarray(
        [
            [e, e ^ 1] + [2 * ring[(place_of[e // 2] + off) % chips] + e % 2 for off in offsets]
            for e in range(2 * chips)
        ],
        np.int32,
    )

    def along(step):
        return [
            (2 * ring[at] + core, 2 * ring[(at + step) % chips] + core)
            for at in range(chips)
            for core in range(2)
        ]

    forward, backward = along(1), along(-1)
    sibling = [(e, e ^ 1) for e in range(2 * chips)]

    def shards(expert_ids, route_probs, expert_hidden, down_weight, out_grad):
        tok, top = expert_ids.shape
        n_dp = lax.axis_size("dp")
        n_ex = lax.axis_size("expert")
        cap = expert_hidden.shape[3]
        slots = cap * n_ex
        ff = down_weight.shape[1]
        width = down_weight.shape[2]
        weight = down_weight[0]
        replica = lax.axis_index("dp")
        expert = lax.axis_index("expert")
        per = n_dp // 2
        meta = lax.dynamic_index_in_dim(jnp.asarray(meta_table), expert, 0, keepdims=False)

        def shift(value, step):
            return lax.ppermute(value, "dp", [(i, (i + step) % n_dp) for i in range(n_dp)])

        def ring_send(value, step):
            return lax.ppermute(value, "expert", forward if step > 0 else backward)

        def swap(value):
            return lax.ppermute(value, "expert", sibling)

        room = 128 * -(-max(4 * top, 2 * n_ex) // 128)
        where = replica.reshape(1).astype(jnp.int32)
        packed = pack(where, expert_ids.T, route_probs.T, out_grad, n_dp, room)
        seeds = [packed[0]] + [shift(packed[d], d) for d in range(1, n_dp)]
        blocks = {0: [jnp.stack(seeds[:per]), jnp.stack(seeds[per:])]}
        halves = {step: [ring_send(value, step) for value in blocks[0]] for step in (1, -1)}
        halves[1][1] = after(halves[1][1], meta)

        sibling_weight = swap(weight)
        hidden = expert_hidden[0, 0].transpose(1, 0, 2).reshape(slots, ff)
        hiddens = [(hidden, swap(hidden))]
        for d in range(1, n_dp):
            value = shift(after(hidden, *seeds[1:], halves[1][0], halves[-1][0]), d)
            hiddens.append((value, None))

        parts, scaleds, layout, facts = {}, [], [], []
        own_back, sent_back = [], [[] for _ in range(1, n_dp)]
        refs = []

        def work(items, *done):
            used, plan = [], []
            for off, d in items:
                value = blocks[off][d // per] if off in (0, half) else blocks[off]
                if not any(value is other for other in used):
                    used.append(value)
                where = [value is other for other in used].index(True)
                plan.append((where, d % per if off in (0, half) else d, d, offsets.index(off)))
            if done:
                gated = [after(used[0], *done)] + used[1:]
            else:
                gated = used
            made, scaled, back, fact = block_product(
                tuple(plan), meta, gated, hiddens, weight, sibling_weight, n_ex, top
            )
            for item, part in zip(items, made):
                parts[item] = part
            for d in sorted(scaled):
                scaleds.append(scaled[d])
                for (off, e), (where, place, _, _) in zip(items, plan):
                    if e == d:
                        if not any(used[where] is other for other in refs):
                            refs.append(used[where])
                        layout.append(([used[where] is other for other in refs].index(True), place))
                if d == 0:
                    own_back.append(back[0])
                    facts.append(fact)
                    continue
                sent_back[d - 1].append(shift(after(back[d], *blocks.get(half, ())), -d))
            return made[0]

        near = offsets[: 2 * min(2, half - 1) + 1]
        for step in range(1, half):
            if step == 1:
                blocks[-1] = jnp.concatenate(halves[1], axis=0)
                blocks[1] = jnp.concatenate(halves[-1], axis=0)
            else:
                blocks[-step] = ring_send(blocks[1 - step], 1)
                blocks[step] = ring_send(blocks[step - 1], -1)
            if step == min(2, half - 1):
                ready = work([(off, 0) for off in near])
        arrived = blocks[1 - half], blocks[half - 1]
        sent = after(arrived[0], ready)[:per], after(arrived[1], ready)[per:]
        blocks[half] = [ring_send(sent[0], 1), ring_send(sent[1], -1)]
        for d in range(1, n_dp):
            value = hiddens[d][0]
            hiddens[d] = value, swap(after(value, ready, *arrived))
        later = [[(off, d) for off in near for d in range(1, n_dp)]]
        later.append([(off, d) for off in offsets for d in range(n_dp) if off not in near])
        for items in later:
            for at in range(0, len(items), 12):
                ready = work(sorted(items[at : at + 12], key=lambda item: item[1]), ready)

        carry = {}

        def hop_on(hop, *done):
            every = range(n_dp)
            if hop == half:
                values = [jnp.stack([parts[half, d] for d in every[:per]])]
                values.append(jnp.stack([parts[half, d] for d in every[per:]]))
            else:
                first, last = ((0, per), (per, n_dp)) if hop == half - 1 else ((0, n_dp), (0, n_dp))
                values = sums([([parts[hop, d] for d in every], carry[1], *first)])
                values += sums([([parts[-hop, d] for d in every], carry[-1], *last)])
            values = [after(value, *done) for value in values]
            carry[1] = ring_send(values[0], 1)
            carry[-1] = ring_send(values[1], -1)
            sending[:] = values
            return carry[1], carry[-1]

        sending = []
        hop_on(half)
        second = hop_on(half - 1)
        other = weight_product(
            [after(refs[0], *sending, *[sent[0] for sent in sent_back])] + refs[1:], layout, scaleds, 1, jnp.bfloat16, width
        )
        swapped = swap(after(other, *second, *[sent[-1] for sent in sent_back]))
        third = hop_on(half - 2, other)
        spread, spread_other = spread_product(
            [after(facts[0][0], *second)] + [fact[0] for fact in facts[1:]],
            [fact[1] for fact in facts],
            [own_back] + sent_back,
            slots,
        )
        hidden_grad = spread + swap(spread_other)
        hidden_grad = hidden_grad.reshape(cap, n_ex, ff).transpose(1, 0, 2)[None, None]
        for hop in range(half - 3, 0, -1):
            hop_on(hop, spread)
        weight_grad = weight_product(
            [after(refs[0], *third)] + refs[1:], layout, scaleds, 0, jnp.float32, width, swapped
        )
        totals = close([after(parts[0, 0], weight_grad)] + [parts[0, d] for d in range(1, n_dp)], carry[1], carry[-1])
        pieces = [totals[0]] + [shift(totals[d], -d) for d in range(1, n_dp)]
        layer_out, prob_grad = home(where, expert_ids.T, pieces, width, n_ex)
        return (layer_out, prob_grad.T, hidden_grad, weight_grad[None])

    return shards


def solution(mesh):
    placed = (
        P(("dp", "expert"), None),
        P(("dp", "expert"), None),
        P("dp", "expert", None, None, None),
        P("expert", None, "dp"),
        P(("dp", "expert"), None),
    )
    return jax.shard_map(
        body(chip_ring(mesh)),
        mesh=mesh,
        in_specs=placed,
        out_specs=(
            P(("dp", "expert"), None),
            P(("dp", "expert"), None),
            P("dp", "expert", None, None, None),
            P("expert", None, "dp"),
        ),
        check_vma=False,
    )
```

```python
import functools

import jax
import jax.numpy as jnp
import numpy as np
from jax import lax
from jax.experimental import pallas as pl
from jax.experimental.pallas import tpu as pltpu
from jax.sharding import PartitionSpec as P

MIB = 1024 * 1024


def kernel_memory(rows):
    return pltpu.CompilerParams(vmem_limit_bytes=(20 if rows <= 1024 else 48) * MIB)


def dot(a, b, ca, cb):
    return lax.dot_general(a, b, (((ca,), (cb,)), ((), ())), preferred_element_type=jnp.float32)


def after(value, *done):
    return lax.optimization_barrier((value, *done))[0]


def chip_ring(mesh):
    chips = mesh.shape["expert"] // 2
    devices = mesh.devices.reshape(mesh.shape["dp"], -1)
    if not hasattr(devices[0, 0], "coords"):
        return list(range(chips))
    at = [tuple(devices[0, 2 * chip].coords)[1:] for chip in range(chips)]
    rows = max(z for _, z in at) + 1
    cols = max(y for y, _ in at) + 1
    if rows * cols != chips or rows % 2:
        return list(range(chips))
    walk = [(0, z) for z in range(rows)]
    for step, z in enumerate(reversed(range(rows))):
        span = range(1, cols)
        walk += [(y, z) for y in (span if step % 2 == 0 else reversed(span))]
    return [at.index(place) for place in walk]


def pack_kernel(top, n_out, where, ids_in, probs_in, grads_in, *refs):
    outs, (ids, probs, grads, sems) = refs[:n_out], refs[n_out:]
    copies = [
        pltpu.make_async_copy(source, target, sems.at[i])
        for i, (source, target) in enumerate([(ids_in, ids), (probs_in, probs), (grads_in, grads)])
    ]
    for copy in copies:
        copy.start()
    for copy in copies:
        copy.wait()
    tok = grads.shape[0]
    width = grads.shape[1] // len(outs)
    room = outs[0].shape[1] - width
    row = lax.broadcasted_iota(jnp.int32, (tok, tok), 0)
    col = lax.broadcasted_iota(jnp.int32, (tok, tok), 1)
    same = (row == col).astype(jnp.float32)

    def columns(value):
        return lax.dot_general(
            same,
            value,
            (((1,), (1,)), ((), ())),
            precision=lax.Precision.HIGHEST,
            preferred_element_type=jnp.float32,
        )

    prob = columns(probs[...])
    high = prob.astype(jnp.bfloat16)
    middle = (prob - high.astype(jnp.float32)).astype(jnp.bfloat16)
    low = (prob - high.astype(jnp.float32) - middle.astype(jnp.float32)).astype(jnp.bfloat16)
    named = columns(ids[...].astype(jnp.float32)).astype(jnp.bfloat16)
    blank = jnp.zeros((tok, room - 4 * top), jnp.bfloat16)
    routes = jnp.concatenate([named, high, middle, low, blank], axis=1)
    for d, out in enumerate(outs):
        at = lax.rem(where[0] + d, len(outs)) * width
        out[:, :width] = grads[:, pl.ds(pl.multiple_of(at, 128), width)]
        out[:, width:] = routes


def pack(where, ids, probs, grads, n_dp, room):
    top, tok = ids.shape
    width = grads.shape[1] // n_dp
    vmem = pl.BlockSpec(memory_space=pltpu.VMEM)
    return pl.pallas_call(
        functools.partial(pack_kernel, top, n_dp),
        in_specs=[pl.BlockSpec(memory_space=pltpu.SMEM)] + [pl.BlockSpec(memory_space=pltpu.HBM)] * 3,
        out_specs=[vmem] * n_dp,
        out_shape=[jax.ShapeDtypeStruct((tok, width + room), jnp.bfloat16)] * n_dp,
        scratch_shapes=[
            pltpu.VMEM(ids.shape, ids.dtype),
            pltpu.VMEM(probs.shape, probs.dtype),
            pltpu.VMEM(grads.shape, grads.dtype),
            pltpu.SemaphoreType.DMA((3,)),
        ],
        compiler_params=kernel_memory(tok),
        name="pack",
    )(where, ids, probs, grads)


def sum_kernel(starts, n_out, *refs):
    outs = refs[-n_out:]
    at = 0
    for out, (n_rows, first, last, base) in zip(outs, starts):
        carry = refs[at + n_rows]
        for i in range(n_rows):
            value = refs[at + i][...]
            if first <= i < last:
                value = value.astype(jnp.float32) + carry[i - first + base].astype(jnp.float32)
            out[i] = value.astype(jnp.bfloat16)
        at += n_rows + 1


def sums(jobs):
    tok, full = jobs[0][0][0].shape
    flat, starts, shapes = [], [], []
    for parts, carry, first, last, base in jobs:
        flat += list(parts) + [carry]
        starts.append((len(parts), first, last, base))
        shapes.append(jax.ShapeDtypeStruct((len(parts), tok, full), jnp.bfloat16))
    vmem = pl.BlockSpec(memory_space=pltpu.VMEM)
    return pl.pallas_call(
        functools.partial(sum_kernel, tuple(starts), len(shapes)),
        in_specs=[vmem] * len(flat),
        out_specs=[vmem] * len(shapes),
        out_shape=shapes,
        compiler_params=kernel_memory(tok),
        name="sums",
    )(*flat)


def close_kernel(n_dp, *refs):
    parts, (one, two), outs = refs[:n_dp], refs[n_dp : n_dp + 2], refs[n_dp + 2 :]
    for d, out in enumerate(outs):
        value = parts[d][...].astype(jnp.float32) + one[d].astype(jnp.float32)
        out[...] = (value + two[d].astype(jnp.float32)).astype(jnp.bfloat16)


def close(parts, one, two):
    vmem = pl.BlockSpec(memory_space=pltpu.VMEM)
    return pl.pallas_call(
        functools.partial(close_kernel, len(parts)),
        in_specs=[vmem] * (len(parts) + 2),
        out_specs=[vmem] * len(parts),
        out_shape=[jax.ShapeDtypeStruct(part.shape, jnp.bfloat16) for part in parts],
        compiler_params=kernel_memory(parts[0].shape[0]),
        name="close",
    )(*parts, one, two)


def home_kernel(n_ex, where, ids, *refs):
    pieces, (layer, prob) = refs[:-2], refs[-2:]
    n_dp = len(pieces)
    top, tok = ids.shape
    width = layer.shape[1] // n_dp
    inner = jnp.zeros((tok, n_ex), jnp.float32)
    for d, piece in enumerate(pieces):
        at = lax.rem(where[0] + d, n_dp) * width
        layer[:, pl.ds(pl.multiple_of(at, 128), width)] = piece[:, :width]
        more = piece[:, width:].astype(jnp.float32)
        inner = inner + more[:, :n_ex] + more[:, n_ex : 2 * n_ex]
    row = lax.broadcasted_iota(jnp.int32, (n_ex, n_ex), 0)
    col = lax.broadcasted_iota(jnp.int32, (n_ex, n_ex), 1)
    inner = lax.dot_general(
        (row == col).astype(jnp.float32),
        inner,
        (((1,), (1,)), ((), ())),
        precision=lax.Precision.HIGHEST,
        preferred_element_type=jnp.float32,
    )
    row = lax.broadcasted_iota(jnp.int32, (n_ex, tok), 0)
    for k in range(top):
        mine = row == ids[k : k + 1, :]
        prob[k : k + 1, :] = jnp.sum(jnp.where(mine, inner, 0.0), axis=0, keepdims=True)


def home(where, ids, pieces, width, n_ex):
    top, tok = ids.shape
    vmem = pl.BlockSpec(memory_space=pltpu.VMEM)
    return pl.pallas_call(
        functools.partial(home_kernel, n_ex),
        in_specs=[pl.BlockSpec(memory_space=pltpu.SMEM)] + [vmem] * (1 + len(pieces)),
        out_specs=[vmem] * 2,
        out_shape=[
            jax.ShapeDtypeStruct((tok, len(pieces) * width), jnp.bfloat16),
            jax.ShapeDtypeStruct((top, tok), jnp.float32),
        ],
        compiler_params=kernel_memory(tok),
        name="home",
    )(where, ids, *pieces)


def block_kernel(plan, refs_in, n_dp, n_ex, top, *refs):
    meta = refs[0]
    blocks = refs[1 : 1 + refs_in]
    at = 1 + refs_in
    replicas = sorted({item[2] for item in plan})
    hid = {d: refs[at + 2 * i : at + 2 * i + 2] for i, d in enumerate(replicas)}
    at += 2 * len(replicas)
    weights = refs[at : at + 2]
    at += 2
    parts = refs[at : at + len(plan)]
    at += len(plan)
    outs = {d: refs[at + 2 * i : at + 2 * i + 2] for i, d in enumerate(replicas)}
    at += 2 * len(replicas)
    index, prob = refs[at : at + 2] if 0 in replicas else (None, None)

    _, tok, full = blocks[0].shape
    ff, width = weights[0].shape
    slots = hid[replicas[0]][0].shape[0]
    count = len(plan) * tok
    rows = [blocks[where][place] for where, place, _, _ in plan]
    routes = jnp.concatenate([row[:, width:] for row in rows], axis=0).astype(jnp.float32)
    named = routes[:, :top]
    chance = routes[:, top : 2 * top] + routes[:, 2 * top : 3 * top] + routes[:, 3 * top : 4 * top]
    row = lax.broadcasted_iota(jnp.int32, (tok, tok), 0)
    col = lax.broadcasted_iota(jnp.int32, (tok, tok), 1)
    earlier = (col < row).astype(jnp.float32)
    lane = lax.broadcasted_iota(jnp.int32, (tok, slots), 1)
    spans = {d: [i for i, item in enumerate(plan) if item[2] == d] for d in replicas}
    helds, scaleds = [], []
    for x in range(2):
        mine = named == meta[x].astype(jnp.float32)
        here = jnp.sum(jnp.where(mine, chance, 0.0), axis=1, keepdims=True)
        taken = jnp.broadcast_to((here > 0.0).astype(jnp.float32), (count, 128))
        held = []
        for d in replicas:
            picks = []
            for n, i in enumerate(spans[d]):
                span = slice(i * tok, (i + 1) * tok)
                position = dot(earlier, taken[span], 1, 0)[:, :1].astype(jnp.int32)
                slot = jnp.where(here[span] > 0.0, position * n_ex + meta[2 + plan[i][3]], -1)
                picks.append((lane == slot).astype(jnp.bfloat16))
                if d == 0:
                    index[n * tok : (n + 1) * tok, x : x + 1] = slot
                    prob[n * tok : (n + 1) * tok, x : x + 1] = here[span]
            held.append(dot(jnp.concatenate(picks, axis=0), hid[d][x][...], 1, 0))
        held = jnp.concatenate(held, axis=0)
        scaled = (held * here).astype(jnp.bfloat16)
        base = 0
        for d in replicas:
            size = len(spans[d]) * tok
            outs[d][0][x] = scaled[base : base + size]
            base += size
        helds.append(held)
        scaleds.append(scaled)

    tile = 512
    for step in range(width // tile):
        cols = slice(step * tile, (step + 1) * tile)
        value = dot(scaleds[0], weights[0][:, cols], 1, 0) + dot(scaleds[1], weights[1][:, cols], 1, 0)
        value = value.astype(jnp.bfloat16)
        for i, out in enumerate(parts):
            out[:, cols] = value[i * tok : (i + 1) * tok]

    lhs = jnp.concatenate([row[:, :width] for row in rows], axis=0)
    lane = lax.broadcasted_iota(jnp.int32, (count, full - width), 1)
    extra = jnp.zeros((count, full - width), jnp.float32)
    for x in range(2):
        inner = jnp.zeros((count, 1), jnp.float32)
        step_ff = 256
        for step in range(ff // step_ff):
            cols = slice(step * step_ff, (step + 1) * step_ff)
            value = dot(lhs, weights[x][cols, :], 1, 1)
            inner = inner + jnp.sum(value * helds[x][:, cols], axis=1, keepdims=True)
            value = value.astype(jnp.bfloat16)
            base = 0
            for d in replicas:
                size = len(spans[d]) * tok
                outs[d][1][x, :, cols] = value[base : base + size]
                base += size
        high = inner.astype(jnp.bfloat16).astype(jnp.float32)
        extra = jnp.where(lane == meta[x], high, extra)
        extra = jnp.where(lane == meta[x] + n_ex, inner - high, extra)
    extra = extra.astype(jnp.bfloat16)
    for i, out in enumerate(parts):
        out[:, width:] = extra[i * tok : (i + 1) * tok]


def block_product(plan, meta, blocks, hiddens, w_own, w_sib, n_ex, top):
    n_dp = len(hiddens)
    _, tok, full = blocks[0].shape
    ff, width = w_own.shape
    slots = hiddens[0][0].shape[0]
    replicas = sorted({item[2] for item in plan})
    vmem = pl.BlockSpec(memory_space=pltpu.VMEM)
    bf16 = lambda *shape: jax.ShapeDtypeStruct(shape, jnp.bfloat16)
    out_shape = [bf16(tok, full) for _ in plan]
    sizes = {d: tok * sum(item[2] == d for item in plan) for d in replicas}
    for d in replicas:
        out_shape += [bf16(2, sizes[d], ff)] * 2
    if 0 in replicas:
        out_shape.append(jax.ShapeDtypeStruct((sizes[0], 2), jnp.int32))
        out_shape.append(jax.ShapeDtypeStruct((sizes[0], 2), jnp.float32))
    hid = [value for d in replicas for value in hiddens[d]]
    count = len(plan) * tok
    chips_rows = n_ex * tok * n_dp // 2
    made = pl.pallas_call(
        functools.partial(block_kernel, plan, len(blocks), n_dp, n_ex, top),
        in_specs=[pl.BlockSpec(memory_space=pltpu.SMEM)] + [vmem] * (len(blocks) + len(hid) + 2),
        out_specs=[vmem] * len(out_shape),
        out_shape=out_shape,
        compiler_params=kernel_memory(chips_rows),
        cost_estimate=pl.CostEstimate(
            flops=8 * count * ff * width,
            bytes_accessed=4 * ff * width + 4 * count * (full + ff),
            transcendentals=0,
        ),
        name="block_product",
    )(meta, *blocks, *hid, w_own, w_sib)
    parts = made[: len(plan)]
    rest = made[len(plan) :]
    scaled = {d: rest[2 * i] for i, d in enumerate(replicas)}
    back = {d: rest[2 * i + 1] for i, d in enumerate(replicas)}
    return parts, scaled, back, rest[2 * len(replicas) :]


def spread_kernel(sizes, *refs):
    n_parts = len(sizes[0])
    index, prob = refs[:n_parts], refs[n_parts : 2 * n_parts]
    backs = list(refs[2 * n_parts : -2])
    outs = refs[-2:]
    slots = outs[0].shape[0]
    slot = jnp.concatenate([ref[...] for ref in index], axis=0)
    weight = jnp.concatenate([ref[...] for ref in prob], axis=0)
    lane = lax.broadcasted_iota(jnp.int32, (slot.shape[0], slots), 1)
    for x, out in enumerate(outs):
        back, at = None, 0
        for pieces in sizes:
            value = jnp.concatenate([ref[x] for ref in backs[at : at + len(pieces)]], axis=0)
            at += len(pieces)
            value = value.astype(jnp.float32)
            back = value if back is None else back + value
        pick = (lane == slot[:, x : x + 1]).astype(jnp.bfloat16)
        mine = (back * weight[:, x : x + 1]).astype(jnp.bfloat16)
        out[...] = dot(pick, mine, 0, 0).astype(jnp.bfloat16)


def spread_product(index, prob, backs, slots):
    sizes = [[part.shape[1] for part in parts] for parts in backs]
    ff = backs[0][0].shape[2]
    rows = sum(sizes[0])
    flat = [part for parts in backs for part in parts]
    vmem = pl.BlockSpec(memory_space=pltpu.VMEM)
    return pl.pallas_call(
        functools.partial(spread_kernel, sizes),
        in_specs=[vmem] * (2 * len(index) + len(flat)),
        out_specs=[vmem] * 2,
        out_shape=[jax.ShapeDtypeStruct((slots, ff), jnp.bfloat16)] * 2,
        compiler_params=kernel_memory(rows * len(backs)),
        cost_estimate=pl.CostEstimate(
            flops=4 * rows * slots * ff,
            bytes_accessed=4 * (1 + len(backs)) * rows * ff,
            transcendentals=0,
        ),
        name="spread_product",
    )(*index, *prob, *flat)


def weight_kernel(n_refs, n_scaled, layout, *refs):
    blocks, scaleds, more = refs[:n_refs], refs[n_refs : n_refs + n_scaled], refs[n_refs + n_scaled : -2]
    out, turned = refs[-2:]

    @pl.when(pl.program_id(0) == 0)
    def _():
        turned[...] = jnp.concatenate([ref[0] for ref in scaleds], axis=0).T

    rows = jnp.concatenate([blocks[where][place] for where, place in layout], axis=0)
    total = dot(turned[...], rows, 1, 0)
    for ref in more:
        total = total + ref[...].astype(jnp.float32)
    out[...] = total.astype(out.dtype)


def weight_product(blocks, layout, scaleds, x, dtype, width, *more):
    tok = blocks[0].shape[1]
    ff = scaleds[0].shape[2]
    rows = len(layout) * tok
    tile = 512 if width >= 2048 else 256
    return pl.pallas_call(
        functools.partial(weight_kernel, len(blocks), len(scaleds), layout),
        grid=(width // tile,),
        in_specs=[pl.BlockSpec(block.shape[:2] + (tile,), lambda i: (0, 0, i)) for block in blocks]
        + [
            pl.BlockSpec((1,) + value.shape[1:], lambda i: (x, 0, 0), pipeline_mode=pl.Buffered(1))
            for value in scaleds
        ]
        + [pl.BlockSpec((ff, tile), lambda i: (0, i)) for _ in more],
        out_specs=pl.BlockSpec((ff, tile), lambda i: (0, i)),
        out_shape=jax.ShapeDtypeStruct((ff, width), dtype),
        scratch_shapes=[pltpu.VMEM((ff, rows), jnp.bfloat16)],
        compiler_params=kernel_memory(rows),
        cost_estimate=pl.CostEstimate(
            flops=2 * rows * width * ff,
            bytes_accessed=2 * rows * (width + ff) + 4 * ff * width,
            transcendentals=0,
        ),
        name="weight_product",
    )(*blocks, *scaleds, *more)


def body(ring):
    chips = len(ring)
    half = chips // 2
    offsets = [0]
    for step in range(1, half):
        offsets += [-step, step]
    offsets.append(half)
    place_of = {chip: at for at, chip in enumerate(ring)}
    meta_table = np.asarray(
        [
            [e, e ^ 1] + [2 * ring[(place_of[e // 2] + off) % chips] + e % 2 for off in offsets]
            for e in range(2 * chips)
        ],
        np.int32,
    )

    def along(step):
        return [
            (2 * ring[at] + core, 2 * ring[(at + step) % chips] + core)
            for at in range(chips)
            for core in range(2)
        ]

    forward, backward = along(1), along(-1)
    sibling = [(e, e ^ 1) for e in range(2 * chips)]

    def shards(expert_ids, route_probs, expert_hidden, down_weight, out_grad):
        tok, top = expert_ids.shape
        n_dp = lax.axis_size("dp")
        n_ex = lax.axis_size("expert")
        cap = expert_hidden.shape[3]
        slots = cap * n_ex
        ff = down_weight.shape[1]
        width = down_weight.shape[2]
        weight = down_weight[0]
        replica = lax.axis_index("dp")
        expert = lax.axis_index("expert")
        per = n_dp // 2
        meta = lax.dynamic_index_in_dim(jnp.asarray(meta_table), expert, 0, keepdims=False)

        def shift(value, step):
            return lax.ppermute(value, "dp", [(i, (i + step) % n_dp) for i in range(n_dp)])

        def ring_send(value, step):
            return lax.ppermute(value, "expert", forward if step > 0 else backward)

        def swap(value):
            return lax.ppermute(value, "expert", sibling)

        room = 128 * -(-max(4 * top, 2 * n_ex) // 128)
        where = replica.reshape(1).astype(jnp.int32)
        packed = pack(where, expert_ids.T, route_probs.T, out_grad, n_dp, room)
        seeds = [packed[0]] + [shift(packed[d], d) for d in range(1, n_dp)]
        blocks = {0: [jnp.stack(seeds[:per]), jnp.stack(seeds[per:])]}
        halves = {step: [ring_send(value, step) for value in blocks[0]] for step in (1, -1)}
        halves[1][1] = after(halves[1][1], meta)

        sibling_weight = swap(weight)
        hidden = expert_hidden[0, 0].transpose(1, 0, 2).reshape(slots, ff)
        hiddens = [(hidden, swap(hidden))]
        for d in range(1, n_dp):
            value = shift(after(hidden, *seeds[1:], halves[1][0], halves[-1][0]), d)
            hiddens.append((value, None))

        parts, scaleds, layout, facts = {}, [], [], []
        own_back, sent_back = [], [[] for _ in range(1, n_dp)]
        refs = []

        def work(items, *done):
            used, plan = [], []
            for off, d in items:
                value = blocks[off][d // per] if off in (0, half) else blocks[off]
                if not any(value is other for other in used):
                    used.append(value)
                where = [value is other for other in used].index(True)
                plan.append((where, d % per if off in (0, half) else d, d, offsets.index(off)))
            if done:
                gated = [after(used[0], *done)] + used[1:]
            else:
                gated = used
            made, scaled, back, fact = block_product(
                tuple(plan), meta, gated, hiddens, weight, sibling_weight, n_ex, top
            )
            for item, part in zip(items, made):
                parts[item] = part
            for d in sorted(scaled):
                scaleds.append(scaled[d])
                for (off, e), (where, place, _, _) in zip(items, plan):
                    if e == d:
                        if not any(used[where] is other for other in refs):
                            refs.append(used[where])
                        layout.append(([used[where] is other for other in refs].index(True), place))
                if d == 0:
                    own_back.append(back[0])
                    facts.append(fact)
                    continue
                sent_back[d - 1].append(shift(after(back[d], *blocks.get(half, ())), -d))
            return made[0]

        near = offsets[: 2 * min(2, half - 1) + 1]
        for step in range(1, half):
            if step == 1:
                blocks[-1] = jnp.concatenate(halves[1], axis=0)
                blocks[1] = jnp.concatenate(halves[-1], axis=0)
            else:
                blocks[-step] = ring_send(blocks[1 - step], 1)
                blocks[step] = ring_send(blocks[step - 1], -1)
            if step == min(2, half - 1):
                ready = work([(off, 0) for off in near])
        arrived = blocks[1 - half], blocks[half - 1]
        sent = after(arrived[0], ready)[:per], after(arrived[1], ready)[per:]
        blocks[half] = [ring_send(sent[0], 1), ring_send(sent[1], -1)]
        for d in range(1, n_dp):
            value = hiddens[d][0]
            hiddens[d] = value, swap(after(value, ready, *arrived))
        later = [[(off, d) for off in near for d in range(1, n_dp)]]
        later.append([(off, d) for off in offsets for d in range(n_dp) if off not in near])
        for items in later:
            for at in range(0, len(items), 12):
                ready = work(sorted(items[at : at + 12], key=lambda item: item[1]), ready)

        carry = {}

        def hop_on(hop, *done):
            every = range(n_dp)
            if hop == half:
                values = [jnp.stack([parts[half, d] for d in every[:per]])]
                values.append(jnp.stack([parts[half, d] for d in every[per:]]))
            else:
                first, last = ((0, per), (per, n_dp)) if hop == half - 1 else ((0, n_dp), (0, n_dp))
                values = sums([([parts[hop, d] for d in every], carry[1], *first, 0)])
                values += sums([([parts[-hop, d] for d in every], carry[-1], *last, 0)])
            values = [after(value, *done) for value in values]
            carry[1] = ring_send(values[0], 1)
            carry[-1] = ring_send(values[1], -1)
            sending[:] = values
            return carry[1], carry[-1]

        sending = []
        hop_on(half)
        second = hop_on(half - 1)
        other = weight_product(
            [after(refs[0], *sending, *[sent[0] for sent in sent_back])] + refs[1:], layout, scaleds, 1, jnp.bfloat16, width
        )
        swapped = swap(after(other, *second, *[sent[-1] for sent in sent_back]))
        third = hop_on(half - 2, other)
        weight_grad = weight_product(
            [after(refs[0], *sending)] + refs[1:], layout, scaleds, 0, jnp.float32, width, swapped
        )
        spread, spread_other = spread_product(
            [after(facts[0][0], *second, weight_grad)] + [fact[0] for fact in facts[1:]],
            [fact[1] for fact in facts],
            [own_back] + sent_back,
            slots,
        )
        hidden_grad = spread + swap(after(spread_other, *third))
        hidden_grad = hidden_grad.reshape(cap, n_ex, ff).transpose(1, 0, 2)[None, None]
        for hop in range(half - 3, 1, -1):
            hop_on(hop, spread)

        groups = [range(per, n_dp), range(per)]
        ends = {}
        for direction in (1, -1):
            jobs = [([parts[direction, d] for d in g], carry[direction], 0, len(g), g[0]) for g in groups]
            ends[direction] = [ring_send(after(value, spread), direction) for value in sums(jobs)]
        pieces = {}
        for i, group in enumerate(groups):
            totals = close([parts[0, d] for d in group], ends[1][i], ends[-1][i])
            for d, total in zip(group, totals):
                pieces[d] = total if d == 0 else shift(total, -d)
        layer_out, prob_grad = home(where, after(expert_ids.T, hidden_grad), [pieces[d] for d in range(n_dp)], width, n_ex)
        return (layer_out, prob_grad.T, hidden_grad, weight_grad[None])

    return shards


def solution(mesh):
    placed = (
        P(("dp", "expert"), None),
        P(("dp", "expert"), None),
        P("dp", "expert", None, None, None),
        P("expert", None, "dp"),
        P(("dp", "expert"), None),
    )
    return jax.shard_map(
        body(chip_ring(mesh)),
        mesh=mesh,
        in_specs=placed,
        out_specs=(
            P(("dp", "expert"), None),
            P(("dp", "expert"), None),
            P("dp", "expert", None, None, None),
            P("expert", None, "dp"),
        ),
        check_vma=False,
    )
```

```python
import functools

import jax
import jax.numpy as jnp
import numpy as np
from jax import lax
from jax.experimental import pallas as pl
from jax.experimental.pallas import tpu as pltpu
from jax.sharding import PartitionSpec as P

MIB = 1024 * 1024


def kernel_memory(rows):
    return pltpu.CompilerParams(vmem_limit_bytes=(20 if rows <= 1024 else 48) * MIB)


def dot(a, b, ca, cb):
    return lax.dot_general(a, b, (((ca,), (cb,)), ((), ())), preferred_element_type=jnp.float32)


def after(value, *done):
    return lax.optimization_barrier((value, *done))[0]


def chip_ring(mesh):
    chips = mesh.shape["expert"] // 2
    devices = mesh.devices.reshape(mesh.shape["dp"], -1)
    if not hasattr(devices[0, 0], "coords"):
        return list(range(chips))
    at = [tuple(devices[0, 2 * chip].coords)[1:] for chip in range(chips)]
    rows = max(z for _, z in at) + 1
    cols = max(y for y, _ in at) + 1
    if rows * cols != chips or rows % 2:
        return list(range(chips))
    walk = [(0, z) for z in range(rows)]
    for step, z in enumerate(reversed(range(rows))):
        span = range(1, cols)
        walk += [(y, z) for y in (span if step % 2 == 0 else reversed(span))]
    return [at.index(place) for place in walk]


def pack_kernel(top, n_out, where, ids_in, probs_in, grads_in, *refs):
    outs, (ids, probs, grads, sems) = refs[:n_out], refs[n_out:]
    copies = [
        pltpu.make_async_copy(source, target, sems.at[i])
        for i, (source, target) in enumerate([(ids_in, ids), (probs_in, probs), (grads_in, grads)])
    ]
    for copy in copies:
        copy.start()
    for copy in copies:
        copy.wait()
    tok = grads.shape[0]
    width = grads.shape[1] // len(outs)
    room = outs[0].shape[1] - width
    row = lax.broadcasted_iota(jnp.int32, (tok, tok), 0)
    col = lax.broadcasted_iota(jnp.int32, (tok, tok), 1)
    same = (row == col).astype(jnp.float32)

    def columns(value):
        return lax.dot_general(
            same,
            value,
            (((1,), (1,)), ((), ())),
            precision=lax.Precision.HIGHEST,
            preferred_element_type=jnp.float32,
        )

    prob = columns(probs[...])
    high = prob.astype(jnp.bfloat16)
    middle = (prob - high.astype(jnp.float32)).astype(jnp.bfloat16)
    low = (prob - high.astype(jnp.float32) - middle.astype(jnp.float32)).astype(jnp.bfloat16)
    named = columns(ids[...].astype(jnp.float32)).astype(jnp.bfloat16)
    blank = jnp.zeros((tok, room - 4 * top), jnp.bfloat16)
    routes = jnp.concatenate([named, high, middle, low, blank], axis=1)
    for d, out in enumerate(outs):
        at = lax.rem(where[0] + d, len(outs)) * width
        out[:, :width] = grads[:, pl.ds(pl.multiple_of(at, 128), width)]
        out[:, width:] = routes


def pack(where, ids, probs, grads, n_dp, room):
    top, tok = ids.shape
    width = grads.shape[1] // n_dp
    vmem = pl.BlockSpec(memory_space=pltpu.VMEM)
    return pl.pallas_call(
        functools.partial(pack_kernel, top, n_dp),
        in_specs=[pl.BlockSpec(memory_space=pltpu.SMEM)] + [pl.BlockSpec(memory_space=pltpu.HBM)] * 3,
        out_specs=[vmem] * n_dp,
        out_shape=[jax.ShapeDtypeStruct((tok, width + room), jnp.bfloat16)] * n_dp,
        scratch_shapes=[
            pltpu.VMEM(ids.shape, ids.dtype),
            pltpu.VMEM(probs.shape, probs.dtype),
            pltpu.VMEM(grads.shape, grads.dtype),
            pltpu.SemaphoreType.DMA((3,)),
        ],
        compiler_params=kernel_memory(tok),
        name="pack",
    )(where, ids, probs, grads)


def sum_kernel(starts, n_out, *refs):
    outs = refs[-n_out:]
    at = 0
    for out, (n_rows, first, last, base) in zip(outs, starts):
        carry = refs[at + n_rows]
        for i in range(n_rows):
            value = refs[at + i][...]
            if first <= i < last:
                value = value.astype(jnp.float32) + carry[i - first + base].astype(jnp.float32)
            out[i] = value.astype(jnp.bfloat16)
        at += n_rows + 1


def sums(jobs):
    tok, full = jobs[0][0][0].shape
    flat, starts, shapes = [], [], []
    for parts, carry, first, last, base in jobs:
        flat += list(parts) + [carry]
        starts.append((len(parts), first, last, base))
        shapes.append(jax.ShapeDtypeStruct((len(parts), tok, full), jnp.bfloat16))
    vmem = pl.BlockSpec(memory_space=pltpu.VMEM)
    return pl.pallas_call(
        functools.partial(sum_kernel, tuple(starts), len(shapes)),
        in_specs=[vmem] * len(flat),
        out_specs=[vmem] * len(shapes),
        out_shape=shapes,
        compiler_params=kernel_memory(tok),
        name="sums",
    )(*flat)


def close_kernel(n_dp, *refs):
    parts, (one, two), outs = refs[:n_dp], refs[n_dp : n_dp + 2], refs[n_dp + 2 :]
    for d, out in enumerate(outs):
        value = parts[d][...].astype(jnp.float32) + one[d].astype(jnp.float32)
        out[...] = (value + two[d].astype(jnp.float32)).astype(jnp.bfloat16)


def close(parts, one, two):
    vmem = pl.BlockSpec(memory_space=pltpu.VMEM)
    return pl.pallas_call(
        functools.partial(close_kernel, len(parts)),
        in_specs=[vmem] * (len(parts) + 2),
        out_specs=[vmem] * len(parts),
        out_shape=[jax.ShapeDtypeStruct(part.shape, jnp.bfloat16) for part in parts],
        compiler_params=kernel_memory(parts[0].shape[0]),
        name="close",
    )(*parts, one, two)


def home_kernel(n_ex, where, ids, *refs):
    pieces, (layer, prob) = refs[:-2], refs[-2:]
    n_dp = len(pieces)
    top, tok = ids.shape
    width = layer.shape[1] // n_dp
    inner = jnp.zeros((tok, n_ex), jnp.float32)
    for d, piece in enumerate(pieces):
        at = lax.rem(where[0] + d, n_dp) * width
        layer[:, pl.ds(pl.multiple_of(at, 128), width)] = piece[:, :width]
        more = piece[:, width:].astype(jnp.float32)
        inner = inner + more[:, :n_ex] + more[:, n_ex : 2 * n_ex]
    row = lax.broadcasted_iota(jnp.int32, (n_ex, n_ex), 0)
    col = lax.broadcasted_iota(jnp.int32, (n_ex, n_ex), 1)
    inner = lax.dot_general(
        (row == col).astype(jnp.float32),
        inner,
        (((1,), (1,)), ((), ())),
        precision=lax.Precision.HIGHEST,
        preferred_element_type=jnp.float32,
    )
    row = lax.broadcasted_iota(jnp.int32, (n_ex, tok), 0)
    for k in range(top):
        mine = row == ids[k : k + 1, :]
        prob[k : k + 1, :] = jnp.sum(jnp.where(mine, inner, 0.0), axis=0, keepdims=True)


def home(where, ids, pieces, width, n_ex):
    top, tok = ids.shape
    vmem = pl.BlockSpec(memory_space=pltpu.VMEM)
    return pl.pallas_call(
        functools.partial(home_kernel, n_ex),
        in_specs=[pl.BlockSpec(memory_space=pltpu.SMEM)] + [vmem] * (1 + len(pieces)),
        out_specs=[vmem] * 2,
        out_shape=[
            jax.ShapeDtypeStruct((tok, len(pieces) * width), jnp.bfloat16),
            jax.ShapeDtypeStruct((top, tok), jnp.float32),
        ],
        compiler_params=kernel_memory(tok),
        name="home",
    )(where, ids, *pieces)


def block_kernel(plan, refs_in, n_dp, n_ex, top, *refs):
    meta = refs[0]
    blocks = refs[1 : 1 + refs_in]
    at = 1 + refs_in
    replicas = sorted({item[2] for item in plan})
    hid = {d: refs[at + 2 * i : at + 2 * i + 2] for i, d in enumerate(replicas)}
    at += 2 * len(replicas)
    weights = refs[at : at + 2]
    at += 2
    parts = refs[at : at + len(plan)]
    at += len(plan)
    outs = {d: refs[at + 2 * i : at + 2 * i + 2] for i, d in enumerate(replicas)}
    at += 2 * len(replicas)
    index, prob = refs[at : at + 2] if 0 in replicas else (None, None)

    _, tok, full = blocks[0].shape
    ff, width = weights[0].shape
    slots = hid[replicas[0]][0].shape[0]
    count = len(plan) * tok
    rows = [blocks[where][place] for where, place, _, _ in plan]
    routes = jnp.concatenate([row[:, width:] for row in rows], axis=0).astype(jnp.float32)
    named = routes[:, :top]
    chance = routes[:, top : 2 * top] + routes[:, 2 * top : 3 * top] + routes[:, 3 * top : 4 * top]
    row = lax.broadcasted_iota(jnp.int32, (tok, tok), 0)
    col = lax.broadcasted_iota(jnp.int32, (tok, tok), 1)
    earlier = (col < row).astype(jnp.float32)
    lane = lax.broadcasted_iota(jnp.int32, (tok, slots), 1)
    spans = {d: [i for i, item in enumerate(plan) if item[2] == d] for d in replicas}
    helds, scaleds = [], []
    for x in range(2):
        mine = named == meta[x].astype(jnp.float32)
        here = jnp.sum(jnp.where(mine, chance, 0.0), axis=1, keepdims=True)
        taken = jnp.broadcast_to((here > 0.0).astype(jnp.float32), (count, 128))
        held = []
        for d in replicas:
            picks = []
            for n, i in enumerate(spans[d]):
                span = slice(i * tok, (i + 1) * tok)
                position = dot(earlier, taken[span], 1, 0)[:, :1].astype(jnp.int32)
                slot = jnp.where(here[span] > 0.0, position * n_ex + meta[2 + plan[i][3]], -1)
                picks.append((lane == slot).astype(jnp.bfloat16))
                if d == 0:
                    index[n * tok : (n + 1) * tok, x : x + 1] = slot
                    prob[n * tok : (n + 1) * tok, x : x + 1] = here[span]
            held.append(dot(jnp.concatenate(picks, axis=0), hid[d][x][...], 1, 0))
        held = jnp.concatenate(held, axis=0)
        scaled = (held * here).astype(jnp.bfloat16)
        base = 0
        for d in replicas:
            size = len(spans[d]) * tok
            outs[d][0][x] = scaled[base : base + size]
            base += size
        helds.append(held)
        scaleds.append(scaled)

    tile = 512
    for step in range(width // tile):
        cols = slice(step * tile, (step + 1) * tile)
        value = dot(scaleds[0], weights[0][:, cols], 1, 0) + dot(scaleds[1], weights[1][:, cols], 1, 0)
        value = value.astype(jnp.bfloat16)
        for i, out in enumerate(parts):
            out[:, cols] = value[i * tok : (i + 1) * tok]

    lhs = jnp.concatenate([row[:, :width] for row in rows], axis=0)
    lane = lax.broadcasted_iota(jnp.int32, (count, full - width), 1)
    extra = jnp.zeros((count, full - width), jnp.float32)
    for x in range(2):
        inner = jnp.zeros((count, 1), jnp.float32)
        step_ff = 256
        for step in range(ff // step_ff):
            cols = slice(step * step_ff, (step + 1) * step_ff)
            value = dot(lhs, weights[x][cols, :], 1, 1)
            inner = inner + jnp.sum(value * helds[x][:, cols], axis=1, keepdims=True)
            value = value.astype(jnp.bfloat16)
            base = 0
            for d in replicas:
                size = len(spans[d]) * tok
                outs[d][1][x, :, cols] = value[base : base + size]
                base += size
        high = inner.astype(jnp.bfloat16).astype(jnp.float32)
        extra = jnp.where(lane == meta[x], high, extra)
        extra = jnp.where(lane == meta[x] + n_ex, inner - high, extra)
    extra = extra.astype(jnp.bfloat16)
    for i, out in enumerate(parts):
        out[:, width:] = extra[i * tok : (i + 1) * tok]


def block_product(plan, meta, blocks, hiddens, w_own, w_sib, n_ex, top):
    n_dp = len(hiddens)
    _, tok, full = blocks[0].shape
    ff, width = w_own.shape
    slots = hiddens[0][0].shape[0]
    replicas = sorted({item[2] for item in plan})
    vmem = pl.BlockSpec(memory_space=pltpu.VMEM)
    bf16 = lambda *shape: jax.ShapeDtypeStruct(shape, jnp.bfloat16)
    out_shape = [bf16(tok, full) for _ in plan]
    sizes = {d: tok * sum(item[2] == d for item in plan) for d in replicas}
    for d in replicas:
        out_shape += [bf16(2, sizes[d], ff)] * 2
    if 0 in replicas:
        out_shape.append(jax.ShapeDtypeStruct((sizes[0], 2), jnp.int32))
        out_shape.append(jax.ShapeDtypeStruct((sizes[0], 2), jnp.float32))
    hid = [value for d in replicas for value in hiddens[d]]
    count = len(plan) * tok
    chips_rows = n_ex * tok * n_dp // 2
    made = pl.pallas_call(
        functools.partial(block_kernel, plan, len(blocks), n_dp, n_ex, top),
        in_specs=[pl.BlockSpec(memory_space=pltpu.SMEM)] + [vmem] * (len(blocks) + len(hid) + 2),
        out_specs=[vmem] * len(out_shape),
        out_shape=out_shape,
        compiler_params=kernel_memory(chips_rows),
        cost_estimate=pl.CostEstimate(
            flops=8 * count * ff * width,
            bytes_accessed=4 * ff * width + 4 * count * (full + ff),
            transcendentals=0,
        ),
        name="block_product",
    )(meta, *blocks, *hid, w_own, w_sib)
    parts = made[: len(plan)]
    rest = made[len(plan) :]
    scaled = {d: rest[2 * i] for i, d in enumerate(replicas)}
    back = {d: rest[2 * i + 1] for i, d in enumerate(replicas)}
    return parts, scaled, back, rest[2 * len(replicas) :]


def spread_kernel(sizes, *refs):
    n_parts = len(sizes[0])
    index, prob = refs[:n_parts], refs[n_parts : 2 * n_parts]
    backs = list(refs[2 * n_parts : -2])
    outs = refs[-2:]
    slots = outs[0].shape[0]
    slot = jnp.concatenate([ref[...] for ref in index], axis=0)
    weight = jnp.concatenate([ref[...] for ref in prob], axis=0)
    lane = lax.broadcasted_iota(jnp.int32, (slot.shape[0], slots), 1)
    for x, out in enumerate(outs):
        back, at = None, 0
        for pieces in sizes:
            value = jnp.concatenate([ref[x] for ref in backs[at : at + len(pieces)]], axis=0)
            at += len(pieces)
            value = value.astype(jnp.float32)
            back = value if back is None else back + value
        pick = (lane == slot[:, x : x + 1]).astype(jnp.bfloat16)
        mine = (back * weight[:, x : x + 1]).astype(jnp.bfloat16)
        out[...] = dot(pick, mine, 0, 0).astype(jnp.bfloat16)


def spread_product(index, prob, backs, slots):
    sizes = [[part.shape[1] for part in parts] for parts in backs]
    ff = backs[0][0].shape[2]
    rows = sum(sizes[0])
    flat = [part for parts in backs for part in parts]
    vmem = pl.BlockSpec(memory_space=pltpu.VMEM)
    return pl.pallas_call(
        functools.partial(spread_kernel, sizes),
        in_specs=[vmem] * (2 * len(index) + len(flat)),
        out_specs=[vmem] * 2,
        out_shape=[jax.ShapeDtypeStruct((slots, ff), jnp.bfloat16)] * 2,
        compiler_params=kernel_memory(rows * len(backs)),
        cost_estimate=pl.CostEstimate(
            flops=4 * rows * slots * ff,
            bytes_accessed=4 * (1 + len(backs)) * rows * ff,
            transcendentals=0,
        ),
        name="spread_product",
    )(*index, *prob, *flat)


def weight_kernel(n_refs, n_scaled, layout, *refs):
    blocks, scaleds, more = refs[:n_refs], refs[n_refs : n_refs + n_scaled], refs[n_refs + n_scaled : -2]
    out, turned = refs[-2:]

    @pl.when(pl.program_id(0) == 0)
    def _():
        turned[...] = jnp.concatenate([ref[0] for ref in scaleds], axis=0).T

    rows = jnp.concatenate([blocks[where][place] for where, place in layout], axis=0)
    total = dot(turned[...], rows, 1, 0)
    for ref in more:
        total = total + ref[...].astype(jnp.float32)
    out[...] = total.astype(out.dtype)


def weight_product(blocks, layout, scaleds, x, dtype, width, *more):
    tok = blocks[0].shape[1]
    ff = scaleds[0].shape[2]
    rows = len(layout) * tok
    tile = 512 if width >= 2048 else 256
    return pl.pallas_call(
        functools.partial(weight_kernel, len(blocks), len(scaleds), layout),
        grid=(width // tile,),
        in_specs=[pl.BlockSpec(block.shape[:2] + (tile,), lambda i: (0, 0, i)) for block in blocks]
        + [
            pl.BlockSpec((1,) + value.shape[1:], lambda i: (x, 0, 0), pipeline_mode=pl.Buffered(1))
            for value in scaleds
        ]
        + [pl.BlockSpec((ff, tile), lambda i: (0, i)) for _ in more],
        out_specs=pl.BlockSpec((ff, tile), lambda i: (0, i)),
        out_shape=jax.ShapeDtypeStruct((ff, width), dtype),
        scratch_shapes=[pltpu.VMEM((ff, rows), jnp.bfloat16)],
        compiler_params=kernel_memory(rows),
        cost_estimate=pl.CostEstimate(
            flops=2 * rows * width * ff,
            bytes_accessed=2 * rows * (width + ff) + 4 * ff * width,
            transcendentals=0,
        ),
        name="weight_product",
    )(*blocks, *scaleds, *more)


def body(ring):
    chips = len(ring)
    half = chips // 2
    offsets = [0]
    for step in range(1, half):
        offsets += [-step, step]
    offsets.append(half)
    place_of = {chip: at for at, chip in enumerate(ring)}
    meta_table = np.asarray(
        [
            [e, e ^ 1] + [2 * ring[(place_of[e // 2] + off) % chips] + e % 2 for off in offsets]
            for e in range(2 * chips)
        ],
        np.int32,
    )

    def along(step):
        return [
            (2 * ring[at] + core, 2 * ring[(at + step) % chips] + core)
            for at in range(chips)
            for core in range(2)
        ]

    forward, backward = along(1), along(-1)
    sibling = [(e, e ^ 1) for e in range(2 * chips)]

    def shards(expert_ids, route_probs, expert_hidden, down_weight, out_grad):
        tok, top = expert_ids.shape
        n_dp = lax.axis_size("dp")
        n_ex = lax.axis_size("expert")
        cap = expert_hidden.shape[3]
        slots = cap * n_ex
        ff = down_weight.shape[1]
        width = down_weight.shape[2]
        weight = down_weight[0]
        replica = lax.axis_index("dp")
        expert = lax.axis_index("expert")
        per = n_dp // 2
        meta = lax.dynamic_index_in_dim(jnp.asarray(meta_table), expert, 0, keepdims=False)

        def shift(value, step):
            return lax.ppermute(value, "dp", [(i, (i + step) % n_dp) for i in range(n_dp)])

        def ring_send(value, step):
            return lax.ppermute(value, "expert", forward if step > 0 else backward)

        def swap(value):
            return lax.ppermute(value, "expert", sibling)

        room = 128 * -(-max(4 * top, 2 * n_ex) // 128)
        where = replica.reshape(1).astype(jnp.int32)
        packed = pack(where, expert_ids.T, route_probs.T, out_grad, n_dp, room)
        seeds = [packed[0]] + [shift(packed[d], d) for d in range(1, n_dp)]
        blocks = {0: [jnp.stack(seeds[:per]), jnp.stack(seeds[per:])]}
        halves = {step: [ring_send(value, step) for value in blocks[0]] for step in (1, -1)}
        halves[1][1] = after(halves[1][1], meta)

        sibling_weight = swap(weight)
        hidden = expert_hidden[0, 0].transpose(1, 0, 2).reshape(slots, ff)
        hiddens = [(hidden, swap(hidden))]
        for d in range(1, n_dp):
            value = shift(after(hidden, *seeds[1:], halves[1][0], halves[-1][0]), d)
            hiddens.append((value, None))

        parts, scaleds, layout, facts = {}, [], [], []
        own_back, sent_back = [], [[] for _ in range(1, n_dp)]
        refs = []

        def work(items, *done):
            used, plan = [], []
            for off, d in items:
                value = blocks[off][d // per] if off in (0, half) else blocks[off]
                if not any(value is other for other in used):
                    used.append(value)
                where = [value is other for other in used].index(True)
                plan.append((where, d % per if off in (0, half) else d, d, offsets.index(off)))
            if done:
                gated = [after(used[0], *done)] + used[1:]
            else:
                gated = used
            made, scaled, back, fact = block_product(
                tuple(plan), meta, gated, hiddens, weight, sibling_weight, n_ex, top
            )
            for item, part in zip(items, made):
                parts[item] = part
            for d in sorted(scaled):
                scaleds.append(scaled[d])
                for (off, e), (where, place, _, _) in zip(items, plan):
                    if e == d:
                        if not any(used[where] is other for other in refs):
                            refs.append(used[where])
                        layout.append(([used[where] is other for other in refs].index(True), place))
                if d == 0:
                    own_back.append(back[0])
                    facts.append(fact)
                    continue
                sent_back[d - 1].append(shift(after(back[d], *blocks.get(half, ())), -d))
            return made[0]

        near = offsets[: 2 * min(2, half - 1) + 1]
        for step in range(1, half):
            if step == 1:
                blocks[-1] = jnp.concatenate(halves[1], axis=0)
                blocks[1] = jnp.concatenate(halves[-1], axis=0)
            else:
                blocks[-step] = ring_send(blocks[1 - step], 1)
                blocks[step] = ring_send(blocks[step - 1], -1)
            if step == min(2, half - 1):
                ready = work([(off, 0) for off in near])
        arrived = blocks[1 - half], blocks[half - 1]
        sent = after(arrived[0], ready)[:per], after(arrived[1], ready)[per:]
        blocks[half] = [ring_send(sent[0], 1), ring_send(sent[1], -1)]
        for d in range(1, n_dp):
            value = hiddens[d][0]
            hiddens[d] = value, swap(after(value, ready, *arrived))
        later = [[(off, d) for off in near for d in range(1, n_dp)]]
        later.append([(off, d) for off in offsets for d in range(n_dp) if off not in near])
        for items in later:
            for at in range(0, len(items), 12):
                ready = work(sorted(items[at : at + 12], key=lambda item: item[1]), ready)

        carry = {}

        def hop_on(hop, *done):
            every = range(n_dp)
            if hop == half:
                values = [jnp.stack([parts[half, d] for d in every[:per]])]
                values.append(jnp.stack([parts[half, d] for d in every[per:]]))
            else:
                first, last = ((0, per), (per, n_dp)) if hop == half - 1 else ((0, n_dp), (0, n_dp))
                values = sums([([parts[hop, d] for d in every], carry[1], *first, 0)])
                values += sums([([parts[-hop, d] for d in every], carry[-1], *last, 0)])
            values = [after(value, *done) for value in values]
            carry[1] = ring_send(values[0], 1)
            carry[-1] = ring_send(values[1], -1)
            sending[:] = values
            return carry[1], carry[-1]

        sending = []
        hop_on(half)
        second = hop_on(half - 1)
        other = weight_product(
            [after(refs[0], *sending, *[sent[0] for sent in sent_back])] + refs[1:], layout, scaleds, 1, jnp.bfloat16, width
        )
        swapped = swap(after(other, *second, *[sent[-1] for sent in sent_back]))
        third = hop_on(half - 2, other)
        spread, spread_other = spread_product(
            [after(facts[0][0], *second, *sending)] + [fact[0] for fact in facts[1:]],
            [fact[1] for fact in facts],
            [own_back] + sent_back,
            slots,
        )
        weight_grad = weight_product(
            [after(refs[0], spread)] + refs[1:], layout, scaleds, 0, jnp.float32, width, swapped
        )
        hidden_grad = spread + swap(after(spread_other, *third, weight_grad))
        hidden_grad = hidden_grad.reshape(cap, n_ex, ff).transpose(1, 0, 2)[None, None]
        for hop in range(half - 3, 1, -1):
            hop_on(hop, spread)

        groups = [range(per, n_dp), range(per)]
        ends = {}
        for direction in (1, -1):
            jobs = [([parts[direction, d] for d in g], carry[direction], 0, len(g), g[0]) for g in groups]
            ends[direction] = [ring_send(after(value, weight_grad), direction) for value in sums(jobs)]
        pieces = {}
        for i, group in enumerate(groups):
            totals = close([parts[0, d] for d in group], ends[1][i], ends[-1][i])
            for d, total in zip(group, totals):
                pieces[d] = total if d == 0 else shift(total, -d)
        layer_out, prob_grad = home(where, after(expert_ids.T, hidden_grad), [pieces[d] for d in range(n_dp)], width, n_ex)
        return (layer_out, prob_grad.T, hidden_grad, weight_grad[None])

    return shards


def solution(mesh):
    placed = (
        P(("dp", "expert"), None),
        P(("dp", "expert"), None),
        P("dp", "expert", None, None, None),
        P("expert", None, "dp"),
        P(("dp", "expert"), None),
    )
    return jax.shard_map(
        body(chip_ring(mesh)),
        mesh=mesh,
        in_specs=placed,
        out_specs=(
            P(("dp", "expert"), None),
            P(("dp", "expert"), None),
            P("dp", "expert", None, None, None),
            P("expert", None, "dp"),
        ),
        check_vma=False,
    )
```
